32 devices in a mesh: mp: 2 (over y), row: 8 (over z, x), col: 2 (over core).
Axes of the slice: x: 2, y: 2, z: 4, core: 2. Of those that a mesh axis runs over, the one named last changes fastest.
Arguments:
- ancestor_cov: float32 [2048, 4, 2, 128], P(('mp', 'row'), None, 'col'), parts along dimension 0, as said below
- panel_factor: float32 [1536, 2, 512], P(('mp', 'row'), None, 'col'), parts along dimension 0, may hold values from -0.1875 to 0.1875
- diag_inverse: float32 [1024, 2, 512], P('mp', None, 'row'), parts along dimension 0, as said below
- structure: int32 [4, 6], P('mp'), parts along dimension 0, may hold values from 0 to 7, as said below
- live_counts: int32 [4], P('mp'), parts along dimension 0, may hold values from 1 to 6, as said below
Outputs:
- panel_cov: float32 [2048, 2, 512], P(('mp', 'row'), None, 'col'), parts along dimension 0
- diag_cov: float32 [1024, 2, 512], P(('mp', 'row'), None, 'col'), parts along dimension 0
The draws below stay inside these ranges and needn't reach their ends.
There are 2 independent parts, one for each index of `mp`. The reference program is written for one: setup_inputs(seed, part) draws one part's arguments, and reference() takes and returns one part's arrays. A program takes and returns all parts, laid end to end along the dimension named above; each array names one. Nothing has to cross between parts.
Inputs may be any that keep to these rules, and one draw needn't show every extreme that they name: ancestor_cov is symmetric as the matrix C. Each diag_inverse[:, m, :] is lower triangular. `structure`: for each member the first live_counts entries are distinct ancestor tile rows in increasing order; the later entries are padding and are not used. `live_counts`: in every draw one of the two supernodes uses all 6 slots.
All inputs are finite; a program needn't handle non-finite values.
Results may differ from the reference program's by a relative error of at most 0.0001.
Values sent between devices are 32-bit elements; how exact they have to be, the bound alone decides.
No kernel may reach another device: no remote copies, remote signals or barrier semaphores. Data moves between devices by JAX's collectives and lax.ppermute only.
A program may use at most 128 MiB of HBM per device.

```python
import math
import jax
import jax.numpy as jnp
from jax import lax

TILE = 128
BW = 512
NA = 8
LC = 4
NSK = 6
N_COL = 2


def draw_ancestor_cov(key, part):
    key = jax.random.fold_in(key, 11)
    first_key, second_key = jax.random.split(key)
    size_all = NA * TILE
    noise_field = jax.random.normal(first_key, (size_all, size_all), jnp.float32)
    diag_values = jax.random.uniform(second_key, (size_all,), jnp.float32, 1.0, 3.0)
    coupling = (noise_field + noise_field.T) * (0.4 / math.sqrt(NSK * TILE))
    positions = jnp.arange(size_all)
    matrix = jnp.where(positions[:, None] == positions[None, :], diag_values[None, :], coupling)
    return matrix.reshape(size_all, LC, N_COL, TILE)


def draw_diag_inverse(key, part):
    key = jax.random.fold_in(key, 12)
    first_key, second_key = jax.random.split(key)
    noise_field = jax.random.normal(first_key, (BW, 2, BW), jnp.float32)
    diag_values = jax.random.uniform(second_key, (BW, 2, BW), jnp.float32, 0.5, 1.5)
    row_pos = jnp.arange(BW)[:, None, None]
    col_pos = jnp.arange(BW)[None, None, :]
    lower = jnp.where(row_pos > col_pos, noise_field / math.sqrt(BW), 0.0)
    return jnp.where(row_pos == col_pos, diag_values, lower)


def draw_structure(key, part):
    key = jax.random.fold_in(key, 13)
    lists = []
    for member in range(2):
        chosen = jax.random.permutation(jax.random.fold_in(key, member), NA)[:NSK]
        lists.append(jnp.sort(chosen))
    return jnp.stack(lists, axis=0).astype(jnp.int32)


def draw_live_counts(key, part):
    key = jax.random.fold_in(key, 14)
    first_key, second_key = jax.random.split(key)
    full_member = jax.random.randint(first_key, (), 0, 2)
    other_count = jax.random.randint(second_key, (), 1, NSK + 1)
    members = jnp.arange(2)
    return jnp.where(members == full_member, NSK, other_count).astype(jnp.int32)


def level_of(key, shape, pieces, least, high):
    def one(dim, shards_of):
        steps = jax.random.uniform(jax.random.fold_in(jax.random.fold_in(key, 6), dim), (shards_of,), jnp.float32, least / len(pieces), high / len(pieces))
        return jnp.repeat(jnp.exp(steps), shape[dim] // shards_of).reshape((-1,) + (1,) * (len(shape) - dim - 1))

    gain = one(*pieces[0])
    for cut in pieces[1:]:
        gain = gain * one(*cut)
    return gain


def centred(key, shape, width, most, shards=(), kind=jnp.bfloat16):
    entries = jax.random.normal(key, shape, jnp.float32) * width
    if len(shards) > 0:
        entries = level_of(key, shape, shards, -0.22, 0.18) * entries
    return jnp.clip(entries, min=-most, max=most).astype(kind)


def setup_inputs(seed: int = 0, part: int = 0) -> dict:
    streams_of = jax.random.split(jax.random.key(seed), 6)
    own_keys = jax.random.split(jax.random.fold_in(streams_of[5], part), 6)
    ancestor_cov = draw_ancestor_cov(jax.random.fold_in(jax.random.fold_in(streams_of[5], part), 71), part)
    panel_factor = centred(own_keys[1], (NSK * TILE, 2, BW), (2 * BW) ** -0.5, 0.1875, ((0, 8), (2, 2)), jnp.float32)
    diag_inverse = draw_diag_inverse(jax.random.fold_in(jax.random.fold_in(streams_of[5], part), 71), part)
    structure = draw_structure(jax.random.fold_in(jax.random.fold_in(streams_of[5], part), 71), part)
    live_counts = draw_live_counts(jax.random.fold_in(jax.random.fold_in(streams_of[5], part), 71), part)
    return {"ancestor_cov": ancestor_cov, "panel_factor": panel_factor, "diag_inverse": diag_inverse, "structure": structure, "live_counts": live_counts}


def reference(ancestor_cov, panel_factor, diag_inverse, structure, live_counts):
    full_rows = NA * TILE
    dense_cov = ancestor_cov.reshape(full_rows, full_rows)
    tile_offsets = jnp.arange(TILE, dtype=jnp.int32)
    slot_index = jnp.arange(NSK, dtype=jnp.int32)
    panel_list = []
    diag_list = []
    for member in range(2):
        inverse_block = diag_inverse[:, member, :]
        scaled = jnp.dot(panel_factor[:, member, :], inverse_block, precision=lax.Precision.HIGHEST, preferred_element_type=jnp.float32)
        slot_alive = slot_index < live_counts[member]
        alive_rows = jnp.repeat(slot_alive, TILE)
        scaled = jnp.where(alive_rows[:, None], scaled, jnp.zeros_like(scaled))
        picked = (structure[member][:, None] * TILE + tile_offsets[None, :]).reshape(-1).astype(jnp.int32)
        sub_cov = dense_cov[picked][:, picked]
        product = jnp.dot(sub_cov, scaled, precision=lax.Precision.HIGHEST, preferred_element_type=jnp.float32)
        target = jnp.where(alive_rows, picked, full_rows).astype(jnp.int32)
        panel = jnp.zeros((full_rows, BW), jnp.float32).at[target].set(-product, mode="drop")
        diag_block = jnp.dot(inverse_block.T, inverse_block, precision=lax.Precision.HIGHEST, preferred_element_type=jnp.float32)
        diag_block = diag_block + jnp.dot(scaled.T, product, precision=lax.Precision.HIGHEST, preferred_element_type=jnp.float32)
        panel_list.append(panel)
        diag_list.append(diag_block)
    return jnp.stack(panel_list, axis=1), jnp.stack(diag_list, axis=1)
```

```python
import functools

import jax
import jax.numpy as jnp
from jax import lax
from jax.experimental import pallas as pl
from jax.experimental.pallas import tpu as pltpu
from jax.sharding import PartitionSpec as P

F32 = jnp.float32
BF16 = jnp.bfloat16
NT = (((1,), (1,)), ((), ()))
NN = (((1,), (0,)), ((), ()))
TN = (((0,), (0,)), ((), ()))
VMEM_LIMIT = 48 * 1024 * 1024


def halves(value):
    high = value.astype(BF16)
    low = (value - high.astype(F32)).astype(BF16)
    return high, low


def dot3(left, right, dims):
    left_high, left_low = left
    right_high, right_low = right

    def one(a, b):
        return lax.dot_general(a, b, dims, preferred_element_type=F32)

    return one(left_high, right_low) + one(left_low, right_high) + one(left_high, right_high)


def main_kernel(rows, tile, slots, *refs):
    structure, live, place = refs[:3]
    c_own, c_sib, c_near, c_near_sib = refs[3:7]
    factor_blocks = refs[7:7 + rows]
    inverse_blocks = refs[7 + rows:7 + 2 * rows]
    panel_keep, panel_send = refs[7 + 2 * rows:9 + 2 * rows]
    diag_out = refs[9 + 2 * rows:9 + 3 * rows]
    pick_high, pick_low, f_high, f_low, d_high, d_low, own_f, diag_part = refs[9 + 3 * rows:]
    row = place[0]
    col = place[1]
    share = factor_blocks[0].shape[0]
    width = inverse_blocks[0].shape[0]
    half = panel_keep.shape[1]
    for step in range(rows):
        source = row ^ step
        high, low = halves(factor_blocks[step][...])
        at = pl.ds(pl.multiple_of(source * share, share), share)
        f_high[at, :] = high
        f_low[at, :] = low
        high, low = halves(inverse_blocks[step][...])
        at = pl.ds(pl.multiple_of(source * width, width), width)
        d_high[at, :] = high
        d_low[at, :] = low
    local_blocks = c_own.shape[0] // tile
    for slot in range(slots):
        anc = structure[col, slot]
        alive = slot < live[col]
        block = anc // 2
        mine = anc % 2 == col
        for part, (here, there) in enumerate(((c_own, c_sib), (c_near, c_near_sib))):
            at = pl.ds(block, tile, stride=local_blocks)
            value = jnp.where(mine, here[at, :], there[at, :])
            value = jnp.where(alive, value, 0.0)
            high, low = halves(value)
            pick_high[part * tile:(part + 1) * tile, slot * tile:(slot + 1) * tile] = high
            pick_low[part * tile:(part + 1) * tile, slot * tile:(slot + 1) * tile] = low
    inverse = (d_high[...], d_low[...])
    own_f[...] = jnp.zeros_like(own_f)
    in_struct = False
    for slot in range(slots):
        alive = slot < live[col]
        for part in range(2):
            hit = alive & (structure[col, slot] == row ^ part)
            if part == 0:
                in_struct = in_struct | hit

            @pl.when(hit)
            def _(slot=slot, part=part):
                own_f[0, part * tile:(part + 1) * tile, :] = f_high[slot * tile:(slot + 1) * tile, :]
                own_f[1, part * tile:(part + 1) * tile, :] = f_low[slot * tile:(slot + 1) * tile, :]

    grown = dot3((pick_high[...], pick_low[...]), (f_high[...], f_low[...]), NN)
    product = dot3(halves(grown), inverse, NT)
    scaled = dot3((own_f[0], own_f[1]), inverse, NT)
    panel = jnp.where(in_struct, -product[:tile], 0.0)

    @pl.when(col == 0)
    def _():
        panel_keep[...] = panel[:, :half]
        panel_send[...] = panel[:, half:]

    @pl.when(col == 1)
    def _():
        panel_keep[...] = panel[:, half:]
        panel_send[...] = panel[:, :half]

    diag_part[...] = dot3(halves(scaled), halves(product), TN)
    at = pl.ds(pl.multiple_of(row * width, width), width)
    base = dot3((d_high[at, :], d_low[at, :]), inverse, NT)
    diag_part[at, :] = diag_part[at, :] + base
    for step in range(rows // 2):
        at = pl.ds(pl.multiple_of((row ^ (2 * step)) * width, width), width)
        block = diag_part[at, :]
        for other in range(2):
            @pl.when(col == other)
            def _():
                diag_out[2 * step][...] = block[:, other * half:(other + 1) * half]
                diag_out[2 * step + 1][...] = block[:, (1 - other) * half:(2 - other) * half]


def last_kernel(count, *refs):
    place, keep, got = refs[:3]
    pieces = refs[3:3 + count]
    panel_out, diag_out = refs[3 + count:]
    col = place[1]
    lanes = 128
    same = pieces[0][...]
    cross = pieces[1][...]
    for step in range(1, count // 2):
        same = same + pieces[2 * step][...]
        cross = cross + pieces[2 * step + 1][...]
    values = ((panel_out, keep[...], got[...]), (diag_out, same, cross))
    for out, mine, other in values:
        first = jnp.where(col == 0, mine, other)
        second = jnp.where(col == 0, other, mine)
        lane_blocks = mine.shape[1] // lanes
        for block in range(lane_blocks):
            at = slice(block * lanes, (block + 1) * lanes)
            out[pl.ds(2 * block, mine.shape[0], stride=2 * lane_blocks), :] = first[:, at]
            out[pl.ds(2 * block + 1, mine.shape[0], stride=2 * lane_blocks), :] = second[:, at]


def many_rows(ancestor_cov, panel_factor, diag_inverse, structure, live_counts):
    tile_rows = ancestor_cov.shape[0]
    local_blocks = ancestor_cov.shape[1]
    col_count = lax.axis_size("col")
    col_id = lax.axis_index("col")
    row_id = lax.axis_index("row")
    flat_cov = ancestor_cov.reshape(tile_rows, local_blocks * tile_rows)
    half_width = panel_factor.shape[2]
    slot_total = structure.shape[1]
    whole_inverse = lax.all_gather(diag_inverse, "row", axis=2, tiled=True)
    inverse_part = lax.dynamic_slice_in_dim(whole_inverse, col_id * half_width, half_width, 0)
    factor_term = jnp.einsum(
        "rsk,ksn->rsn", panel_factor, inverse_part, precision=lax.Precision.HIGHEST
    )
    slot_index = jnp.arange(slot_total, dtype=jnp.int32)
    slot_alive = slot_index[None, :] < live_counts[:, None]
    own_slot = slot_alive & (structure == row_id)
    in_struct = jnp.any(own_slot, axis=1)
    own_pos = jnp.sum(jnp.where(own_slot, slot_index[None, :], 0), axis=1)
    tile_offsets = jnp.arange(tile_rows, dtype=jnp.int32)
    factor_rows = lax.psum(factor_term, "col")
    arrived = lax.all_gather(factor_rows, "row", axis=0, tiled=True)
    row_count = arrived.shape[0]
    global_row = jnp.arange(row_count, dtype=jnp.int32)
    slot_of = global_row // tile_rows
    offset = global_row % tile_rows
    chooser = (slot_of[:, None] == slot_index[None, :]).astype(jnp.int32)
    product_list = []
    owned_list = []
    for member in range(2):
        anc_block = jnp.sum(chooser * structure[member][None, :], axis=1)
        is_live = slot_of < live_counts[member]
        is_match = is_live & (anc_block % col_count == col_id)
        column_index = anc_block // col_count * tile_rows + offset
        sig_cols = jnp.take(flat_cov, column_index, axis=1)
        weighted = jnp.where(is_match[:, None], arrived[:, member, :], 0.0)
        product_list.append(
            jnp.dot(
                sig_cols,
                weighted,
                precision=lax.Precision.HIGHEST,
                preferred_element_type=jnp.float32,
            )
        )
        source = own_pos[member] * tile_rows + tile_offsets
        in_range = in_struct[member] & (source >= 0) & (source < row_count)
        fetched = jnp.take(arrived[:, member, :], jnp.clip(source, 0, row_count - 1), axis=0)
        owned_list.append(jnp.where(in_range[:, None], fetched, 0.0))
    partial_sum = jnp.stack(product_list, axis=1)
    owned = jnp.stack(owned_list, axis=1)
    summed_all = lax.psum(partial_sum, "col")
    product_half = lax.dynamic_slice_in_dim(summed_all, col_id * half_width, half_width, 2)
    panel_cov = -product_half * in_struct.astype(jnp.float32)[None, :, None]
    spread_term = lax.psum_scatter(
        jnp.einsum("tsi,tsn->isn", owned, product_half, precision=lax.Precision.HIGHEST),
        "row",
        scatter_dimension=0,
        tiled=True,
    )
    inverse_half = lax.dynamic_slice_in_dim(whole_inverse, col_id * half_width, half_width, 2)
    base_term = jnp.einsum(
        "ksi,ksn->isn", diag_inverse, inverse_half, precision=lax.Precision.HIGHEST
    )
    diag_cov = base_term + spread_term
    return (panel_cov, diag_cov)


def local(ancestor_cov, panel_factor, diag_inverse, structure, live_counts):
    rows = lax.axis_size("row")
    if rows != 8:
        return many_rows(ancestor_cov, panel_factor, diag_inverse, structure, live_counts)
    tile = ancestor_cov.shape[0]
    local_blocks = ancestor_cov.shape[1]
    share, _, half = panel_factor.shape
    whole, _, width = diag_inverse.shape
    slots = structure.shape[1]
    col = lax.axis_index("col")
    row = lax.axis_index("row")

    def move(value, step, flip):
        pairs = [
            (r * 2 + c, (r ^ step) * 2 + (c ^ flip)) for r in range(rows) for c in range(2)
        ]
        return lax.ppermute(value, ("row", "col"), pairs)

    c_own = ancestor_cov.reshape(tile * local_blocks, 128)
    c_near = move(c_own, 1, 0)
    c_sib = move(c_own, 0, 1)
    inverse_own = lax.dynamic_index_in_dim(diag_inverse.transpose(1, 2, 0), col, 0, keepdims=False)
    f_keep = lax.dynamic_index_in_dim(panel_factor, col, 1, keepdims=False)
    f_send = lax.dynamic_index_in_dim(panel_factor, 1 - col, 1, keepdims=False)
    f_got = move(f_send, 0, 1)
    inverse = [inverse_own] + [move(inverse_own, 2 * k, 0) for k in range(1, rows // 2)]
    factor_own = jnp.concatenate(
        [jnp.where(col == 0, f_keep, f_got), jnp.where(col == 0, f_got, f_keep)], axis=1
    )
    factor = [factor_own] + [move(factor_own, 2 * k, 0) for k in range(1, rows // 2)]
    c_near_sib = move(c_near, 0, 1)
    inverse_near = [move(value, 1, 0) for value in inverse]
    factor_near = [move(value, 1, 0) for value in factor]
    inverse_blocks = [v for pair in zip(inverse, inverse_near) for v in pair]
    factor_blocks = [v for pair in zip(factor, factor_near) for v in pair]
    place = jnp.stack([row, col]).astype(jnp.int32)
    smem = pl.BlockSpec(memory_space=pltpu.SMEM)
    vmem = pl.BlockSpec(memory_space=pltpu.VMEM)
    outs = pl.pallas_call(
        functools.partial(main_kernel, rows, tile, slots),
        out_shape=[jax.ShapeDtypeStruct((tile, half), F32)] * 2
        + [jax.ShapeDtypeStruct((width, half), F32)] * rows,
        in_specs=[smem] * 3 + [vmem] * (4 + 2 * rows),
        out_specs=[vmem] * (2 + rows),
        scratch_shapes=[
            pltpu.VMEM((2 * tile, slots * tile), BF16),
            pltpu.VMEM((2 * tile, slots * tile), BF16),
            pltpu.VMEM((slots * tile, whole), BF16),
            pltpu.VMEM((slots * tile, whole), BF16),
            pltpu.VMEM((whole, whole), BF16),
            pltpu.VMEM((whole, whole), BF16),
            pltpu.VMEM((2, 2 * tile, whole), BF16),
            pltpu.VMEM((whole, whole), F32),
        ],
        compiler_params=pltpu.CompilerParams(vmem_limit_bytes=VMEM_LIMIT),
        name="products",
    )(structure, live_counts, place, c_own, c_sib, c_near, c_near_sib, *factor_blocks, *inverse_blocks)
    panel_keep, panel_send = outs[:2]
    diag_pieces = outs[2:]
    pieces = [diag_pieces[0]] + [move(diag_pieces[j], 2 * (j // 2), j % 2) for j in range(1, rows)]
    panel_got = move(panel_send, 0, 1)
    panel, diag = pl.pallas_call(
        functools.partial(last_kernel, rows),
        out_shape=[
            jax.ShapeDtypeStruct((tile * 2 * half // 128, 128), F32),
            jax.ShapeDtypeStruct((width * 2 * half // 128, 128), F32),
        ],
        in_specs=[smem] + [vmem] * (2 + rows),
        out_specs=[vmem] * 2,
        compiler_params=pltpu.CompilerParams(vmem_limit_bytes=VMEM_LIMIT),
        name="sums",
    )(place, panel_keep, panel_got, *pieces)

    def unfold(value, count):
        return value.reshape(count, half // 128, 2, 128).transpose(0, 2, 1, 3).reshape(count, 2, half)

    return unfold(panel, tile), unfold(diag, width)


def solution(mesh):
    placed = (
        P(("mp", "row"), None, "col", None),
        P(("mp", "row"), None, "col"),
        P("mp", None, "row"),
        P("mp", None),
        P("mp"),
    )
    return jax.shard_map(
        local,
        mesh=mesh,
        in_specs=placed,
        out_specs=(P(("mp", "row"), None, "col"), P(("mp", "row"), None, "col")),
        check_vma=False,
    )
```

```python
import functools

import jax
import jax.numpy as jnp
from jax import lax
from jax.experimental import pallas as pl
from jax.experimental.pallas import tpu as pltpu
from jax.sharding import PartitionSpec as P

F32 = jnp.float32
BF16 = jnp.bfloat16
NT = (((1,), (1,)), ((), ()))
NN = (((1,), (0,)), ((), ()))
TN = (((0,), (0,)), ((), ()))
VMEM_LIMIT = 20 * 1024 * 1024


def halves(value):
    high = value.astype(BF16)
    low = (value - high.astype(F32)).astype(BF16)
    return high, low


def dot3(left, right, dims):
    left_high, left_low = left
    right_high, right_low = right

    def one(a, b):
        return lax.dot_general(a, b, dims, preferred_element_type=F32)

    return one(left_high, right_low) + one(left_low, right_high) + one(left_high, right_high)


def main_kernel(rows, tile, slots, *refs):
    structure, live, place = refs[:3]
    c_own, c_sib, c_near, c_near_sib = refs[3:7]
    factor_blocks = refs[7:7 + rows]
    inverse_blocks = refs[7 + rows:7 + rows + rows // 2]
    panel_keep, panel_send, diag_out = refs[7 + rows + rows // 2:10 + rows + rows // 2]
    pick_high, pick_low, f_high, f_low, d_high, d_low, own_f, diag_part = refs[10 + rows + rows // 2:]
    row = place[0]
    col = place[1]
    share = factor_blocks[0].shape[0]
    width = inverse_blocks[0].shape[0] // 2
    half = panel_keep.shape[1]
    for step in range(rows):
        high, low = halves(factor_blocks[step][...])
        at = pl.ds(pl.multiple_of((row ^ step) * share, share), share)
        f_high[at, :] = high
        f_low[at, :] = low
    for step in range(rows // 2):
        high, low = halves(inverse_blocks[step][...])
        at = pl.ds(pl.multiple_of((row // 2 ^ step) * 2 * width, 2 * width), 2 * width)
        d_high[at, :] = high
        d_low[at, :] = low
    local_blocks = c_own.shape[0] // tile
    for slot in range(slots):
        anc = structure[col, slot]
        alive = slot < live[col]
        block = anc // 2
        mine = anc % 2 == col
        for part, (here, there) in enumerate(((c_own, c_sib), (c_near, c_near_sib))):
            at = pl.ds(block, tile, stride=local_blocks)
            value = jnp.where(mine, here[at, :], there[at, :])
            value = jnp.where(alive, value, 0.0)
            high, low = halves(value)
            pick_high[part * tile:(part + 1) * tile, slot * tile:(slot + 1) * tile] = high
            pick_low[part * tile:(part + 1) * tile, slot * tile:(slot + 1) * tile] = low
    inverse = (d_high[...], d_low[...])
    own_f[...] = jnp.zeros_like(own_f)
    in_struct = False
    for slot in range(slots):
        alive = slot < live[col]
        for part in range(2):
            hit = alive & (structure[col, slot] == row ^ part)
            if part == 0:
                in_struct = in_struct | hit

            @pl.when(hit)
            def _(slot=slot, part=part):
                own_f[0, part * tile:(part + 1) * tile, :] = f_high[slot * tile:(slot + 1) * tile, :]
                own_f[1, part * tile:(part + 1) * tile, :] = f_low[slot * tile:(slot + 1) * tile, :]

    grown = dot3((pick_high[...], pick_low[...]), (f_high[...], f_low[...]), NN)
    product = dot3(halves(grown), inverse, NT)
    scaled = dot3((own_f[0], own_f[1]), inverse, NT)
    panel = jnp.where(in_struct, -product[:tile], 0.0)

    @pl.when(col == 0)
    def _():
        panel_keep[...] = panel[:, :half]
        panel_send[...] = panel[:, half:]

    @pl.when(col == 1)
    def _():
        panel_keep[...] = panel[:, half:]
        panel_send[...] = panel[:, :half]

    diag_part[...] = dot3(halves(scaled), halves(product), TN)
    at = pl.ds(pl.multiple_of(row * width, width), width)
    base = dot3((d_high[at, :], d_low[at, :]), inverse, NT)
    diag_part[at, :] = diag_part[at, :] + base
    for step in range(rows // 2):
        at = pl.ds(pl.multiple_of((2 * step + row % 2) * width, width), width)
        for other in range(2):
            diag_out[2 * step + other] = diag_part[at, other * half:(other + 1) * half]


def last_kernel(place, keep, got, pieces, panel_out, diag_out):
    col = place[1]
    lanes = 128
    count = pieces.shape[0]
    members = [pieces[m] for m in range(2)]
    for step in range(2, count):
        members[step % 2] = members[step % 2] + pieces[step]
    keep_value = keep[...]
    got_value = got[...]
    panels = (jnp.where(col == 0, keep_value, got_value), jnp.where(col == 0, got_value, keep_value))
    for out, values in ((panel_out, panels), (diag_out, members)):
        blocks = values[0].shape[1] // lanes
        for block in range(blocks):
            for member in range(2):
                at = pl.ds(2 * block + member, values[0].shape[0], stride=2 * blocks)
                out[at, :] = values[member][:, block * lanes:(block + 1) * lanes]


def many_rows(ancestor_cov, panel_factor, diag_inverse, structure, live_counts):
    tile_rows = ancestor_cov.shape[0]
    local_blocks = ancestor_cov.shape[1]
    col_count = lax.axis_size("col")
    col_id = lax.axis_index("col")
    row_id = lax.axis_index("row")
    flat_cov = ancestor_cov.reshape(tile_rows, local_blocks * tile_rows)
    half_width = panel_factor.shape[2]
    slot_total = structure.shape[1]
    whole_inverse = lax.all_gather(diag_inverse, "row", axis=2, tiled=True)
    inverse_part = lax.dynamic_slice_in_dim(whole_inverse, col_id * half_width, half_width, 0)
    factor_term = jnp.einsum(
        "rsk,ksn->rsn", panel_factor, inverse_part, precision=lax.Precision.HIGHEST
    )
    slot_index = jnp.arange(slot_total, dtype=jnp.int32)
    slot_alive = slot_index[None, :] < live_counts[:, None]
    own_slot = slot_alive & (structure == row_id)
    in_struct = jnp.any(own_slot, axis=1)
    own_pos = jnp.sum(jnp.where(own_slot, slot_index[None, :], 0), axis=1)
    tile_offsets = jnp.arange(tile_rows, dtype=jnp.int32)
    factor_rows = lax.psum(factor_term, "col")
    arrived = lax.all_gather(factor_rows, "row", axis=0, tiled=True)
    row_count = arrived.shape[0]
    global_row = jnp.arange(row_count, dtype=jnp.int32)
    slot_of = global_row // tile_rows
    offset = global_row % tile_rows
    chooser = (slot_of[:, None] == slot_index[None, :]).astype(jnp.int32)
    product_list = []
    owned_list = []
    for member in range(2):
        anc_block = jnp.sum(chooser * structure[member][None, :], axis=1)
        is_live = slot_of < live_counts[member]
        is_match = is_live & (anc_block % col_count == col_id)
        column_index = anc_block // col_count * tile_rows + offset
        sig_cols = jnp.take(flat_cov, column_index, axis=1)
        weighted = jnp.where(is_match[:, None], arrived[:, member, :], 0.0)
        product_list.append(
            jnp.dot(
                sig_cols,
                weighted,
                precision=lax.Precision.HIGHEST,
                preferred_element_type=jnp.float32,
            )
        )
        source = own_pos[member] * tile_rows + tile_offsets
        in_range = in_struct[member] & (source >= 0) & (source < row_count)
        fetched = jnp.take(arrived[:, member, :], jnp.clip(source, 0, row_count - 1), axis=0)
        owned_list.append(jnp.where(in_range[:, None], fetched, 0.0))
    partial_sum = jnp.stack(product_list, axis=1)
    owned = jnp.stack(owned_list, axis=1)
    summed_all = lax.psum(partial_sum, "col")
    product_half = lax.dynamic_slice_in_dim(summed_all, col_id * half_width, half_width, 2)
    panel_cov = -product_half * in_struct.astype(jnp.float32)[None, :, None]
    spread_term = lax.psum_scatter(
        jnp.einsum("tsi,tsn->isn", owned, product_half, precision=lax.Precision.HIGHEST),
        "row",
        scatter_dimension=0,
        tiled=True,
    )
    inverse_half = lax.dynamic_slice_in_dim(whole_inverse, col_id * half_width, half_width, 2)
    base_term = jnp.einsum(
        "ksi,ksn->isn", diag_inverse, inverse_half, precision=lax.Precision.HIGHEST
    )
    diag_cov = base_term + spread_term
    return (panel_cov, diag_cov)


def local(ancestor_cov, panel_factor, diag_inverse, structure, live_counts):
    rows = lax.axis_size("row")
    if rows != 8:
        return many_rows(ancestor_cov, panel_factor, diag_inverse, structure, live_counts)
    tile = ancestor_cov.shape[0]
    local_blocks = ancestor_cov.shape[1]
    share, _, half = panel_factor.shape
    whole, _, width = diag_inverse.shape
    slots = structure.shape[1]
    col = lax.axis_index("col")
    row = lax.axis_index("row")

    def move(value, step, flip):
        pairs = [
            (r * 2 + c, (r ^ step) * 2 + (c ^ flip)) for r in range(rows) for c in range(2)
        ]
        return lax.ppermute(value, ("row", "col"), pairs)

    def ordered(mine, other, index):
        return jnp.concatenate(
            [jnp.where(index == 0, mine, other), jnp.where(index == 0, other, mine)], axis=0
        )

    c_own = ancestor_cov.reshape(tile * local_blocks, 128)
    c_near = move(c_own, 1, 0)
    f_keep = lax.dynamic_index_in_dim(panel_factor, col, 1, keepdims=False)
    f_send = lax.dynamic_index_in_dim(panel_factor, 1 - col, 1, keepdims=False)
    f_got = move(f_send, 0, 1)
    inverse_own = lax.dynamic_index_in_dim(diag_inverse.transpose(1, 2, 0), col, 0, keepdims=False)
    inverse_pair = ordered(inverse_own, move(inverse_own, 1, 0), row % 2)
    factor_own = jnp.concatenate(
        [jnp.where(col == 0, f_keep, f_got), jnp.where(col == 0, f_got, f_keep)], axis=1
    )

    def spread(value):
        far = move(value, 4, 0)
        return [value, move(value, 2, 0), far, move(far, 2, 0)]

    factor = spread(factor_own)
    inverse_blocks = spread(inverse_pair)
    factor_blocks = [v for block in factor for v in (block, move(block, 1, 0))]
    c_sib = move(c_own, 0, 1)
    c_near_sib = move(c_near, 0, 1)
    place = jnp.stack([row, col]).astype(jnp.int32)
    smem = pl.BlockSpec(memory_space=pltpu.SMEM)
    vmem = pl.BlockSpec(memory_space=pltpu.VMEM)
    outs = pl.pallas_call(
        functools.partial(main_kernel, rows, tile, slots),
        out_shape=[jax.ShapeDtypeStruct((tile, half), F32)] * 2
        + [jax.ShapeDtypeStruct((rows, width, half), F32)],
        in_specs=[smem] * 3 + [vmem] * (4 + rows + rows // 2),
        out_specs=[vmem] * 3,
        scratch_shapes=[
            pltpu.VMEM((2 * tile, slots * tile), BF16),
            pltpu.VMEM((2 * tile, slots * tile), BF16),
            pltpu.VMEM((slots * tile, whole), BF16),
            pltpu.VMEM((slots * tile, whole), BF16),
            pltpu.VMEM((whole, whole), BF16),
            pltpu.VMEM((whole, whole), BF16),
            pltpu.VMEM((2, 2 * tile, whole), BF16),
            pltpu.VMEM((whole, whole), F32),
        ],
        compiler_params=pltpu.CompilerParams(vmem_limit_bytes=VMEM_LIMIT),
        name="products",
    )(structure, live_counts, place, c_own, c_sib, c_near, c_near_sib, *factor_blocks, *inverse_blocks)
    panel_keep, panel_send, diag_pieces = outs
    panel_got = move(panel_send, 0, 1)
    groups = [
        [(2 * z + x) * 2 + c for z in range(rows // 2) for c in range(2)] for x in range(2)
    ]
    pieces = lax.all_to_all(
        diag_pieces, ("row", "col"), 0, 0, axis_index_groups=groups, tiled=True
    )
    panel, diag = pl.pallas_call(
        last_kernel,
        out_shape=[
            jax.ShapeDtypeStruct((tile * 2 * half // 128, 128), F32),
            jax.ShapeDtypeStruct((width * 2 * half // 128, 128), F32),
        ],
        in_specs=[smem] + [vmem] * 3,
        out_specs=[vmem] * 2,
        compiler_params=pltpu.CompilerParams(vmem_limit_bytes=VMEM_LIMIT),
        name="sums",
    )(place, panel_keep, panel_got, pieces)

    def unfold(value, count):
        return value.reshape(count, half // 128, 2, 128).transpose(0, 2, 1, 3).reshape(count, 2, half)

    return unfold(panel, tile), unfold(diag, width)


def solution(mesh):
    placed = (
        P(("mp", "row"), None, "col", None),
        P(("mp", "row"), None, "col"),
        P("mp", None, "row"),
        P("mp", None),
        P("mp"),
    )
    return jax.shard_map(
        local,
        mesh=mesh,
        in_specs=placed,
        out_specs=(P(("mp", "row"), None, "col"), P(("mp", "row"), None, "col")),
        check_vma=False,
    )
```

```python
import functools

import jax
import jax.numpy as jnp
from jax import lax
from jax.experimental import pallas as pl
from jax.experimental.pallas import tpu as pltpu
from jax.sharding import PartitionSpec as P

F32 = jnp.float32
BF16 = jnp.bfloat16
NT = (((1,), (1,)), ((), ()))
NN = (((1,), (0,)), ((), ()))
TN = (((0,), (0,)), ((), ()))
VMEM_LIMIT = 20 * 1024 * 1024


def halves(value):
    high = value.astype(BF16)
    low = (value - high.astype(F32)).astype(BF16)
    return high, low


def dot3(left, right, dims):
    left_high, left_low = left
    right_high, right_low = right

    def one(a, b):
        return lax.dot_general(a, b, dims, preferred_element_type=F32)

    return one(left_high, right_low) + one(left_low, right_high) + one(left_high, right_high)


def pack_kernel(place, factor, inverse, own, send):
    x = place[1]
    c = place[2]
    half = own.shape[1]
    share = factor.shape[0] * 128 // (2 * half)
    blocks = half // 128
    for out, member in ((own, x), (send, 1 - x)):
        for block in range(blocks):
            at = pl.ds(2 * block + member, share, stride=2 * blocks)
            out[:share, block * 128:(block + 1) * 128] = factor[at, :]
        out[share:, :] = inverse[member, :, pl.ds(pl.multiple_of(c * half, half), half)]


def product_kernel(share, tile, slots, *refs):
    structure, live, place, c_keep, c_got = refs[:5]
    mine = refs[5:12]
    theirs = refs[12:15]
    panel_out = refs[15:19]
    w_out = refs[19:23]
    f_high, f_low, d_high, d_low, pick_high, pick_low, product = refs[23:]
    z, x, c = place[0], place[1], place[2]
    member = x
    half = mine[0].shape[1]
    width = mine[0].shape[0] - share
    near = 1 - x
    mine_at = []
    for index, step in ((0, 0), (2, 2), (4, 1)):
        mine_at += [(index, 0, 2 * (z ^ step) + x), (index + 1, 0, 2 * (z ^ step) + near)]
    mine_at += [(6, 0, 2 * (z ^ 3) + x), (6, share + width, 2 * (z ^ 3) + near)]
    block = share + width
    theirs_at = [(0, 0, 2 * z + x), (0, block, 2 * z + near)]
    for index, step in ((0, 2), (2, 1)):
        theirs_at += [(1, index * block, 2 * (z ^ step) + x), (1, (index + 1) * block, 2 * (z ^ step) + near)]
    theirs_at += [(2, 0, 2 * (z ^ 3) + x), (2, block, 2 * (z ^ 3) + near)]
    for lanes, pieces, table in ((0, mine, mine_at), (half, theirs, theirs_at)):
        for index, first, source in table:
            high, low = halves(pieces[index][first:first + share, :])
            at = pl.ds(pl.multiple_of(source * share, share), share)
            f_high[at, lanes:lanes + half] = high
            f_low[at, lanes:lanes + half] = low
            high, low = halves(pieces[index][first + share:first + block, :])
            at = pl.ds(pl.multiple_of(source * width, width), width)
            d_high[at, lanes:lanes + half] = high
            d_low[at, lanes:lanes + half] = low
    part = tile // 2
    blocks = c_keep.shape[1] // part
    in_struct = [False, False]
    for slot in range(slots):
        anc = structure[member, slot]
        alive = slot < live[member]
        own_column = anc % 2 == c
        rows = pl.ds(anc // 2, part, stride=blocks)
        for which in range(2):
            value = jnp.where(own_column, c_keep[which, rows, :], c_got[which, rows, :])
            high, low = halves(jnp.where(alive, value, 0.0))
            at = pl.ds(pl.multiple_of((x ^ which) * part, part), part)
            pick_high[at, slot * tile:(slot + 1) * tile] = high
            pick_low[at, slot * tile:(slot + 1) * tile] = low
            in_struct[which] = in_struct[which] | (alive & (anc == 2 * z + (x ^ which)))
    grown = dot3((pick_high[...], pick_low[...]), (f_high[...], f_low[...]), NN)
    product[...] = dot3(halves(grown), (d_high[...], d_low[...]), NT)
    for which in range(2):
        at = pl.ds(pl.multiple_of((x ^ which) * part, part), part)
        for flip in range(2):
            lanes = pl.ds(pl.multiple_of((c ^ flip) * half, half), half)
            panel_out[2 * which + flip][...] = jnp.where(in_struct[which], -product[at, lanes], 0.0)
    for step in range(4):
        wide = 2 * width
        w_out[step][...] = product[:, pl.ds(pl.multiple_of((z ^ step) * wide, wide), wide)]


def scaled_kernel(tile, slots, place, f_high, f_low, d_high, d_low, s_high, s_low, base, own_high, own_low):
    z, c = place[0], place[2]
    part = tile // 2
    half = f_high.shape[1] // 2
    wide = base.shape[0]
    for slot in range(slots):
        at = pl.ds(pl.multiple_of(slot * tile + c * part, part), part)
        own_high[slot * part:(slot + 1) * part, :] = f_high[at, :]
        own_low[slot * part:(slot + 1) * part, :] = f_low[at, :]
    scaled = dot3((own_high[...], own_low[...]), (d_high[...], d_low[...]), NT)
    s_high[...], s_low[...] = halves(scaled)
    at = pl.ds(pl.multiple_of(z * wide, wide), wide)
    base[...] = dot3(
        (d_high[at, :half], d_low[at, :half]), (d_high[:, :half], d_low[:, :half]), NT
    )


def diag_kernel(tile, slots, structure, live, place, w0, w1, w2, w3, s_high, s_low, base, *refs):
    outs = refs[:4]
    w_all, pick_high, pick_low, total = refs[4:]
    z, x, c = place[0], place[1], place[2]
    part = tile // 2
    half = outs[0].shape[1]
    width = outs[0].shape[0]
    for step, piece in enumerate((w0, w1, w2, w3)):
        w_all[pl.ds(pl.multiple_of((z ^ step) * tile, tile), tile), :] = piece[...]
    for slot in range(slots):
        value = w_all[pl.ds(pl.multiple_of(structure[x, slot] * part, part), part), :]
        high, low = halves(jnp.where(slot < live[x], value, 0.0))
        pick_high[slot * part:(slot + 1) * part, :] = high
        pick_low[slot * part:(slot + 1) * part, :] = low
    total[...] = base[...] + dot3((pick_high[...], pick_low[...]), (s_high[...], s_low[...]), TN)
    for which in range(2):
        at = pl.ds(pl.multiple_of((x ^ which) * width, width), width)
        for flip in range(2):
            lanes = pl.ds(pl.multiple_of((c ^ flip) * half, half), half)
            outs[2 * which + flip][...] = total[at, lanes]


def last_kernel(place, *refs):
    panel = refs[:4]
    diag = refs[4:8]
    panel_out, diag_out = refs[8:]
    x, c = place[1], place[2]
    half = panel[0].shape[1]
    part = panel[0].shape[0]
    width = diag[0].shape[0]
    blocks = half // 128
    for which in range(2):
        member = x ^ which
        total = diag[2 * which][...] + diag[2 * which + 1][...]
        for block in range(blocks):
            lanes = slice(block * 128, (block + 1) * 128)
            at = pl.ds(2 * block + member, width, stride=2 * blocks)
            diag_out[at, :] = total[:, lanes]
            for flip in range(2):
                first = (c ^ flip) * (part * 2 * blocks) + 2 * block + member
                panel_out[pl.ds(first, part, stride=2 * blocks), :] = panel[2 * which + flip][:, lanes]


def many_rows(ancestor_cov, panel_factor, diag_inverse, structure, live_counts):
    tile_rows = ancestor_cov.shape[0]
    local_blocks = ancestor_cov.shape[1]
    col_count = lax.axis_size("col")
    col_id = lax.axis_index("col")
    row_id = lax.axis_index("row")
    flat_cov = ancestor_cov.reshape(tile_rows, local_blocks * tile_rows)
    half_width = panel_factor.shape[2]
    slot_total = structure.shape[1]
    whole_inverse = lax.all_gather(diag_inverse, "row", axis=2, tiled=True)
    inverse_part = lax.dynamic_slice_in_dim(whole_inverse, col_id * half_width, half_width, 0)
    factor_term = jnp.einsum(
        "rsk,ksn->rsn", panel_factor, inverse_part, precision=lax.Precision.HIGHEST
    )
    slot_index = jnp.arange(slot_total, dtype=jnp.int32)
    slot_alive = slot_index[None, :] < live_counts[:, None]
    own_slot = slot_alive & (structure == row_id)
    in_struct = jnp.any(own_slot, axis=1)
    own_pos = jnp.sum(jnp.where(own_slot, slot_index[None, :], 0), axis=1)
    tile_offsets = jnp.arange(tile_rows, dtype=jnp.int32)
    factor_rows = lax.psum(factor_term, "col")
    arrived = lax.all_gather(factor_rows, "row", axis=0, tiled=True)
    row_count = arrived.shape[0]
    global_row = jnp.arange(row_count, dtype=jnp.int32)
    slot_of = global_row // tile_rows
    offset = global_row % tile_rows
    chooser = (slot_of[:, None] == slot_index[None, :]).astype(jnp.int32)
    product_list = []
    owned_list = []
    for member in range(2):
        anc_block = jnp.sum(chooser * structure[member][None, :], axis=1)
        is_live = slot_of < live_counts[member]
        is_match = is_live & (anc_block % col_count == col_id)
        column_index = anc_block // col_count * tile_rows + offset
        sig_cols = jnp.take(flat_cov, column_index, axis=1)
        weighted = jnp.where(is_match[:, None], arrived[:, member, :], 0.0)
        product_list.append(
            jnp.dot(
                sig_cols,
                weighted,
                precision=lax.Precision.HIGHEST,
                preferred_element_type=jnp.float32,
            )
        )
        source = own_pos[member] * tile_rows + tile_offsets
        in_range = in_struct[member] & (source >= 0) & (source < row_count)
        fetched = jnp.take(arrived[:, member, :], jnp.clip(source, 0, row_count - 1), axis=0)
        owned_list.append(jnp.where(in_range[:, None], fetched, 0.0))
    partial_sum = jnp.stack(product_list, axis=1)
    owned = jnp.stack(owned_list, axis=1)
    summed_all = lax.psum(partial_sum, "col")
    product_half = lax.dynamic_slice_in_dim(summed_all, col_id * half_width, half_width, 2)
    panel_cov = -product_half * in_struct.astype(jnp.float32)[None, :, None]
    spread_term = lax.psum_scatter(
        jnp.einsum("tsi,tsn->isn", owned, product_half, precision=lax.Precision.HIGHEST),
        "row",
        scatter_dimension=0,
        tiled=True,
    )
    inverse_half = lax.dynamic_slice_in_dim(whole_inverse, col_id * half_width, half_width, 2)
    base_term = jnp.einsum(
        "ksi,ksn->isn", diag_inverse, inverse_half, precision=lax.Precision.HIGHEST
    )
    diag_cov = base_term + spread_term
    return (panel_cov, diag_cov)


def local(ancestor_cov, panel_factor, diag_inverse, structure, live_counts):
    rows = lax.axis_size("row")
    if rows != 8:
        return many_rows(ancestor_cov, panel_factor, diag_inverse, structure, live_counts)
    tile = ancestor_cov.shape[0]
    local_blocks = ancestor_cov.shape[1]
    share, _, half = panel_factor.shape
    whole, _, width = diag_inverse.shape
    slots = structure.shape[1]
    col = lax.axis_index("col")
    row = lax.axis_index("row")
    place = jnp.stack([row // 2, row % 2, col]).astype(jnp.int32)
    smem = pl.BlockSpec(memory_space=pltpu.SMEM)
    vmem = pl.BlockSpec(memory_space=pltpu.VMEM)

    def like(*shape, dtype=F32):
        return jax.ShapeDtypeStruct(shape, dtype)

    def call(kernel, name, outs, scalars, arrays, scratch=()):
        return pl.pallas_call(
            kernel,
            out_shape=outs,
            in_specs=[smem] * len(scalars) + [vmem] * len(arrays),
            out_specs=[vmem] * len(outs),
            scratch_shapes=list(scratch),
            compiler_params=pltpu.CompilerParams(vmem_limit_bytes=VMEM_LIMIT),
            name=name,
        )(*scalars, *arrays)

    def move(value, z_step, x_step, flip):
        pairs = [
            (r * 2 + c, (r ^ (2 * z_step + x_step)) * 2 + (c ^ flip))
            for r in range(rows)
            for c in range(2)
        ]
        return lax.ppermute(value, ("row", "col"), pairs)

    factor_lines = (
        panel_factor.reshape(share, 2, half // 128, 128).transpose(0, 2, 1, 3).reshape(-1, 128)
    )
    bundle = share + width
    own, send = call(
        pack_kernel,
        "pack",
        [like(bundle, half)] * 2,
        [place],
        [factor_lines, diag_inverse.transpose(1, 2, 0)],
    )
    near = move(send, 0, 1, 0)
    own_far = move(own, 2, 0, 0)
    own_side = move(own, 1, 0, 0)
    c_own = ancestor_cov.reshape(2, -1, 128)
    c_near = move(c_own, 0, 1, 0)
    near_far = move(near, 2, 0, 0)
    near_side = move(near, 1, 0, 0)
    opposite = move(jnp.concatenate([own_far, near_far]), 1, 0, 0)
    c_both = jnp.stack([c_own, c_near], axis=1)
    c_keep = lax.dynamic_index_in_dim(c_both, col, 0, keepdims=False)
    c_got = move(lax.dynamic_index_in_dim(c_both, 1 - col, 0, keepdims=False), 0, 0, 1)
    theirs = [
        move(jnp.concatenate([own, near]), 0, 0, 1),
        move(jnp.concatenate([own_far, near_far, own_side, near_side]), 0, 0, 1),
        move(opposite, 0, 0, 1),
    ]
    mine = [own, near, own_far, near_far, own_side, near_side, opposite]
    part = tile // 2
    outs = call(
        functools.partial(product_kernel, share, tile, slots),
        "products",
        [like(part, half)] * 4
        + [like(tile, 2 * width)] * 4
        + [like(slots * tile, whole, dtype=BF16)] * 2
        + [like(whole, whole, dtype=BF16)] * 2,
        [structure, live_counts, place],
        [c_keep, c_got] + mine + theirs,
        [
            pltpu.VMEM((tile, slots * tile), BF16),
            pltpu.VMEM((tile, slots * tile), BF16),
            pltpu.VMEM((tile, whole), F32),
        ],
    )
    panel, w, split = outs[:4], outs[4:8], outs[8:]
    w = [w[0]] + [move(w[step], step, 0, 0) for step in range(1, 4)]
    steps = ((0, 0), (0, 1), (1, 0), (1, 1))
    panel = [panel[0]] + [move(v, 0, *s) for v, s in zip(panel[1:], steps[1:])]
    scaled = call(
        functools.partial(scaled_kernel, tile, slots),
        "scaled",
        [like(slots * part, whole, dtype=BF16)] * 2 + [like(2 * width, whole)],
        [place],
        split,
        [pltpu.VMEM((slots * part, whole), BF16)] * 2,
    )
    diag = call(
        functools.partial(diag_kernel, tile, slots),
        "diag_block",
        [like(width, half)] * 4,
        [structure, live_counts, place],
        w + list(scaled),
        [
            pltpu.VMEM((rows * part, 2 * width), F32),
            pltpu.VMEM((slots * part, 2 * width), BF16),
            pltpu.VMEM((slots * part, 2 * width), BF16),
            pltpu.VMEM((2 * width, whole), F32),
        ],
    )
    diag = [diag[0]] + [move(v, 0, *s) for v, s in zip(diag[1:], steps[1:])]
    panel_lines, diag_lines = call(
        last_kernel,
        "outputs",
        [like(tile * 2 * half // 128, 128), like(width * 2 * half // 128, 128)],
        [place],
        panel + diag,
    )

    def unfold(value, count):
        return value.reshape(count, half // 128, 2, 128).transpose(0, 2, 1, 3).reshape(count, 2, half)

    return unfold(panel_lines, tile), unfold(diag_lines, width)


def solution(mesh):
    placed = (
        P(("mp", "row"), None, "col", None),
        P(("mp", "row"), None, "col"),
        P("mp", None, "row"),
        P("mp", None),
        P("mp"),
    )
    return jax.shard_map(
        local,
        mesh=mesh,
        in_specs=placed,
        out_specs=(P(("mp", "row"), None, "col"), P(("mp", "row"), None, "col")),
        check_vma=False,
    )
```

```python
import functools

import jax
import jax.numpy as jnp
from jax import lax
from jax.experimental import pallas as pl
from jax.experimental.pallas import tpu as pltpu
from jax.sharding import PartitionSpec as P

F32 = jnp.float32
BF16 = jnp.bfloat16
NT = (((1,), (1,)), ((), ()))
NN = (((1,), (0,)), ((), ()))
TN = (((0,), (0,)), ((), ()))
VMEM_LIMIT = 20 * 1024 * 1024


def halves(value):
    high = value.astype(BF16)
    low = (value - high.astype(F32)).astype(BF16)
    return high, low


def dot3(left, right, dims):
    left_high, left_low = left
    right_high, right_low = right

    def one(a, b):
        return lax.dot_general(a, b, dims, preferred_element_type=F32)

    return one(left_high, right_low) + one(left_low, right_high) + one(left_high, right_high)


def split(value, high, low, at):
    high[at], low[at] = halves(value)


def pack_kernel(place, factor, inverse, own, send, lines, sem):
    x = place[1]
    c = place[2]
    half = own.shape[1]
    width = inverse.shape[1]
    share = own.shape[0] - width
    blocks = half // 128
    lanes = pl.ds(pl.multiple_of(c * half, half), half)
    copies = [pltpu.make_async_copy(factor, lines, sem.at[0])]
    for index, (out, member) in enumerate(((own, x), (send, 1 - x))):
        copies.append(
            pltpu.make_async_copy(
                inverse.at[member, :, lanes], out.at[pl.ds(share, width), :], sem.at[1 + index]
            )
        )
    for copy in copies:
        copy.start()
    copies[0].wait()
    for out, member in ((own, x), (send, 1 - x)):
        for block in range(blocks):
            at = pl.ds(2 * block + member, share, stride=2 * blocks)
            out[:share, block * 128:(block + 1) * 128] = lines[at, :]
    copies[1].wait()
    copies[2].wait()


def early_kernel(share, tile, slots, structure, live, place, c_own, c_near, c_sib, *refs):
    mine = refs[:6]
    theirs = refs[6]
    grown, last_high, last_low, f_high, f_low, d_high, d_low, pick = refs[7:]
    z, x, c = place[0], place[1], place[2]
    half = theirs.shape[1]
    block = mine[0].shape[0]
    width = block - share
    for index in range(6):
        source = 2 * (z ^ (0, 2, 1)[index // 2]) + (x ^ (index % 2))
        f_at = pl.ds(pl.multiple_of(source * share, share), share)
        d_at = pl.ds(pl.multiple_of(source * width, width), width)
        for first, value in ((0, mine[index]), (half, theirs.at[index * block:(index + 1) * block, :])):
            lanes = slice(first, first + half)
            split(value[:share, :], f_high, f_low, (f_at, lanes))
            split(value[share:, :], d_high, d_low, (d_at, lanes))
    far = 2 * (z ^ 3) * share
    f_at = pl.ds(pl.multiple_of(far, 2 * share), 2 * share)
    f_high[f_at, :] = jnp.zeros((2 * share, 2 * half), BF16)
    f_low[f_at, :] = jnp.zeros((2 * share, 2 * half), BF16)
    blocks = c_own.shape[0] // tile
    for slot in range(slots):
        anc = structure[x, slot]
        rows = pl.ds(anc // 2, tile, stride=blocks)
        other = pl.ds(c_own.shape[0] + anc // 2, tile, stride=blocks)
        for which, (here, there) in enumerate(((c_own, rows), (c_near, other))):
            value = jnp.where(anc % 2 == c, here[rows, :], c_sib[there, :])
            at = pl.ds(pl.multiple_of((x ^ which) * tile, tile), tile)
            pick[at, slot * tile:(slot + 1) * tile] = jnp.where(slot < live[x], value, 0.0)
    picked = pick[...]
    grown[...] = dot3(halves(picked), (f_high[...], f_low[...]), NN)
    total = slots * tile
    turned = pltpu.roll(picked, total - far, 1)
    last_high[...], last_low[...] = halves(turned[:, :last_high.shape[1]])


def product_kernel(share, tile, slots, structure, live, place, *refs):
    grown, last_high, last_low, d_high, d_low, mine, theirs = refs[:7]
    panel_out = refs[7:9]
    w_out = refs[9:13]
    ff_high, ff_low, fd_high, fd_low = refs[13:17]
    product = refs[17]
    z, x, c = place[0], place[1], place[2]
    half = mine.shape[1]
    block = mine.shape[0] // 2
    width = block - share
    for which in range(2):
        first = which * block
        f_at = pl.ds(pl.multiple_of((x ^ which) * share, share), share)
        d_at = pl.ds(pl.multiple_of((x ^ which) * width, width), width)
        for lane, value in ((0, mine), (half, theirs)):
            lanes = slice(lane, lane + half)
            split(value[first:first + share, :], ff_high, ff_low, (f_at, lanes))
            split(value[first + share:first + block, :], fd_high, fd_low, (d_at, lanes))
    wide = 2 * width
    depth = 2 * share
    last = (last_high[:, :depth], last_low[:, :depth])
    value = grown[...] + dot3(last, (ff_high[...], ff_low[...]), NN)
    value = halves(value)
    product[...] = dot3(value, (d_high[...], d_low[...]), NT)
    far = pl.ds(pl.multiple_of((z ^ 3) * wide, wide), wide)
    product[:, far] = dot3(value, (fd_high[...], fd_low[...]), NT)
    lanes = pl.ds(pl.multiple_of(c * half, half), half)
    for which in range(2):
        at = pl.ds(pl.multiple_of((x ^ which) * tile, tile), tile)
        used = False
        for slot in range(slots):
            used = used | ((slot < live[x]) & (structure[x, slot] == 2 * z + (x ^ which)))
        panel_out[which][...] = jnp.where(used, -product[at, lanes], 0.0)
    low_lane = lax.broadcasted_iota(jnp.int32, (tile, wide), 1) < width
    for step in range(4):
        columns = pl.ds(pl.multiple_of((z ^ step) * wide, wide), wide)
        first = product[:tile, columns]
        second = product[tile:, columns]
        left = jnp.where(c == 0, first, pltpu.roll(first, width, 1))
        right = jnp.where(c == 0, pltpu.roll(second, width, 1), second)
        w_out[step][...] = jnp.where(low_lane, left, right)


def scaled_kernel(share, place, *refs):
    f_high, f_low, d_high, d_low, ff_high, ff_low, fd_high, fd_low = refs[:8]
    s_high, s_low, base, all_f_high, all_f_low, all_d_high, all_d_low = refs[8:]
    z, c = place[0], place[2]
    wide = fd_high.shape[0]
    width = wide // 2
    depth = 2 * share
    f_at = pl.ds(pl.multiple_of((z ^ 3) * depth, depth), depth)
    d_at = pl.ds(pl.multiple_of((z ^ 3) * wide, wide), wide)
    for whole, early, late, at in (
        (all_f_high, f_high, ff_high, f_at),
        (all_f_low, f_low, ff_low, f_at),
        (all_d_high, d_high, fd_high, d_at),
        (all_d_low, d_low, fd_low, d_at),
    ):
        whole[...] = early[...]
        whole[at, :] = late[...]
    inverse = (all_d_high[...], all_d_low[...])
    scaled = dot3((all_f_high[...], all_f_low[...]), inverse, NT)
    s_high[...], s_low[...] = halves(scaled)
    at = pl.ds(pl.multiple_of((2 * z + c) * width, width), width)
    base[...] = dot3((all_d_high[at, :], all_d_low[at, :]), inverse, NT)


def diag_kernel(tile, slots, structure, live, place, w0, w1, w2, w3, s_high, s_low, base, *refs):
    keep, cross, w_all, pick_high, pick_low, total = refs
    z, x = place[0], place[1]
    half = keep.shape[1]
    width = keep.shape[0]
    for step, piece in enumerate((w0, w1, w2, w3)):
        w_all[z ^ step] = piece[...]
    for slot in range(slots):
        anc = structure[x, slot]
        value = w_all[anc // 2]
        value = jnp.where(anc % 2 == 0, value, pltpu.roll(value, width, 1))
        at = slice(slot * tile, (slot + 1) * tile)
        split(jnp.where(slot < live[x], value, 0.0), pick_high, pick_low, (at, slice(None)))
    picked = (pick_high[...], pick_low[...])
    total[...] = base[...] + dot3(picked, (s_high[...], s_low[...]), TN)[:width]
    keep[...] = total[:, pl.ds(pl.multiple_of(x * half, half), half)]
    cross[...] = total[:, pl.ds(pl.multiple_of((1 - x) * half, half), half)]


def lines_kernel(place, mine, other, out):
    x = place[1]
    blocks = mine.shape[1] // 128
    for member, value in ((x, mine), (1 - x, other)):
        for block in range(blocks):
            at = pl.ds(2 * block + member, mine.shape[0], stride=2 * blocks)
            out[at, :] = value[:, block * 128:(block + 1) * 128]


def diag_lines_kernel(place, keep, met, far, out):
    x, c = place[1], place[2]
    blocks = keep.shape[1] // 128
    mine = jnp.where(c == x, keep[...], met[...])
    other = jnp.where(c == x, met[...], far[...])
    for member, value in ((x, mine), (1 - x, other)):
        for block in range(blocks):
            at = pl.ds(2 * block + member, keep.shape[0], stride=2 * blocks)
            out[at, :] = value[:, block * 128:(block + 1) * 128]


def many_rows(ancestor_cov, panel_factor, diag_inverse, structure, live_counts):
    tile_rows = ancestor_cov.shape[0]
    local_blocks = ancestor_cov.shape[1]
    col_count = lax.axis_size("col")
    col_id = lax.axis_index("col")
    row_id = lax.axis_index("row")
    flat_cov = ancestor_cov.reshape(tile_rows, local_blocks * tile_rows)
    half_width = panel_factor.shape[2]
    slot_total = structure.shape[1]
    whole_inverse = lax.all_gather(diag_inverse, "row", axis=2, tiled=True)
    inverse_part = lax.dynamic_slice_in_dim(whole_inverse, col_id * half_width, half_width, 0)
    factor_term = jnp.einsum(
        "rsk,ksn->rsn", panel_factor, inverse_part, precision=lax.Precision.HIGHEST
    )
    slot_index = jnp.arange(slot_total, dtype=jnp.int32)
    slot_alive = slot_index[None, :] < live_counts[:, None]
    own_slot = slot_alive & (structure == row_id)
    in_struct = jnp.any(own_slot, axis=1)
    own_pos = jnp.sum(jnp.where(own_slot, slot_index[None, :], 0), axis=1)
    tile_offsets = jnp.arange(tile_rows, dtype=jnp.int32)
    factor_rows = lax.psum(factor_term, "col")
    arrived = lax.all_gather(factor_rows, "row", axis=0, tiled=True)
    row_count = arrived.shape[0]
    global_row = jnp.arange(row_count, dtype=jnp.int32)
    slot_of = global_row // tile_rows
    offset = global_row % tile_rows
    chooser = (slot_of[:, None] == slot_index[None, :]).astype(jnp.int32)
    product_list = []
    owned_list = []
    for member in range(2):
        anc_block = jnp.sum(chooser * structure[member][None, :], axis=1)
        is_live = slot_of < live_counts[member]
        is_match = is_live & (anc_block % col_count == col_id)
        column_index = anc_block // col_count * tile_rows + offset
        sig_cols = jnp.take(flat_cov, column_index, axis=1)
        weighted = jnp.where(is_match[:, None], arrived[:, member, :], 0.0)
        product_list.append(
            jnp.dot(
                sig_cols,
                weighted,
                precision=lax.Precision.HIGHEST,
                preferred_element_type=jnp.float32,
            )
        )
        source = own_pos[member] * tile_rows + tile_offsets
        in_range = in_struct[member] & (source >= 0) & (source < row_count)
        fetched = jnp.take(arrived[:, member, :], jnp.clip(source, 0, row_count - 1), axis=0)
        owned_list.append(jnp.where(in_range[:, None], fetched, 0.0))
    partial_sum = jnp.stack(product_list, axis=1)
    owned = jnp.stack(owned_list, axis=1)
    summed_all = lax.psum(partial_sum, "col")
    product_half = lax.dynamic_slice_in_dim(summed_all, col_id * half_width, half_width, 2)
    panel_cov = -product_half * in_struct.astype(jnp.float32)[None, :, None]
    spread_term = lax.psum_scatter(
        jnp.einsum("tsi,tsn->isn", owned, product_half, precision=lax.Precision.HIGHEST),
        "row",
        scatter_dimension=0,
        tiled=True,
    )
    inverse_half = lax.dynamic_slice_in_dim(whole_inverse, col_id * half_width, half_width, 2)
    base_term = jnp.einsum(
        "ksi,ksn->isn", diag_inverse, inverse_half, precision=lax.Precision.HIGHEST
    )
    diag_cov = base_term + spread_term
    return (panel_cov, diag_cov)


def local(ancestor_cov, panel_factor, diag_inverse, structure, live_counts):
    rows = lax.axis_size("row")
    if rows != 8:
        return many_rows(ancestor_cov, panel_factor, diag_inverse, structure, live_counts)
    tile = ancestor_cov.shape[0]
    share, _, half = panel_factor.shape
    whole, _, width = diag_inverse.shape
    slots = structure.shape[1]
    col = lax.axis_index("col")
    row = lax.axis_index("row")
    place = jnp.stack([row // 2, row % 2, col]).astype(jnp.int32)
    smem = pl.BlockSpec(memory_space=pltpu.SMEM)
    vmem = pl.BlockSpec(memory_space=pltpu.VMEM)

    def like(*shape, dtype=F32):
        return jax.ShapeDtypeStruct(shape, dtype)

    def call(kernel, name, outs, scalars, arrays, scratch=(), space=vmem, limit=VMEM_LIMIT):
        return pl.pallas_call(
            kernel,
            out_shape=outs,
            in_specs=[smem] * len(scalars) + [space] * len(arrays),
            out_specs=[vmem] * len(outs),
            scratch_shapes=list(scratch),
            compiler_params=pltpu.CompilerParams(vmem_limit_bytes=limit),
            name=name,
        )(*scalars, *arrays)

    def send_to(value, target):
        pairs = []
        for r in range(rows):
            for c in range(2):
                to = target(r // 2, r % 2, c)
                if to is not None:
                    pairs.append((r * 2 + c, (to[0] * 2 + to[1]) * 2 + to[2]))
        return lax.ppermute(value, ("row", "col"), pairs)

    def move(value, z_step, x_step, flip):
        return send_to(value, lambda z, x, c: (z ^ z_step, x ^ x_step, c ^ flip))

    factor_lines = (
        panel_factor.reshape(share, 2, half // 128, 128).transpose(0, 2, 1, 3).reshape(-1, 128)
    )
    bundle = share + width
    own, send = call(
        pack_kernel,
        "pack",
        [like(bundle, half)] * 2,
        [place],
        [factor_lines, diag_inverse.transpose(1, 2, 0)],
        [pltpu.VMEM(factor_lines.shape, F32), pltpu.SemaphoreType.DMA((3,))],
        pl.BlockSpec(memory_space=pl.ANY),
        60 * 1024 * 1024,
    )
    c_own = ancestor_cov.reshape(-1, 128)
    own_side = move(own, 1, 0, 0)
    near = move(send, 0, 1, 0)
    own_far = move(own, 2, 0, 0)
    c_near = move(c_own, 0, 1, 0)
    near_far = move(near, 2, 0, 0)
    near_side = move(near, 1, 0, 0)
    own_far, near_far, c_near = lax.optimization_barrier((own_far, near_far, c_near))
    opposite = move(jnp.concatenate([own_far, near_far]), 1, 0, 0)
    c_sib = move(jnp.concatenate([c_own, c_near]), 0, 0, 1)
    mine = [own, near, own_far, near_far, own_side, near_side]
    theirs = move(jnp.concatenate(mine), 0, 0, 1)
    split_f = [like(slots * tile, whole, dtype=BF16)] * 2
    split_d = [like(whole, whole, dtype=BF16)] * 2
    grown, last_high, last_low, f_high, f_low, d_high, d_low = call(
        functools.partial(early_kernel, share, tile, slots),
        "early",
        [like(2 * tile, whole)] + [like(2 * tile, 256, dtype=BF16)] * 2 + split_f + split_d,
        [structure, live_counts, place],
        [c_own, c_near, c_sib] + mine + [theirs],
        [pltpu.VMEM((2 * tile, slots * tile), F32)],
    )
    opposite, grown = lax.optimization_barrier((opposite, grown))
    opposite_theirs = move(opposite, 0, 0, 1)
    outs = call(
        functools.partial(product_kernel, share, tile, slots),
        "products",
        [like(tile, half)] * 2
        + [like(tile, 2 * width)] * 4
        + [like(2 * share, whole, dtype=BF16)] * 2
        + [like(2 * width, whole, dtype=BF16)] * 2,
        [structure, live_counts, place],
        [grown, last_high, last_low, d_high, d_low, opposite, opposite_theirs],
        [pltpu.VMEM((2 * tile, whole), F32)],
    )
    panel, w, late = outs[:2], outs[2:6], outs[6:]
    w = [w[0]] + [move(w[step], step, 0, 0) for step in range(1, 4)]
    panel_got = move(panel[1], 0, 1, 0)
    s_high, s_low, base = call(
        functools.partial(scaled_kernel, share),
        "scaled",
        split_f + [like(width, whole)],
        [place],
        [f_high, f_low, d_high, d_low, *late],
        [pltpu.VMEM(s.shape, BF16) for s in split_f + split_d],
    )
    keep, cross = call(
        functools.partial(diag_kernel, tile, slots),
        "diag_block",
        [like(width, half)] * 2,
        [structure, live_counts, place],
        [*w, s_high, s_low, base],
        [
            pltpu.VMEM((rows // 2, tile, 2 * width), F32),
            pltpu.VMEM((slots * tile, 2 * width), BF16),
            pltpu.VMEM((slots * tile, 2 * width), BF16),
            pltpu.VMEM((width, whole), F32),
        ],
    )
    met = send_to(cross, lambda z, x, c: (z, x, 1 - c) if c == x else (z, 1 - x, c))
    far = send_to(keep, lambda z, x, c: None if c == x else (z, 1 - x, 1 - c))
    lines = 2 * half // 128
    (panel_lines,) = call(
        lines_kernel, "panel_lines", [like(tile * lines, 128)], [place], [panel[0], panel_got]
    )
    (diag_lines,) = call(
        diag_lines_kernel, "diag_lines", [like(width * lines, 128)], [place], [keep, met, far]
    )

    def unfold(value, count):
        return value.reshape(count, half // 128, 2, 128).transpose(0, 2, 1, 3).reshape(count, 2, half)

    return unfold(panel_lines, tile), unfold(diag_lines, width)


def solution(mesh):
    placed = (
        P(("mp", "row"), None, "col", None),
        P(("mp", "row"), None, "col"),
        P("mp", None, "row"),
        P("mp", None),
        P("mp"),
    )
    return jax.shard_map(
        local,
        mesh=mesh,
        in_specs=placed,
        out_specs=(P(("mp", "row"), None, "col"), P(("mp", "row"), None, "col")),
        check_vma=False,
    )
```

```python
import functools

import jax
import jax.numpy as jnp
from jax import lax
from jax.experimental import pallas as pl
from jax.experimental.pallas import tpu as pltpu
from jax.sharding import PartitionSpec as P

F32 = jnp.float32
BF16 = jnp.bfloat16
NT = (((1,), (1,)), ((), ()))
NN = (((1,), (0,)), ((), ()))
TN = (((0,), (0,)), ((), ()))
VMEM_LIMIT = 20 * 1024 * 1024
PACK_LIMIT = 60 * 1024 * 1024


def halves(value):
    high = value.astype(BF16)
    low = (value - high.astype(F32)).astype(BF16)
    return high, low


def dot3(left, right, dims):
    left_high, left_low = left
    right_high, right_low = right

    def one(a, b):
        return lax.dot_general(a, b, dims, preferred_element_type=F32)

    return one(left_high, right_low) + one(left_low, right_high) + one(left_high, right_high)


def split(value, high, low, at):
    high[at], low[at] = halves(value)


def pack_kernel(factor, inverse, cov, own, send, near, lines, held, sem):
    x = lax.axis_index("row") % 2
    c = lax.axis_index("col")
    width = held.shape[1]
    blocks = held.shape[2] // 128
    block = own.shape[0] // blocks
    share = block - width
    lanes = pl.ds(pl.multiple_of(c * held.shape[2], held.shape[2]), held.shape[2])
    copies = [
        pltpu.make_async_copy(factor, lines, sem.at[0]),
        pltpu.make_async_copy(inverse.at[:, :, lanes], held, sem.at[1]),
        pltpu.make_async_copy(cov, near.at[pl.ds(own.shape[0], cov.shape[0]), :], sem.at[2]),
    ]
    for copy in copies:
        copy.start()
    copies[0].wait()
    copies[1].wait()
    for outs, member in (((own,), x), ((send, near), 1 - x)):
        for b in range(blocks):
            rows = lines[pl.ds(2 * b + member, share, stride=2 * blocks), :]
            cols = held[member, :, b * 128:(b + 1) * 128]
            for out in outs:
                out[b * block:b * block + share, :] = rows
                out[b * block + share:(b + 1) * block, :] = cols
    copies[2].wait()


def early_kernel(share, tile, slots, structure, live, place, c_own, *refs):
    mine = refs[:7]
    theirs = refs[7]
    grown, last_high, last_low, f_high, f_low, d_high, d_low, pick = refs[8:]
    z, x, c = place[0], place[1], place[2]
    size = mine[0].shape[0]
    whole = d_high.shape[0]
    half = whole // 2
    lane_blocks = half // 128
    block = size // lane_blocks
    width = block - share
    near_x = 1 - x
    sources = (
        2 * z + x,
        2 * (z ^ 2) + x,
        2 * (z ^ 2) + near_x,
        2 * (z ^ 1) + x,
        2 * (z ^ 1) + near_x,
        2 * (z ^ 3) + x,
        2 * z + near_x,
    )
    for index, source in enumerate(sources):
        f_at = pl.ds(pl.multiple_of(source * share, share), share)
        d_at = pl.ds(pl.multiple_of(source * width, width), width)
        for first, ref, start in ((0, mine[index], 0), (half, theirs, index * size)):
            for b in range(lane_blocks):
                lanes = slice(first + b * 128, first + (b + 1) * 128)
                top = start + b * block
                split(ref[top:top + share, :], f_high, f_low, (f_at, lanes))
                split(ref[top + share:top + block, :], d_high, d_low, (d_at, lanes))
    last = (2 * (z ^ 3) + near_x) * share
    f_at = pl.ds(pl.multiple_of(last, share), share)
    f_high[f_at, :] = jnp.zeros((share, whole), BF16)
    f_low[f_at, :] = jnp.zeros((share, whole), BF16)
    d_at = pl.ds(pl.multiple_of((2 * (z ^ 3) + near_x) * width, width), width)
    d_high[d_at, :] = jnp.zeros((width, whole), BF16)
    d_low[d_at, :] = jnp.zeros((width, whole), BF16)
    blocks = c_own.shape[0] // tile
    for slot in range(slots):
        anc = structure[x, slot]
        for which, (here, start, offset) in enumerate(
            ((c_own, 0, 7 * size + c_own.shape[0]), (mine[6], size, 7 * size))
        ):
            here_at = pl.ds(start + anc // 2, tile, stride=blocks)
            there_at = pl.ds(offset + anc // 2, tile, stride=blocks)
            value = jnp.where(anc % 2 == c, here[here_at, :], theirs[there_at, :])
            at = pl.ds(pl.multiple_of((x ^ which) * tile, tile), tile)
            pick[at, slot * tile:(slot + 1) * tile] = jnp.where(slot < live[x], value, 0.0)
    picked = pick[...]
    grown[...] = dot3(halves(picked), (f_high[...], f_low[...]), NN)
    total = slots * tile
    turned = pltpu.roll(picked, total - last, 1)
    last_high[...], last_low[...] = halves(turned[:, :last_high.shape[1]])


def product_kernel(share, tile, slots, structure, live, place, *refs):
    grown, last_high, last_low, d_high, d_low, mine, theirs = refs[:7]
    panel_out = refs[7:9]
    w_out = refs[9:13]
    ff_high, ff_low, fd_high, fd_low = refs[13:17]
    product = refs[17]
    z, x, c = place[0], place[1], place[2]
    wide = fd_high.shape[0]
    width = wide // 2
    half = d_high.shape[0] // 2
    lane_blocks = half // 128
    block = share + width
    far = pl.ds(pl.multiple_of((z ^ 3) * wide, wide), wide)
    fd_high[...] = d_high[far, :]
    fd_low[...] = d_low[far, :]
    d_at = pl.ds(pl.multiple_of((1 - x) * width, width), width)
    for first, ref in ((0, mine), (half, theirs)):
        for b in range(lane_blocks):
            lanes = slice(first + b * 128, first + (b + 1) * 128)
            top = b * block
            split(ref[top:top + share, :], ff_high, ff_low, (slice(None), lanes))
            split(ref[top + share:top + block, :], fd_high, fd_low, (d_at, lanes))
    last = (last_high[:, :share], last_low[:, :share])
    value = grown[...] + dot3(last, (ff_high[...], ff_low[...]), NN)
    value = halves(value)
    product[...] = dot3(value, (d_high[...], d_low[...]), NT)
    product[:, far] = dot3(value, (fd_high[...], fd_low[...]), NT)
    lanes = pl.ds(pl.multiple_of(c * half, half), half)
    for which in range(2):
        at = pl.ds(pl.multiple_of((x ^ which) * tile, tile), tile)
        used = False
        for slot in range(slots):
            used = used | ((slot < live[x]) & (structure[x, slot] == 2 * z + (x ^ which)))
        panel_out[which][...] = jnp.where(used, -product[at, lanes], 0.0)
    low_lane = lax.broadcasted_iota(jnp.int32, (tile, wide), 1) < width
    for step in range(4):
        columns = pl.ds(pl.multiple_of((z ^ step) * wide, wide), wide)
        first = product[:tile, columns]
        second = product[tile:, columns]
        left = jnp.where(c == 0, first, pltpu.roll(first, width, 1))
        right = jnp.where(c == 0, pltpu.roll(second, width, 1), second)
        w_out[step][...] = jnp.where(low_lane, left, right)


def scaled_kernel(share, place, *refs):
    f_high, f_low, d_high, d_low, ff_high, ff_low, fd_high, fd_low = refs[:8]
    s_high, s_low, base, all_f_high, all_f_low, all_d_high, all_d_low = refs[8:]
    z, x, c = place[0], place[1], place[2]
    wide = fd_high.shape[0]
    width = wide // 2
    f_at = pl.ds(pl.multiple_of((2 * (z ^ 3) + 1 - x) * share, share), share)
    d_at = pl.ds(pl.multiple_of((z ^ 3) * wide, wide), wide)
    for whole, early, late, at in (
        (all_f_high, f_high, ff_high, f_at),
        (all_f_low, f_low, ff_low, f_at),
        (all_d_high, d_high, fd_high, d_at),
        (all_d_low, d_low, fd_low, d_at),
    ):
        whole[...] = early[...]
        whole[at, :] = late[...]
    inverse = (all_d_high[...], all_d_low[...])
    scaled = dot3((all_f_high[...], all_f_low[...]), inverse, NT)
    s_high[...], s_low[...] = halves(scaled)
    at = pl.ds(pl.multiple_of((2 * z + c) * width, width), width)
    base[...] = dot3((all_d_high[at, :], all_d_low[at, :]), inverse, NT)


def diag_kernel(tile, slots, structure, live, place, w0, w1, w2, w3, s_high, s_low, base, *refs):
    keep, cross, w_all, pick_high, pick_low, total = refs
    z, x = place[0], place[1]
    half = keep.shape[1]
    width = keep.shape[0]
    for step, piece in enumerate((w0, w1, w2, w3)):
        w_all[z ^ step] = piece[...]
    for slot in range(slots):
        anc = structure[x, slot]
        value = w_all[anc // 2]
        value = jnp.where(anc % 2 == 0, value, pltpu.roll(value, width, 1))
        at = slice(slot * tile, (slot + 1) * tile)
        split(jnp.where(slot < live[x], value, 0.0), pick_high, pick_low, (at, slice(None)))
    picked = (pick_high[...], pick_low[...])
    total[...] = base[...] + dot3(picked, (s_high[...], s_low[...]), TN)[:width]
    keep[...] = total[:, pl.ds(pl.multiple_of(x * half, half), half)]
    cross[...] = total[:, pl.ds(pl.multiple_of((1 - x) * half, half), half)]


def lines_kernel(place, mine, other, out):
    x = place[1]
    blocks = mine.shape[1] // 128
    for member, value in ((x, mine), (1 - x, other)):
        for block in range(blocks):
            at = pl.ds(2 * block + member, mine.shape[0], stride=2 * blocks)
            out[at, :] = value[:, block * 128:(block + 1) * 128]


def diag_lines_kernel(place, keep, met, far, out):
    x, c = place[1], place[2]
    blocks = keep.shape[1] // 128
    mine = jnp.where(c == x, keep[...], met[...])
    other = jnp.where(c == x, met[...], far[...])
    for member, value in ((x, mine), (1 - x, other)):
        for block in range(blocks):
            at = pl.ds(2 * block + member, keep.shape[0], stride=2 * blocks)
            out[at, :] = value[:, block * 128:(block + 1) * 128]


def many_rows(ancestor_cov, panel_factor, diag_inverse, structure, live_counts):
    tile_rows = ancestor_cov.shape[0]
    local_blocks = ancestor_cov.shape[1]
    col_count = lax.axis_size("col")
    col_id = lax.axis_index("col")
    row_id = lax.axis_index("row")
    flat_cov = ancestor_cov.reshape(tile_rows, local_blocks * tile_rows)
    half_width = panel_factor.shape[2]
    slot_total = structure.shape[1]
    whole_inverse = lax.all_gather(diag_inverse, "row", axis=2, tiled=True)
    inverse_part = lax.dynamic_slice_in_dim(whole_inverse, col_id * half_width, half_width, 0)
    factor_term = jnp.einsum(
        "rsk,ksn->rsn", panel_factor, inverse_part, precision=lax.Precision.HIGHEST
    )
    slot_index = jnp.arange(slot_total, dtype=jnp.int32)
    slot_alive = slot_index[None, :] < live_counts[:, None]
    own_slot = slot_alive & (structure == row_id)
    in_struct = jnp.any(own_slot, axis=1)
    own_pos = jnp.sum(jnp.where(own_slot, slot_index[None, :], 0), axis=1)
    tile_offsets = jnp.arange(tile_rows, dtype=jnp.int32)
    factor_rows = lax.psum(factor_term, "col")
    arrived = lax.all_gather(factor_rows, "row", axis=0, tiled=True)
    row_count = arrived.shape[0]
    global_row = jnp.arange(row_count, dtype=jnp.int32)
    slot_of = global_row // tile_rows
    offset = global_row % tile_rows
    chooser = (slot_of[:, None] == slot_index[None, :]).astype(jnp.int32)
    product_list = []
    owned_list = []
    for member in range(2):
        anc_block = jnp.sum(chooser * structure[member][None, :], axis=1)
        is_live = slot_of < live_counts[member]
        is_match = is_live & (anc_block % col_count == col_id)
        column_index = anc_block // col_count * tile_rows + offset
        sig_cols = jnp.take(flat_cov, column_index, axis=1)
        weighted = jnp.where(is_match[:, None], arrived[:, member, :], 0.0)
        product_list.append(
            jnp.dot(
                sig_cols,
                weighted,
                precision=lax.Precision.HIGHEST,
                preferred_element_type=jnp.float32,
            )
        )
        source = own_pos[member] * tile_rows + tile_offsets
        in_range = in_struct[member] & (source >= 0) & (source < row_count)
        fetched = jnp.take(arrived[:, member, :], jnp.clip(source, 0, row_count - 1), axis=0)
        owned_list.append(jnp.where(in_range[:, None], fetched, 0.0))
    partial_sum = jnp.stack(product_list, axis=1)
    owned = jnp.stack(owned_list, axis=1)
    summed_all = lax.psum(partial_sum, "col")
    product_half = lax.dynamic_slice_in_dim(summed_all, col_id * half_width, half_width, 2)
    panel_cov = -product_half * in_struct.astype(jnp.float32)[None, :, None]
    spread_term = lax.psum_scatter(
        jnp.einsum("tsi,tsn->isn", owned, product_half, precision=lax.Precision.HIGHEST),
        "row",
        scatter_dimension=0,
        tiled=True,
    )
    inverse_half = lax.dynamic_slice_in_dim(whole_inverse, col_id * half_width, half_width, 2)
    base_term = jnp.einsum(
        "ksi,ksn->isn", diag_inverse, inverse_half, precision=lax.Precision.HIGHEST
    )
    diag_cov = base_term + spread_term
    return (panel_cov, diag_cov)


def local(ancestor_cov, panel_factor, diag_inverse, structure, live_counts):
    rows = lax.axis_size("row")
    if rows != 8:
        return many_rows(ancestor_cov, panel_factor, diag_inverse, structure, live_counts)
    tile = ancestor_cov.shape[0]
    share, _, half = panel_factor.shape
    whole, _, width = diag_inverse.shape
    slots = structure.shape[1]
    col = lax.axis_index("col")
    row = lax.axis_index("row")
    place = jnp.stack([row // 2, row % 2, col]).astype(jnp.int32)
    smem = pl.BlockSpec(memory_space=pltpu.SMEM)
    vmem = pl.BlockSpec(memory_space=pltpu.VMEM)

    def like(*shape, dtype=F32):
        return jax.ShapeDtypeStruct(shape, dtype)

    def call(kernel, name, outs, scalars, arrays, scratch=(), space=vmem, limit=VMEM_LIMIT):
        return pl.pallas_call(
            kernel,
            out_shape=outs,
            in_specs=[smem] * len(scalars) + [space] * len(arrays),
            out_specs=[vmem] * len(outs),
            scratch_shapes=list(scratch),
            compiler_params=pltpu.CompilerParams(vmem_limit_bytes=limit),
            name=name,
        )(*scalars, *arrays)

    def send_to(value, target):
        pairs = []
        for r in range(rows):
            for c in range(2):
                to = target(r // 2, r % 2, c)
                if to is not None:
                    pairs.append((r * 2 + c, (to[0] * 2 + to[1]) * 2 + to[2]))
        return lax.ppermute(value, ("row", "col"), pairs)

    def move(value, z_step, x_step, flip):
        return send_to(value, lambda z, x, c: (z ^ z_step, x ^ x_step, c ^ flip))

    factor_lines = (
        panel_factor.reshape(share, 2, half // 128, 128).transpose(0, 2, 1, 3).reshape(-1, 128)
    )
    c_own = ancestor_cov.reshape(-1, 128)
    bundle = (share + width) * half // 128
    own, send, send_near = call(
        pack_kernel,
        "pack",
        [like(bundle, 128)] * 2 + [like(bundle + c_own.shape[0], 128)],
        [],
        [factor_lines, diag_inverse.transpose(1, 2, 0), c_own],
        [
            pltpu.VMEM(factor_lines.shape, F32),
            pltpu.VMEM((2, width, half), F32),
            pltpu.SemaphoreType.DMA((3,)),
        ],
        pl.BlockSpec(memory_space=pl.ANY),
        PACK_LIMIT,
    )
    own_far = move(own, 2, 0, 0)
    near_far = move(send, 2, 1, 0)
    own_side = move(own, 1, 0, 0)
    near_side = move(send, 1, 1, 0)
    near = move(send_near, 0, 1, 0)
    own_opposite = move(own_far, 1, 0, 0)
    near_opposite = move(near_far, 1, 0, 0)
    mine = [own, own_far, near_far, own_side, near_side, own_opposite, near]
    theirs = move(jnp.concatenate([*mine, c_own]), 0, 0, 1)
    split_f = [like(slots * tile, whole, dtype=BF16)] * 2
    split_d = [like(whole, whole, dtype=BF16)] * 2
    grown, last_high, last_low, f_high, f_low, d_high, d_low = call(
        functools.partial(early_kernel, share, tile, slots),
        "early",
        [like(2 * tile, whole)] + [like(2 * tile, 128, dtype=BF16)] * 2 + split_f + split_d,
        [structure, live_counts, place],
        [c_own, *mine, theirs],
        [pltpu.VMEM((2 * tile, slots * tile), F32)],
    )
    near_opposite, grown = lax.optimization_barrier((near_opposite, grown))
    opposite_theirs = move(near_opposite, 0, 0, 1)
    outs = call(
        functools.partial(product_kernel, share, tile, slots),
        "products",
        [like(tile, half)] * 2
        + [like(tile, 2 * width)] * 4
        + [like(share, whole, dtype=BF16)] * 2
        + [like(2 * width, whole, dtype=BF16)] * 2,
        [structure, live_counts, place],
        [grown, last_high, last_low, d_high, d_low, near_opposite, opposite_theirs],
        [pltpu.VMEM((2 * tile, whole), F32)],
    )
    panel, w, late = outs[:2], outs[2:6], outs[6:]
    w = [w[0]] + [move(w[step], step, 0, 0) for step in range(1, 4)]
    panel_got = move(panel[1], 0, 1, 0)
    s_high, s_low, base = call(
        functools.partial(scaled_kernel, share),
        "scaled",
        split_f + [like(width, whole)],
        [place],
        [f_high, f_low, d_high, d_low, *late],
        [pltpu.VMEM(s.shape, BF16) for s in split_f + split_d],
    )
    keep, cross = call(
        functools.partial(diag_kernel, tile, slots),
        "diag_block",
        [like(width, half)] * 2,
        [structure, live_counts, place],
        [*w, s_high, s_low, base],
        [
            pltpu.VMEM((rows // 2, tile, 2 * width), F32),
            pltpu.VMEM((slots * tile, 2 * width), BF16),
            pltpu.VMEM((slots * tile, 2 * width), BF16),
            pltpu.VMEM((width, whole), F32),
        ],
    )
    met = send_to(cross, lambda z, x, c: (z, x, 1 - c) if c == x else (z, 1 - x, c))
    far = send_to(keep, lambda z, x, c: None if c == x else (z, 1 - x, 1 - c))
    lines = 2 * half // 128
    panel_got, keep = lax.optimization_barrier((panel_got, keep))
    (panel_lines,) = call(
        lines_kernel, "panel_lines", [like(tile * lines, 128)], [place], [panel[0], panel_got]
    )
    panel_lines, keep = lax.optimization_barrier((panel_lines, keep))
    (diag_lines,) = call(
        diag_lines_kernel, "diag_lines", [like(width * lines, 128)], [place], [keep, met, far]
    )

    def unfold(value, count):
        return value.reshape(count, half // 128, 2, 128).transpose(0, 2, 1, 3).reshape(count, 2, half)

    return unfold(panel_lines, tile), unfold(diag_lines, width)


def solution(mesh):
    placed = (
        P(("mp", "row"), None, "col", None),
        P(("mp", "row"), None, "col"),
        P("mp", None, "row"),
        P("mp", None),
        P("mp"),
    )
    return jax.shard_map(
        local,
        mesh=mesh,
        in_specs=placed,
        out_specs=(P(("mp", "row"), None, "col"), P(("mp", "row"), None, "col")),
        check_vma=False,
    )
```

```python
import functools

import jax
import jax.numpy as jnp
from jax import lax
from jax.experimental import pallas as pl
from jax.experimental.pallas import tpu as pltpu
from jax.sharding import PartitionSpec as P

F32 = jnp.float32
BF16 = jnp.bfloat16
NT = (((1,), (1,)), ((), ()))
NN = (((1,), (0,)), ((), ()))
TN = (((0,), (0,)), ((), ()))
VMEM_LIMIT = 20 * 1024 * 1024


def halves(value):
    high = value.astype(BF16)
    low = (value - high.astype(F32)).astype(BF16)
    return high, low


def dot3(left, right, dims):
    left_high, left_low = left
    right_high, right_low = right

    def one(a, b):
        return lax.dot_general(a, b, dims, preferred_element_type=F32)

    return one(left_high, right_low) + one(left_low, right_high) + one(left_high, right_high)


def split(value, high, low, at):
    high[at], low[at] = halves(value)


def pack_kernel(factor, inverse, cov, own, send, near, lines, held, sem):
    x = lax.axis_index("row") % 2
    c = lax.axis_index("col")
    width = held.shape[1]
    blocks = held.shape[2] // 128
    block = own.shape[0] // blocks
    share = block - width
    lanes = pl.ds(pl.multiple_of(c * held.shape[2], held.shape[2]), held.shape[2])
    copies = [
        pltpu.make_async_copy(factor, lines, sem.at[0]),
        pltpu.make_async_copy(inverse.at[:, :, lanes], held, sem.at[1]),
        pltpu.make_async_copy(cov, near.at[pl.ds(own.shape[0], cov.shape[0]), :], sem.at[2]),
    ]
    for copy in copies:
        copy.start()
    copies[0].wait()
    copies[1].wait()
    for outs, member in (((own,), x), ((send, near), 1 - x)):
        for b in range(blocks):
            rows = lines[pl.ds(2 * b + member, share, stride=2 * blocks), :]
            cols = held[member, :, b * 128:(b + 1) * 128]
            for out in outs:
                out[b * block:b * block + share, :] = rows
                out[b * block + share:(b + 1) * block, :] = cols
    copies[2].wait()


def early_kernel(share, tile, slots, structure, live, place, c_own, *refs):
    mine = refs[:7]
    theirs = refs[7]
    grown, last_high, last_low, f_high, f_low, d_high, d_low, pick = refs[8:]
    z, x, c = place[0], place[1], place[2]
    size = mine[0].shape[0]
    whole = d_high.shape[0]
    half = whole // 2
    lane_blocks = half // 128
    block = size // lane_blocks
    width = block - share
    near_x = 1 - x
    sources = (
        2 * z + x,
        2 * (z ^ 2) + x,
        2 * (z ^ 2) + near_x,
        2 * (z ^ 1) + x,
        2 * (z ^ 1) + near_x,
        2 * (z ^ 3) + x,
        2 * z + near_x,
    )
    for index, source in enumerate(sources):
        f_at = pl.ds(pl.multiple_of(source * share, share), share)
        d_at = pl.ds(pl.multiple_of(source * width, width), width)
        for first, ref, start in ((0, mine[index], 0), (half, theirs, index * size)):
            for b in range(lane_blocks):
                lanes = slice(first + b * 128, first + (b + 1) * 128)
                top = start + b * block
                split(ref[top:top + share, :], f_high, f_low, (f_at, lanes))
                split(ref[top + share:top + block, :], d_high, d_low, (d_at, lanes))
    last = (2 * (z ^ 3) + near_x) * share
    f_at = pl.ds(pl.multiple_of(last, share), share)
    f_high[f_at, :] = jnp.zeros((share, whole), BF16)
    f_low[f_at, :] = jnp.zeros((share, whole), BF16)
    d_at = pl.ds(pl.multiple_of((2 * (z ^ 3) + near_x) * width, width), width)
    d_high[d_at, :] = jnp.zeros((width, whole), BF16)
    d_low[d_at, :] = jnp.zeros((width, whole), BF16)
    blocks = c_own.shape[0] // tile
    for slot in range(slots):
        anc = structure[x, slot]
        for which, (here, start, offset) in enumerate(
            ((c_own, 0, 7 * size + c_own.shape[0]), (mine[6], size, 7 * size))
        ):
            here_at = pl.ds(start + anc // 2, tile, stride=blocks)
            there_at = pl.ds(offset + anc // 2, tile, stride=blocks)
            value = jnp.where(anc % 2 == c, here[here_at, :], theirs[there_at, :])
            at = pl.ds(pl.multiple_of((x ^ which) * tile, tile), tile)
            pick[at, slot * tile:(slot + 1) * tile] = jnp.where(slot < live[x], value, 0.0)
    picked = pick[...]
    grown[...] = dot3(halves(picked), (f_high[...], f_low[...]), NN)
    total = slots * tile
    turned = pltpu.roll(picked, total - last, 1)
    last_high[...], last_low[...] = halves(turned[:, :last_high.shape[1]])


def product_kernel(share, tile, slots, structure, live, place, *refs):
    grown, last_high, last_low, d_high, d_low, mine, theirs = refs[:7]
    panel_out = refs[7:9]
    w_out = refs[9:13]
    ff_high, ff_low, fd_high, fd_low = refs[13:17]
    product = refs[17]
    z, x, c = place[0], place[1], place[2]
    wide = fd_high.shape[0]
    width = wide // 2
    half = d_high.shape[0] // 2
    lane_blocks = half // 128
    block = share + width
    far = pl.ds(pl.multiple_of((z ^ 3) * wide, wide), wide)
    fd_high[...] = d_high[far, :]
    fd_low[...] = d_low[far, :]
    d_at = pl.ds(pl.multiple_of((1 - x) * width, width), width)
    for first, ref in ((0, mine), (half, theirs)):
        for b in range(lane_blocks):
            lanes = slice(first + b * 128, first + (b + 1) * 128)
            top = b * block
            split(ref[top:top + share, :], ff_high, ff_low, (slice(None), lanes))
            split(ref[top + share:top + block, :], fd_high, fd_low, (d_at, lanes))
    last = (last_high[:, :share], last_low[:, :share])
    value = grown[...] + dot3(last, (ff_high[...], ff_low[...]), NN)
    value = halves(value)
    product[...] = dot3(value, (d_high[...], d_low[...]), NT)
    product[:, far] = dot3(value, (fd_high[...], fd_low[...]), NT)
    lanes = pl.ds(pl.multiple_of(c * half, half), half)
    for which in range(2):
        at = pl.ds(pl.multiple_of((x ^ which) * tile, tile), tile)
        used = False
        for slot in range(slots):
            used = used | ((slot < live[x]) & (structure[x, slot] == 2 * z + (x ^ which)))
        panel_out[which][...] = jnp.where(used, -product[at, lanes], 0.0)
    low_lane = lax.broadcasted_iota(jnp.int32, (tile, wide), 1) < width
    for step in range(4):
        columns = pl.ds(pl.multiple_of((z ^ step) * wide, wide), wide)
        first = product[:tile, columns]
        second = product[tile:, columns]
        left = jnp.where(c == 0, first, pltpu.roll(first, width, 1))
        right = jnp.where(c == 0, pltpu.roll(second, width, 1), second)
        w_out[step][...] = jnp.where(low_lane, left, right)


def scaled_kernel(share, place, *refs):
    f_high, f_low, d_high, d_low, ff_high, ff_low, fd_high, fd_low = refs[:8]
    s_high, s_low, base, all_f_high, all_f_low, all_d_high, all_d_low = refs[8:]
    z, x, c = place[0], place[1], place[2]
    wide = fd_high.shape[0]
    width = wide // 2
    f_at = pl.ds(pl.multiple_of((2 * (z ^ 3) + 1 - x) * share, share), share)
    d_at = pl.ds(pl.multiple_of((z ^ 3) * wide, wide), wide)
    for whole, early, late, at in (
        (all_f_high, f_high, ff_high, f_at),
        (all_f_low, f_low, ff_low, f_at),
        (all_d_high, d_high, fd_high, d_at),
        (all_d_low, d_low, fd_low, d_at),
    ):
        whole[...] = early[...]
        whole[at, :] = late[...]
    inverse = (all_d_high[...], all_d_low[...])
    scaled = dot3((all_f_high[...], all_f_low[...]), inverse, NT)
    s_high[...], s_low[...] = halves(scaled)
    at = pl.ds(pl.multiple_of((2 * z + c) * width, width), width)
    base[...] = dot3((all_d_high[at, :], all_d_low[at, :]), inverse, NT)


def diag_kernel(tile, slots, structure, live, place, w0, w1, w2, w3, s_high, s_low, base, *refs):
    keep, cross, w_all, pick_high, pick_low, total = refs
    z, x = place[0], place[1]
    half = keep.shape[1]
    width = keep.shape[0]
    for step, piece in enumerate((w0, w1, w2, w3)):
        w_all[z ^ step] = piece[...]
    for slot in range(slots):
        anc = structure[x, slot]
        value = w_all[anc // 2]
        value = jnp.where(anc % 2 == 0, value, pltpu.roll(value, width, 1))
        at = slice(slot * tile, (slot + 1) * tile)
        split(jnp.where(slot < live[x], value, 0.0), pick_high, pick_low, (at, slice(None)))
    picked = (pick_high[...], pick_low[...])
    total[...] = base[...] + dot3(picked, (s_high[...], s_low[...]), TN)[:width]
    keep[...] = total[:, pl.ds(pl.multiple_of(x * half, half), half)]
    cross[...] = total[:, pl.ds(pl.multiple_of((1 - x) * half, half), half)]


def lines_kernel(place, mine, other, out):
    x = place[1]
    blocks = mine.shape[1] // 128
    for member, value in ((x, mine), (1 - x, other)):
        for block in range(blocks):
            at = pl.ds(2 * block + member, mine.shape[0], stride=2 * blocks)
            out[at, :] = value[:, block * 128:(block + 1) * 128]


def diag_lines_kernel(place, keep, met, far, out):
    x, c = place[1], place[2]
    blocks = keep.shape[1] // 128
    mine = jnp.where(c == x, keep[...], met[...])
    other = jnp.where(c == x, met[...], far[...])
    for member, value in ((x, mine), (1 - x, other)):
        for block in range(blocks):
            at = pl.ds(2 * block + member, keep.shape[0], stride=2 * blocks)
            out[at, :] = value[:, block * 128:(block + 1) * 128]


def many_rows(ancestor_cov, panel_factor, diag_inverse, structure, live_counts):
    tile_rows = ancestor_cov.shape[0]
    local_blocks = ancestor_cov.shape[1]
    col_count = lax.axis_size("col")
    col_id = lax.axis_index("col")
    row_id = lax.axis_index("row")
    flat_cov = ancestor_cov.reshape(tile_rows, local_blocks * tile_rows)
    half_width = panel_factor.shape[2]
    slot_total = structure.shape[1]
    whole_inverse = lax.all_gather(diag_inverse, "row", axis=2, tiled=True)
    inverse_part = lax.dynamic_slice_in_dim(whole_inverse, col_id * half_width, half_width, 0)
    factor_term = jnp.einsum(
        "rsk,ksn->rsn", panel_factor, inverse_part, precision=lax.Precision.HIGHEST
    )
    slot_index = jnp.arange(slot_total, dtype=jnp.int32)
    slot_alive = slot_index[None, :] < live_counts[:, None]
    own_slot = slot_alive & (structure == row_id)
    in_struct = jnp.any(own_slot, axis=1)
    own_pos = jnp.sum(jnp.where(own_slot, slot_index[None, :], 0), axis=1)
    tile_offsets = jnp.arange(tile_rows, dtype=jnp.int32)
    factor_rows = lax.psum(factor_term, "col")
    arrived = lax.all_gather(factor_rows, "row", axis=0, tiled=True)
    row_count = arrived.shape[0]
    global_row = jnp.arange(row_count, dtype=jnp.int32)
    slot_of = global_row // tile_rows
    offset = global_row % tile_rows
    chooser = (slot_of[:, None] == slot_index[None, :]).astype(jnp.int32)
    product_list = []
    owned_list = []
    for member in range(2):
        anc_block = jnp.sum(chooser * structure[member][None, :], axis=1)
        is_live = slot_of < live_counts[member]
        is_match = is_live & (anc_block % col_count == col_id)
        column_index = anc_block // col_count * tile_rows + offset
        sig_cols = jnp.take(flat_cov, column_index, axis=1)
        weighted = jnp.where(is_match[:, None], arrived[:, member, :], 0.0)
        product_list.append(
            jnp.dot(
                sig_cols,
                weighted,
                precision=lax.Precision.HIGHEST,
                preferred_element_type=jnp.float32,
            )
        )
        source = own_pos[member] * tile_rows + tile_offsets
        in_range = in_struct[member] & (source >= 0) & (source < row_count)
        fetched = jnp.take(arrived[:, member, :], jnp.clip(source, 0, row_count - 1), axis=0)
        owned_list.append(jnp.where(in_range[:, None], fetched, 0.0))
    partial_sum = jnp.stack(product_list, axis=1)
    owned = jnp.stack(owned_list, axis=1)
    summed_all = lax.psum(partial_sum, "col")
    product_half = lax.dynamic_slice_in_dim(summed_all, col_id * half_width, half_width, 2)
    panel_cov = -product_half * in_struct.astype(jnp.float32)[None, :, None]
    spread_term = lax.psum_scatter(
        jnp.einsum("tsi,tsn->isn", owned, product_half, precision=lax.Precision.HIGHEST),
        "row",
        scatter_dimension=0,
        tiled=True,
    )
    inverse_half = lax.dynamic_slice_in_dim(whole_inverse, col_id * half_width, half_width, 2)
    base_term = jnp.einsum(
        "ksi,ksn->isn", diag_inverse, inverse_half, precision=lax.Precision.HIGHEST
    )
    diag_cov = base_term + spread_term
    return (panel_cov, diag_cov)


def local(ancestor_cov, panel_factor, diag_inverse, structure, live_counts):
    rows = lax.axis_size("row")
    if rows != 8:
        return many_rows(ancestor_cov, panel_factor, diag_inverse, structure, live_counts)
    tile = ancestor_cov.shape[0]
    share, _, half = panel_factor.shape
    whole, _, width = diag_inverse.shape
    slots = structure.shape[1]
    col = lax.axis_index("col")
    row = lax.axis_index("row")
    place = jnp.stack([row // 2, row % 2, col]).astype(jnp.int32)
    smem = pl.BlockSpec(memory_space=pltpu.SMEM)
    vmem = pl.BlockSpec(memory_space=pltpu.VMEM)

    def like(*shape, dtype=F32):
        return jax.ShapeDtypeStruct(shape, dtype)

    def call(kernel, name, outs, scalars, arrays, scratch=(), space=vmem, limit=VMEM_LIMIT):
        return pl.pallas_call(
            kernel,
            out_shape=outs,
            in_specs=[smem] * len(scalars) + [space] * len(arrays),
            out_specs=[vmem] * len(outs),
            scratch_shapes=list(scratch),
            compiler_params=pltpu.CompilerParams(vmem_limit_bytes=limit),
            name=name,
        )(*scalars, *arrays)

    def send_to(value, target):
        pairs = []
        for r in range(rows):
            for c in range(2):
                to = target(r // 2, r % 2, c)
                if to is not None:
                    pairs.append((r * 2 + c, (to[0] * 2 + to[1]) * 2 + to[2]))
        return lax.ppermute(value, ("row", "col"), pairs)

    def move(value, z_step, x_step, flip):
        return send_to(value, lambda z, x, c: (z ^ z_step, x ^ x_step, c ^ flip))

    factor_lines = (
        panel_factor.reshape(share, 2, half // 128, 128).transpose(0, 2, 1, 3).reshape(-1, 128)
    )
    c_own = ancestor_cov.reshape(-1, 128)
    bundle = (share + width) * half // 128
    own, send, send_near = call(
        pack_kernel,
        "pack",
        [like(bundle, 128)] * 2 + [like(bundle + c_own.shape[0], 128)],
        [],
        [
            pltpu.with_memory_space_constraint(v, pltpu.HBM)
            for v in (factor_lines, diag_inverse.transpose(1, 2, 0), c_own)
        ],
        [
            pltpu.VMEM(factor_lines.shape, F32),
            pltpu.VMEM((2, width, half), F32),
            pltpu.SemaphoreType.DMA((3,)),
        ],
        pl.BlockSpec(memory_space=pltpu.HBM),
    )
    own_far = move(own, 2, 0, 0)
    near_far = move(send, 2, 1, 0)
    own_side = move(own, 1, 0, 0)
    near_side = move(send, 1, 1, 0)
    near = move(send_near, 0, 1, 0)
    own_opposite = move(own_far, 1, 0, 0)
    near_opposite = move(near_far, 1, 0, 0)
    mine = [own, own_far, near_far, own_side, near_side, own_opposite, near]
    theirs = move(jnp.concatenate([*mine, c_own]), 0, 0, 1)
    split_f = [like(slots * tile, whole, dtype=BF16)] * 2
    split_d = [like(whole, whole, dtype=BF16)] * 2
    grown, last_high, last_low, f_high, f_low, d_high, d_low = call(
        functools.partial(early_kernel, share, tile, slots),
        "early",
        [like(2 * tile, whole)] + [like(2 * tile, 128, dtype=BF16)] * 2 + split_f + split_d,
        [structure, live_counts, place],
        [c_own, *mine, theirs],
        [pltpu.VMEM((2 * tile, slots * tile), F32)],
    )
    near_opposite, grown = lax.optimization_barrier((near_opposite, grown))
    opposite_theirs = move(near_opposite, 0, 0, 1)
    outs = call(
        functools.partial(product_kernel, share, tile, slots),
        "products",
        [like(tile, half)] * 2
        + [like(tile, 2 * width)] * 4
        + [like(share, whole, dtype=BF16)] * 2
        + [like(2 * width, whole, dtype=BF16)] * 2,
        [structure, live_counts, place],
        [grown, last_high, last_low, d_high, d_low, near_opposite, opposite_theirs],
        [pltpu.VMEM((2 * tile, whole), F32)],
    )
    panel, w, late = outs[:2], outs[2:6], outs[6:]
    w = [w[0]] + [move(w[step], step, 0, 0) for step in range(1, 4)]
    s_high, s_low, base = call(
        functools.partial(scaled_kernel, share),
        "scaled",
        split_f + [like(width, whole)],
        [place],
        [f_high, f_low, d_high, d_low, *late],
        [pltpu.VMEM(s.shape, BF16) for s in split_f + split_d],
    )
    panel_send, w[1] = lax.optimization_barrier((panel[1], w[1]))
    panel_got = move(panel_send, 0, 1, 0)
    keep, cross = call(
        functools.partial(diag_kernel, tile, slots),
        "diag_block",
        [like(width, half)] * 2,
        [structure, live_counts, place],
        [*w, s_high, s_low, base],
        [
            pltpu.VMEM((rows // 2, tile, 2 * width), F32),
            pltpu.VMEM((slots * tile, 2 * width), BF16),
            pltpu.VMEM((slots * tile, 2 * width), BF16),
            pltpu.VMEM((width, whole), F32),
        ],
    )
    met = send_to(cross, lambda z, x, c: (z, x, 1 - c) if c == x else (z, 1 - x, c))
    far = send_to(keep, lambda z, x, c: None if c == x else (z, 1 - x, 1 - c))
    lines = 2 * half // 128
    panel_got, keep = lax.optimization_barrier((panel_got, keep))
    (panel_lines,) = call(
        lines_kernel, "panel_lines", [like(tile * lines, 128)], [place], [panel[0], panel_got]
    )
    panel_lines, keep = lax.optimization_barrier((panel_lines, keep))
    (diag_lines,) = call(
        diag_lines_kernel, "diag_lines", [like(width * lines, 128)], [place], [keep, met, far]
    )

    def unfold(value, count):
        return value.reshape(count, half // 128, 2, 128).transpose(0, 2, 1, 3).reshape(count, 2, half)

    return unfold(panel_lines, tile), unfold(diag_lines, width)


def solution(mesh):
    placed = (
        P(("mp", "row"), None, "col", None),
        P(("mp", "row"), None, "col"),
        P("mp", None, "row"),
        P("mp", None),
        P("mp"),
    )
    return jax.shard_map(
        local,
        mesh=mesh,
        in_specs=placed,
        out_specs=(P(("mp", "row"), None, "col"), P(("mp", "row"), None, "col")),
        check_vma=False,
    )
```

```python
import functools

import jax
import jax.numpy as jnp
from jax import lax
from jax.experimental import pallas as pl
from jax.experimental.pallas import tpu as pltpu
from jax.sharding import PartitionSpec as P

F32 = jnp.float32
BF16 = jnp.bfloat16
NT = (((1,), (1,)), ((), ()))
NN = (((1,), (0,)), ((), ()))
TN = (((0,), (0,)), ((), ()))
VMEM_LIMIT = 20 * 1024 * 1024


def halves(value):
    high = value.astype(BF16)
    low = (value - high.astype(F32)).astype(BF16)
    return high, low


def dot3(left, right, dims):
    left_high, left_low = left
    right_high, right_low = right

    def one(a, b):
        return lax.dot_general(a, b, dims, preferred_element_type=F32)

    return one(left_high, right_low) + one(left_low, right_high) + one(left_high, right_high)


def split(value, high, low, at):
    high[at], low[at] = halves(value)


def pack_kernel(factor, inverse, own, send, lines, held, sem):
    x = lax.axis_index("row") % 2
    c = lax.axis_index("col")
    width = held.shape[1]
    blocks = held.shape[2] // 128
    block = own.shape[0] // blocks
    share = block - width
    lanes = pl.ds(pl.multiple_of(c * held.shape[2], held.shape[2]), held.shape[2])
    copies = [
        pltpu.make_async_copy(factor, lines, sem.at[0]),
        pltpu.make_async_copy(inverse.at[:, :, lanes], held, sem.at[1]),
    ]
    for copy in copies:
        copy.start()
    for copy in copies:
        copy.wait()
    for out, member in ((own, x), (send, 1 - x)):
        for b in range(blocks):
            rows = lines[pl.ds(2 * b + member, share, stride=2 * blocks), :]
            cols = held[member, :, b * 128:(b + 1) * 128]
            out[b * block:b * block + share, :] = rows
            out[b * block + share:(b + 1) * block, :] = cols


def early_kernel(share, tile, slots, structure, live, place, c_own, *refs):
    mine = refs[:7]
    theirs, near_theirs, c_sib, c_near, c_near_sib = refs[7:12]
    grown, last_high, last_low, f_high, f_low, d_high, d_low, pick = refs[12:]
    z, x, c = place[0], place[1], place[2]
    size = mine[0].shape[0]
    whole = d_high.shape[0]
    half = whole // 2
    lane_blocks = half // 128
    block = size // lane_blocks
    width = block - share
    near_x = 1 - x
    sources = (
        2 * z + x,
        2 * (z ^ 2) + x,
        2 * (z ^ 2) + near_x,
        2 * (z ^ 1) + x,
        2 * (z ^ 1) + near_x,
        2 * (z ^ 3) + x,
        2 * z + near_x,
    )
    for index, source in enumerate(sources):
        f_at = pl.ds(pl.multiple_of(source * share, share), share)
        d_at = pl.ds(pl.multiple_of(source * width, width), width)
        there = (theirs, index * size) if index < 6 else (near_theirs, 0)
        for first, (ref, start) in ((0, (mine[index], 0)), (half, there)):
            for b in range(lane_blocks):
                lanes = slice(first + b * 128, first + (b + 1) * 128)
                top = start + b * block
                split(ref[top:top + share, :], f_high, f_low, (f_at, lanes))
                split(ref[top + share:top + block, :], d_high, d_low, (d_at, lanes))
    last = (2 * (z ^ 3) + near_x) * share
    f_at = pl.ds(pl.multiple_of(last, share), share)
    f_high[f_at, :] = jnp.zeros((share, whole), BF16)
    f_low[f_at, :] = jnp.zeros((share, whole), BF16)
    d_at = pl.ds(pl.multiple_of((2 * (z ^ 3) + near_x) * width, width), width)
    d_high[d_at, :] = jnp.zeros((width, whole), BF16)
    d_low[d_at, :] = jnp.zeros((width, whole), BF16)
    blocks = c_own.shape[0] // tile
    for slot in range(slots):
        anc = structure[x, slot]
        rows = pl.ds(anc // 2, tile, stride=blocks)
        for which, (here, there) in enumerate(((c_own, c_sib), (c_near, c_near_sib))):
            value = jnp.where(anc % 2 == c, here[rows, :], there[rows, :])
            at = pl.ds(pl.multiple_of((x ^ which) * tile, tile), tile)
            pick[at, slot * tile:(slot + 1) * tile] = jnp.where(slot < live[x], value, 0.0)
    picked = pick[...]
    grown[...] = dot3(halves(picked), (f_high[...], f_low[...]), NN)
    total = slots * tile
    turned = pltpu.roll(picked, total - last, 1)
    last_high[...], last_low[...] = halves(turned[:, :last_high.shape[1]])


def product_kernel(share, tile, slots, structure, live, place, *refs):
    grown, last_high, last_low, d_high, d_low, mine, theirs = refs[:7]
    panel_out = refs[7:9]
    w_out = refs[9:13]
    ff_high, ff_low, fd_high, fd_low = refs[13:17]
    product = refs[17]
    z, x, c = place[0], place[1], place[2]
    wide = fd_high.shape[0]
    width = wide // 2
    half = d_high.shape[0] // 2
    lane_blocks = half // 128
    block = share + width
    far = pl.ds(pl.multiple_of((z ^ 3) * wide, wide), wide)
    fd_high[...] = d_high[far, :]
    fd_low[...] = d_low[far, :]
    d_at = pl.ds(pl.multiple_of((1 - x) * width, width), width)
    for first, ref in ((0, mine), (half, theirs)):
        for b in range(lane_blocks):
            lanes = slice(first + b * 128, first + (b + 1) * 128)
            top = b * block
            split(ref[top:top + share, :], ff_high, ff_low, (slice(None), lanes))
            split(ref[top + share:top + block, :], fd_high, fd_low, (d_at, lanes))
    last = (last_high[:, :share], last_low[:, :share])
    value = grown[...] + dot3(last, (ff_high[...], ff_low[...]), NN)
    value = halves(value)
    product[...] = dot3(value, (d_high[...], d_low[...]), NT)
    product[:, far] = dot3(value, (fd_high[...], fd_low[...]), NT)
    lanes = pl.ds(pl.multiple_of(c * half, half), half)
    for which in range(2):
        at = pl.ds(pl.multiple_of((x ^ which) * tile, tile), tile)
        used = False
        for slot in range(slots):
            used = used | ((slot < live[x]) & (structure[x, slot] == 2 * z + (x ^ which)))
        panel_out[which][...] = jnp.where(used, -product[at, lanes], 0.0)
    low_lane = lax.broadcasted_iota(jnp.int32, (tile, wide), 1) < width
    for step in range(4):
        columns = pl.ds(pl.multiple_of((z ^ step) * wide, wide), wide)
        first = product[:tile, columns]
        second = product[tile:, columns]
        left = jnp.where(c == 0, first, pltpu.roll(first, width, 1))
        right = jnp.where(c == 0, pltpu.roll(second, width, 1), second)
        w_out[step][...] = jnp.where(low_lane, left, right)


def scaled_kernel(share, place, *refs):
    f_high, f_low, d_high, d_low, ff_high, ff_low, fd_high, fd_low = refs[:8]
    s_high, s_low, base, all_f_high, all_f_low, all_d_high, all_d_low = refs[8:]
    z, x, c = place[0], place[1], place[2]
    wide = fd_high.shape[0]
    width = wide // 2
    f_at = pl.ds(pl.multiple_of((2 * (z ^ 3) + 1 - x) * share, share), share)
    d_at = pl.ds(pl.multiple_of((z ^ 3) * wide, wide), wide)
    for whole, early, late, at in (
        (all_f_high, f_high, ff_high, f_at),
        (all_f_low, f_low, ff_low, f_at),
        (all_d_high, d_high, fd_high, d_at),
        (all_d_low, d_low, fd_low, d_at),
    ):
        whole[...] = early[...]
        whole[at, :] = late[...]
    inverse = (all_d_high[...], all_d_low[...])
    scaled = dot3((all_f_high[...], all_f_low[...]), inverse, NT)
    s_high[...], s_low[...] = halves(scaled)
    at = pl.ds(pl.multiple_of((2 * z + c) * width, width), width)
    base[...] = dot3((all_d_high[at, :], all_d_low[at, :]), inverse, NT)


def diag_kernel(tile, slots, structure, live, place, w0, w1, w2, w3, s_high, s_low, base, *refs):
    keep, cross, w_all, pick_high, pick_low, total = refs
    z, x = place[0], place[1]
    half = keep.shape[1]
    width = keep.shape[0]
    for step, piece in enumerate((w0, w1, w2, w3)):
        w_all[z ^ step] = piece[...]
    for slot in range(slots):
        anc = structure[x, slot]
        value = w_all[anc // 2]
        value = jnp.where(anc % 2 == 0, value, pltpu.roll(value, width, 1))
        at = slice(slot * tile, (slot + 1) * tile)
        split(jnp.where(slot < live[x], value, 0.0), pick_high, pick_low, (at, slice(None)))
    picked = (pick_high[...], pick_low[...])
    total[...] = base[...] + dot3(picked, (s_high[...], s_low[...]), TN)[:width]
    keep[...] = total[:, pl.ds(pl.multiple_of(x * half, half), half)]
    cross[...] = total[:, pl.ds(pl.multiple_of((1 - x) * half, half), half)]


def lines_kernel(place, mine, other, out):
    x = place[1]
    blocks = mine.shape[1] // 128
    for member, value in ((x, mine), (1 - x, other)):
        for block in range(blocks):
            at = pl.ds(2 * block + member, mine.shape[0], stride=2 * blocks)
            out[at, :] = value[:, block * 128:(block + 1) * 128]


def diag_lines_kernel(place, keep, met, far, out):
    x, c = place[1], place[2]
    blocks = keep.shape[1] // 128
    mine = jnp.where(c == x, keep[...], met[...])
    other = jnp.where(c == x, met[...], far[...])
    for member, value in ((x, mine), (1 - x, other)):
        for block in range(blocks):
            at = pl.ds(2 * block + member, keep.shape[0], stride=2 * blocks)
            out[at, :] = value[:, block * 128:(block + 1) * 128]


def many_rows(ancestor_cov, panel_factor, diag_inverse, structure, live_counts):
    tile_rows = ancestor_cov.shape[0]
    local_blocks = ancestor_cov.shape[1]
    col_count = lax.axis_size("col")
    col_id = lax.axis_index("col")
    row_id = lax.axis_index("row")
    flat_cov = ancestor_cov.reshape(tile_rows, local_blocks * tile_rows)
    half_width = panel_factor.shape[2]
    slot_total = structure.shape[1]
    whole_inverse = lax.all_gather(diag_inverse, "row", axis=2, tiled=True)
    inverse_part = lax.dynamic_slice_in_dim(whole_inverse, col_id * half_width, half_width, 0)
    factor_term = jnp.einsum(
        "rsk,ksn->rsn", panel_factor, inverse_part, precision=lax.Precision.HIGHEST
    )
    slot_index = jnp.arange(slot_total, dtype=jnp.int32)
    slot_alive = slot_index[None, :] < live_counts[:, None]
    own_slot = slot_alive & (structure == row_id)
    in_struct = jnp.any(own_slot, axis=1)
    own_pos = jnp.sum(jnp.where(own_slot, slot_index[None, :], 0), axis=1)
    tile_offsets = jnp.arange(tile_rows, dtype=jnp.int32)
    factor_rows = lax.psum(factor_term, "col")
    arrived = lax.all_gather(factor_rows, "row", axis=0, tiled=True)
    row_count = arrived.shape[0]
    global_row = jnp.arange(row_count, dtype=jnp.int32)
    slot_of = global_row // tile_rows
    offset = global_row % tile_rows
    chooser = (slot_of[:, None] == slot_index[None, :]).astype(jnp.int32)
    product_list = []
    owned_list = []
    for member in range(2):
        anc_block = jnp.sum(chooser * structure[member][None, :], axis=1)
        is_live = slot_of < live_counts[member]
        is_match = is_live & (anc_block % col_count == col_id)
        column_index = anc_block // col_count * tile_rows + offset
        sig_cols = jnp.take(flat_cov, column_index, axis=1)
        weighted = jnp.where(is_match[:, None], arrived[:, member, :], 0.0)
        product_list.append(
            jnp.dot(
                sig_cols,
                weighted,
                precision=lax.Precision.HIGHEST,
                preferred_element_type=jnp.float32,
            )
        )
        source = own_pos[member] * tile_rows + tile_offsets
        in_range = in_struct[member] & (source >= 0) & (source < row_count)
        fetched = jnp.take(arrived[:, member, :], jnp.clip(source, 0, row_count - 1), axis=0)
        owned_list.append(jnp.where(in_range[:, None], fetched, 0.0))
    partial_sum = jnp.stack(product_list, axis=1)
    owned = jnp.stack(owned_list, axis=1)
    summed_all = lax.psum(partial_sum, "col")
    product_half = lax.dynamic_slice_in_dim(summed_all, col_id * half_width, half_width, 2)
    panel_cov = -product_half * in_struct.astype(jnp.float32)[None, :, None]
    spread_term = lax.psum_scatter(
        jnp.einsum("tsi,tsn->isn", owned, product_half, precision=lax.Precision.HIGHEST),
        "row",
        scatter_dimension=0,
        tiled=True,
    )
    inverse_half = lax.dynamic_slice_in_dim(whole_inverse, col_id * half_width, half_width, 2)
    base_term = jnp.einsum(
        "ksi,ksn->isn", diag_inverse, inverse_half, precision=lax.Precision.HIGHEST
    )
    diag_cov = base_term + spread_term
    return (panel_cov, diag_cov)


def local(ancestor_cov, panel_factor, diag_inverse, structure, live_counts):
    rows = lax.axis_size("row")
    if rows != 8:
        return many_rows(ancestor_cov, panel_factor, diag_inverse, structure, live_counts)
    tile = ancestor_cov.shape[0]
    share, _, half = panel_factor.shape
    whole, _, width = diag_inverse.shape
    slots = structure.shape[1]
    col = lax.axis_index("col")
    row = lax.axis_index("row")
    place = jnp.stack([row // 2, row % 2, col]).astype(jnp.int32)
    smem = pl.BlockSpec(memory_space=pltpu.SMEM)
    vmem = pl.BlockSpec(memory_space=pltpu.VMEM)

    def like(*shape, dtype=F32):
        return jax.ShapeDtypeStruct(shape, dtype)

    def call(kernel, name, outs, scalars, arrays, scratch=(), space=vmem, limit=VMEM_LIMIT):
        return pl.pallas_call(
            kernel,
            out_shape=outs,
            in_specs=[smem] * len(scalars) + [space] * len(arrays),
            out_specs=[vmem] * len(outs),
            scratch_shapes=list(scratch),
            compiler_params=pltpu.CompilerParams(vmem_limit_bytes=limit),
            name=name,
        )(*scalars, *arrays)

    def send_to(value, target):
        pairs = []
        for r in range(rows):
            for c in range(2):
                to = target(r // 2, r % 2, c)
                if to is not None:
                    pairs.append((r * 2 + c, (to[0] * 2 + to[1]) * 2 + to[2]))
        return lax.ppermute(value, ("row", "col"), pairs)

    def move(value, z_step, x_step, flip):
        return send_to(value, lambda z, x, c: (z ^ z_step, x ^ x_step, c ^ flip))

    factor_lines = (
        panel_factor.reshape(share, 2, half // 128, 128).transpose(0, 2, 1, 3).reshape(-1, 128)
    )
    c_own = ancestor_cov.reshape(-1, 128)
    bundle = (share + width) * half // 128
    own, send = call(
        pack_kernel,
        "pack",
        [like(bundle, 128)] * 2,
        [],
        [
            pltpu.with_memory_space_constraint(v, pltpu.HBM)
            for v in (factor_lines, diag_inverse.transpose(1, 2, 0))
        ],
        [
            pltpu.VMEM(factor_lines.shape, F32),
            pltpu.VMEM((2, width, half), F32),
            pltpu.SemaphoreType.DMA((2,)),
        ],
        pl.BlockSpec(memory_space=pltpu.HBM),
    )
    own_far = move(own, 2, 0, 0)
    near_far = move(send, 2, 1, 0)
    own_side = move(own, 1, 0, 0)
    near_side = move(send, 1, 1, 0)
    near = move(send, 0, 1, 0)
    c_near = move(c_own, 0, 1, 0)
    own_far, near = lax.optimization_barrier((own_far, near))
    own_opposite = move(own_far, 1, 0, 0)
    near_far, c_near = lax.optimization_barrier((near_far, c_near))
    near_opposite = move(near_far, 1, 0, 0)
    mine = [own, own_far, near_far, own_side, near_side, own_opposite]
    theirs = [
        move(jnp.concatenate(mine), 0, 0, 1),
        move(near, 0, 0, 1),
        move(c_own, 0, 0, 1),
        move(c_near, 0, 0, 1),
    ]
    near_opposite, c_first = lax.optimization_barrier((near_opposite, c_own))
    opposite_theirs = move(near_opposite, 0, 0, 1)
    split_f = [like(slots * tile, whole, dtype=BF16)] * 2
    split_d = [like(whole, whole, dtype=BF16)] * 2
    grown, last_high, last_low, f_high, f_low, d_high, d_low = call(
        functools.partial(early_kernel, share, tile, slots),
        "early",
        [like(2 * tile, whole)] + [like(2 * tile, 128, dtype=BF16)] * 2 + split_f + split_d,
        [structure, live_counts, place],
        [c_first, *mine, near, *theirs[:3], c_near, theirs[3]],
        [pltpu.VMEM((2 * tile, slots * tile), F32)],
    )
    outs = call(
        functools.partial(product_kernel, share, tile, slots),
        "products",
        [like(tile, half)] * 2
        + [like(tile, 2 * width)] * 4
        + [like(share, whole, dtype=BF16)] * 2
        + [like(2 * width, whole, dtype=BF16)] * 2,
        [structure, live_counts, place],
        [grown, last_high, last_low, d_high, d_low, near_opposite, opposite_theirs],
        [pltpu.VMEM((2 * tile, whole), F32)],
    )
    panel, w, late = outs[:2], outs[2:6], outs[6:]
    w = [w[0]] + [move(w[step], step, 0, 0) for step in range(1, 4)]
    s_high, s_low, base = call(
        functools.partial(scaled_kernel, share),
        "scaled",
        split_f + [like(width, whole)],
        [place],
        [f_high, f_low, d_high, d_low, *late],
        [pltpu.VMEM(s.shape, BF16) for s in split_f + split_d],
    )
    panel_send, w[1] = lax.optimization_barrier((panel[1], w[1]))
    panel_got = move(panel_send, 0, 1, 0)
    keep, cross = call(
        functools.partial(diag_kernel, tile, slots),
        "diag_block",
        [like(width, half)] * 2,
        [structure, live_counts, place],
        [*w, s_high, s_low, base],
        [
            pltpu.VMEM((rows // 2, tile, 2 * width), F32),
            pltpu.VMEM((slots * tile, 2 * width), BF16),
            pltpu.VMEM((slots * tile, 2 * width), BF16),
            pltpu.VMEM((width, whole), F32),
        ],
    )
    met = send_to(cross, lambda z, x, c: (z, x, 1 - c) if c == x else (z, 1 - x, c))
    far = send_to(keep, lambda z, x, c: None if c == x else (z, 1 - x, 1 - c))
    lines = 2 * half // 128
    panel_got, keep = lax.optimization_barrier((panel_got, keep))
    (panel_lines,) = call(
        lines_kernel, "panel_lines", [like(tile * lines, 128)], [place], [panel[0], panel_got]
    )
    panel_lines, keep = lax.optimization_barrier((panel_lines, keep))
    (diag_lines,) = call(
        diag_lines_kernel, "diag_lines", [like(width * lines, 128)], [place], [keep, met, far]
    )

    def unfold(value, count):
        return value.reshape(count, half // 128, 2, 128).transpose(0, 2, 1, 3).reshape(count, 2, half)

    return unfold(panel_lines, tile), unfold(diag_lines, width)


def solution(mesh):
    placed = (
        P(("mp", "row"), None, "col", None),
        P(("mp", "row"), None, "col"),
        P("mp", None, "row"),
        P("mp", None),
        P("mp"),
    )
    return jax.shard_map(
        local,
        mesh=mesh,
        in_specs=placed,
        out_specs=(P(("mp", "row"), None, "col"), P(("mp", "row"), None, "col")),
        check_vma=False,
    )
```

```python
import functools

import jax
import jax.numpy as jnp
from jax import lax
from jax.experimental import pallas as pl
from jax.experimental.pallas import tpu as pltpu
from jax.sharding import PartitionSpec as P

F32 = jnp.float32
BF16 = jnp.bfloat16
NT = (((1,), (1,)), ((), ()))
NN = (((1,), (0,)), ((), ()))
TN = (((0,), (0,)), ((), ()))
VMEM_LIMIT = 20 * 1024 * 1024
THERE = ((2, 0), (0, 0), (0, 1), (1, 0), (1, 1), (2, 1))


def halves(value):
    high = value.astype(BF16)
    low = (value - high.astype(F32)).astype(BF16)
    return high, low


def dot3(left, right, dims):
    left_high, left_low = left
    right_high, right_low = right

    def one(a, b):
        return lax.dot_general(a, b, dims, preferred_element_type=F32)

    return one(left_high, right_low) + one(left_low, right_high) + one(left_high, right_high)


def split(value, high, low, at):
    high[at], low[at] = halves(value)


def pack_kernel(factor, inverse, cov, own, send, near, lines, held, sem):
    x = lax.axis_index("row") % 2
    c = lax.axis_index("col")
    width = held.shape[1]
    blocks = held.shape[2] // 128
    block = own.shape[0] // blocks
    share = block - width
    lanes = pl.ds(pl.multiple_of(c * held.shape[2], held.shape[2]), held.shape[2])
    copies = [
        pltpu.make_async_copy(factor, lines, sem.at[0]),
        pltpu.make_async_copy(inverse.at[:, :, lanes], held, sem.at[1]),
        pltpu.make_async_copy(cov, near.at[pl.ds(own.shape[0], cov.shape[0]), :], sem.at[2]),
    ]
    for copy in copies:
        copy.start()
    copies[0].wait()
    copies[1].wait()
    for outs, member in (((own,), x), ((send, near), 1 - x)):
        for b in range(blocks):
            rows = lines[pl.ds(2 * b + member, share, stride=2 * blocks), :]
            cols = held[member, :, b * 128:(b + 1) * 128]
            for out in outs:
                out[b * block:b * block + share, :] = rows
                out[b * block + share:(b + 1) * block, :] = cols
    copies[2].wait()


def early_kernel(share, tile, slots, structure, live, place, c_own, *refs):
    mine = refs[:7]
    theirs = refs[7:10]
    near_theirs, c_sib = refs[10:12]
    grown, last_high, last_low, f_high, f_low, d_high, d_low, pick = refs[12:]
    z, x, c = place[0], place[1], place[2]
    size = mine[0].shape[0]
    whole = d_high.shape[0]
    half = whole // 2
    lane_blocks = half // 128
    block = size // lane_blocks
    width = block - share
    near_x = 1 - x
    sources = (
        2 * z + x,
        2 * (z ^ 2) + x,
        2 * (z ^ 2) + near_x,
        2 * (z ^ 1) + x,
        2 * (z ^ 1) + near_x,
        2 * (z ^ 3) + x,
        2 * z + near_x,
    )
    for index, source in enumerate(sources):
        f_at = pl.ds(pl.multiple_of(source * share, share), share)
        d_at = pl.ds(pl.multiple_of(source * width, width), width)
        there = (near_theirs, 0)
        if index < 6:
            message, start = THERE[index]
            there = (theirs[message], start * size)
        for first, (ref, start) in ((0, (mine[index], 0)), (half, there)):
            for b in range(lane_blocks):
                lanes = slice(first + b * 128, first + (b + 1) * 128)
                top = start + b * block
                split(ref[top:top + share, :], f_high, f_low, (f_at, lanes))
                split(ref[top + share:top + block, :], d_high, d_low, (d_at, lanes))
    last = (2 * (z ^ 3) + near_x) * share
    f_at = pl.ds(pl.multiple_of(last, share), share)
    f_high[f_at, :] = jnp.zeros((share, whole), BF16)
    f_low[f_at, :] = jnp.zeros((share, whole), BF16)
    d_at = pl.ds(pl.multiple_of((2 * (z ^ 3) + near_x) * width, width), width)
    d_high[d_at, :] = jnp.zeros((width, whole), BF16)
    d_low[d_at, :] = jnp.zeros((width, whole), BF16)
    blocks = c_own.shape[0] // tile
    for slot in range(slots):
        anc = structure[x, slot]
        for which, (here, there, start) in enumerate(
            ((c_own, c_sib, 0), (mine[6], near_theirs, size))
        ):
            rows = pl.ds(start + anc // 2, tile, stride=blocks)
            value = jnp.where(anc % 2 == c, here[rows, :], there[rows, :])
            at = pl.ds(pl.multiple_of((x ^ which) * tile, tile), tile)
            pick[at, slot * tile:(slot + 1) * tile] = jnp.where(slot < live[x], value, 0.0)
    picked = pick[...]
    grown[...] = dot3(halves(picked), (f_high[...], f_low[...]), NN)
    total = slots * tile
    turned = pltpu.roll(picked, total - last, 1)
    last_high[...], last_low[...] = halves(turned[:, :last_high.shape[1]])


def product_kernel(share, tile, slots, structure, live, place, *refs):
    grown, last_high, last_low, d_high, d_low, mine, theirs = refs[:7]
    panel_out = refs[7:9]
    w_out = refs[9:13]
    ff_high, ff_low, fd_high, fd_low = refs[13:17]
    product = refs[17]
    z, x, c = place[0], place[1], place[2]
    wide = fd_high.shape[0]
    width = wide // 2
    half = d_high.shape[0] // 2
    lane_blocks = half // 128
    block = share + width
    far = pl.ds(pl.multiple_of((z ^ 3) * wide, wide), wide)
    fd_high[...] = d_high[far, :]
    fd_low[...] = d_low[far, :]
    d_at = pl.ds(pl.multiple_of((1 - x) * width, width), width)
    for first, ref in ((0, mine), (half, theirs)):
        for b in range(lane_blocks):
            lanes = slice(first + b * 128, first + (b + 1) * 128)
            top = b * block
            split(ref[top:top + share, :], ff_high, ff_low, (slice(None), lanes))
            split(ref[top + share:top + block, :], fd_high, fd_low, (d_at, lanes))
    last = (last_high[:, :share], last_low[:, :share])
    value = grown[...] + dot3(last, (ff_high[...], ff_low[...]), NN)
    value = halves(value)
    product[...] = dot3(value, (d_high[...], d_low[...]), NT)
    product[:, far] = dot3(value, (fd_high[...], fd_low[...]), NT)
    lanes = pl.ds(pl.multiple_of(c * half, half), half)
    for which in range(2):
        at = pl.ds(pl.multiple_of((x ^ which) * tile, tile), tile)
        used = False
        for slot in range(slots):
            used = used | ((slot < live[x]) & (structure[x, slot] == 2 * z + (x ^ which)))
        panel_out[which][...] = jnp.where(used, -product[at, lanes], 0.0)
    low_lane = lax.broadcasted_iota(jnp.int32, (tile, wide), 1) < width
    for step in range(4):
        columns = pl.ds(pl.multiple_of((z ^ step) * wide, wide), wide)
        first = product[:tile, columns]
        second = product[tile:, columns]
        left = jnp.where(c == 0, first, pltpu.roll(first, width, 1))
        right = jnp.where(c == 0, pltpu.roll(second, width, 1), second)
        w_out[step][...] = jnp.where(low_lane, left, right)


def scaled_kernel(share, place, *refs):
    f_high, f_low, d_high, d_low, ff_high, ff_low, fd_high, fd_low = refs[:8]
    s_high, s_low, base, all_f_high, all_f_low, all_d_high, all_d_low = refs[8:]
    z, x, c = place[0], place[1], place[2]
    wide = fd_high.shape[0]
    width = wide // 2
    f_at = pl.ds(pl.multiple_of((2 * (z ^ 3) + 1 - x) * share, share), share)
    d_at = pl.ds(pl.multiple_of((z ^ 3) * wide, wide), wide)
    for whole, early, late, at in (
        (all_f_high, f_high, ff_high, f_at),
        (all_f_low, f_low, ff_low, f_at),
        (all_d_high, d_high, fd_high, d_at),
        (all_d_low, d_low, fd_low, d_at),
    ):
        whole[...] = early[...]
        whole[at, :] = late[...]
    inverse = (all_d_high[...], all_d_low[...])
    scaled = dot3((all_f_high[...], all_f_low[...]), inverse, NT)
    s_high[...], s_low[...] = halves(scaled)
    at = pl.ds(pl.multiple_of((2 * z + c) * width, width), width)
    base[...] = dot3((all_d_high[at, :], all_d_low[at, :]), inverse, NT)


def diag_kernel(tile, slots, structure, live, place, w0, w1, w2, w3, s_high, s_low, base, *refs):
    keep, cross, w_all, pick_high, pick_low, total = refs
    z, x = place[0], place[1]
    half = keep.shape[1]
    width = keep.shape[0]
    for step, piece in enumerate((w0, w1, w2, w3)):
        w_all[z ^ step] = piece[...]
    for slot in range(slots):
        anc = structure[x, slot]
        value = w_all[anc // 2]
        value = jnp.where(anc % 2 == 0, value, pltpu.roll(value, width, 1))
        at = slice(slot * tile, (slot + 1) * tile)
        split(jnp.where(slot < live[x], value, 0.0), pick_high, pick_low, (at, slice(None)))
    picked = (pick_high[...], pick_low[...])
    total[...] = base[...] + dot3(picked, (s_high[...], s_low[...]), TN)[:width]
    keep[...] = total[:, pl.ds(pl.multiple_of(x * half, half), half)]
    cross[...] = total[:, pl.ds(pl.multiple_of((1 - x) * half, half), half)]


def lines_kernel(place, mine, other, out):
    x = place[1]
    blocks = mine.shape[1] // 128
    for member, value in ((x, mine), (1 - x, other)):
        for block in range(blocks):
            at = pl.ds(2 * block + member, mine.shape[0], stride=2 * blocks)
            out[at, :] = value[:, block * 128:(block + 1) * 128]


def diag_lines_kernel(place, keep, met, far, out):
    x, c = place[1], place[2]
    blocks = keep.shape[1] // 128
    mine = jnp.where(c == x, keep[...], met[...])
    other = jnp.where(c == x, met[...], far[...])
    for member, value in ((x, mine), (1 - x, other)):
        for block in range(blocks):
            at = pl.ds(2 * block + member, keep.shape[0], stride=2 * blocks)
            out[at, :] = value[:, block * 128:(block + 1) * 128]


def many_rows(ancestor_cov, panel_factor, diag_inverse, structure, live_counts):
    tile_rows = ancestor_cov.shape[0]
    local_blocks = ancestor_cov.shape[1]
    col_count = lax.axis_size("col")
    col_id = lax.axis_index("col")
    row_id = lax.axis_index("row")
    flat_cov = ancestor_cov.reshape(tile_rows, local_blocks * tile_rows)
    half_width = panel_factor.shape[2]
    slot_total = structure.shape[1]
    whole_inverse = lax.all_gather(diag_inverse, "row", axis=2, tiled=True)
    inverse_part = lax.dynamic_slice_in_dim(whole_inverse, col_id * half_width, half_width, 0)
    factor_term = jnp.einsum(
        "rsk,ksn->rsn", panel_factor, inverse_part, precision=lax.Precision.HIGHEST
    )
    slot_index = jnp.arange(slot_total, dtype=jnp.int32)
    slot_alive = slot_index[None, :] < live_counts[:, None]
    own_slot = slot_alive & (structure == row_id)
    in_struct = jnp.any(own_slot, axis=1)
    own_pos = jnp.sum(jnp.where(own_slot, slot_index[None, :], 0), axis=1)
    tile_offsets = jnp.arange(tile_rows, dtype=jnp.int32)
    factor_rows = lax.psum(factor_term, "col")
    arrived = lax.all_gather(factor_rows, "row", axis=0, tiled=True)
    row_count = arrived.shape[0]
    global_row = jnp.arange(row_count, dtype=jnp.int32)
    slot_of = global_row // tile_rows
    offset = global_row % tile_rows
    chooser = (slot_of[:, None] == slot_index[None, :]).astype(jnp.int32)
    product_list = []
    owned_list = []
    for member in range(2):
        anc_block = jnp.sum(chooser * structure[member][None, :], axis=1)
        is_live = slot_of < live_counts[member]
        is_match = is_live & (anc_block % col_count == col_id)
        column_index = anc_block // col_count * tile_rows + offset
        sig_cols = jnp.take(flat_cov, column_index, axis=1)
        weighted = jnp.where(is_match[:, None], arrived[:, member, :], 0.0)
        product_list.append(
            jnp.dot(
                sig_cols,
                weighted,
                precision=lax.Precision.HIGHEST,
                preferred_element_type=jnp.float32,
            )
        )
        source = own_pos[member] * tile_rows + tile_offsets
        in_range = in_struct[member] & (source >= 0) & (source < row_count)
        fetched = jnp.take(arrived[:, member, :], jnp.clip(source, 0, row_count - 1), axis=0)
        owned_list.append(jnp.where(in_range[:, None], fetched, 0.0))
    partial_sum = jnp.stack(product_list, axis=1)
    owned = jnp.stack(owned_list, axis=1)
    summed_all = lax.psum(partial_sum, "col")
    product_half = lax.dynamic_slice_in_dim(summed_all, col_id * half_width, half_width, 2)
    panel_cov = -product_half * in_struct.astype(jnp.float32)[None, :, None]
    spread_term = lax.psum_scatter(
        jnp.einsum("tsi,tsn->isn", owned, product_half, precision=lax.Precision.HIGHEST),
        "row",
        scatter_dimension=0,
        tiled=True,
    )
    inverse_half = lax.dynamic_slice_in_dim(whole_inverse, col_id * half_width, half_width, 2)
    base_term = jnp.einsum(
        "ksi,ksn->isn", diag_inverse, inverse_half, precision=lax.Precision.HIGHEST
    )
    diag_cov = base_term + spread_term
    return (panel_cov, diag_cov)


def local(ancestor_cov, panel_factor, diag_inverse, structure, live_counts):
    rows = lax.axis_size("row")
    if rows != 8:
        return many_rows(ancestor_cov, panel_factor, diag_inverse, structure, live_counts)
    tile = ancestor_cov.shape[0]
    share, _, half = panel_factor.shape
    whole, _, width = diag_inverse.shape
    slots = structure.shape[1]
    col = lax.axis_index("col")
    row = lax.axis_index("row")
    place = jnp.stack([row // 2, row % 2, col]).astype(jnp.int32)
    smem = pl.BlockSpec(memory_space=pltpu.SMEM)
    vmem = pl.BlockSpec(memory_space=pltpu.VMEM)

    def like(*shape, dtype=F32):
        return jax.ShapeDtypeStruct(shape, dtype)

    def call(kernel, name, outs, scalars, arrays, scratch=(), space=vmem, limit=VMEM_LIMIT):
        return pl.pallas_call(
            kernel,
            out_shape=outs,
            in_specs=[smem] * len(scalars) + [space] * len(arrays),
            out_specs=[vmem] * len(outs),
            scratch_shapes=list(scratch),
            compiler_params=pltpu.CompilerParams(vmem_limit_bytes=limit),
            name=name,
        )(*scalars, *arrays)

    def send_to(value, target):
        pairs = []
        for r in range(rows):
            for c in range(2):
                to = target(r // 2, r % 2, c)
                if to is not None:
                    pairs.append((r * 2 + c, (to[0] * 2 + to[1]) * 2 + to[2]))
        return lax.ppermute(value, ("row", "col"), pairs)

    def move(value, z_step, x_step, flip):
        return send_to(value, lambda z, x, c: (z ^ z_step, x ^ x_step, c ^ flip))

    factor_lines = (
        panel_factor.reshape(share, 2, half // 128, 128).transpose(0, 2, 1, 3).reshape(-1, 128)
    )
    c_own = ancestor_cov.reshape(-1, 128)
    bundle = (share + width) * half // 128
    own, send, send_near = call(
        pack_kernel,
        "pack",
        [like(bundle, 128)] * 2 + [like(bundle + c_own.shape[0], 128)],
        [],
        [
            pltpu.with_memory_space_constraint(v, pltpu.HBM)
            for v in (factor_lines, diag_inverse.transpose(1, 2, 0), c_own)
        ],
        [
            pltpu.VMEM(factor_lines.shape, F32),
            pltpu.VMEM((2, width, half), F32),
            pltpu.SemaphoreType.DMA((3,)),
        ],
        pl.BlockSpec(memory_space=pltpu.HBM),
    )
    own_far = move(own, 2, 0, 0)
    near_far = move(send, 2, 1, 0)
    own_side = move(own, 1, 0, 0)
    near_side = move(send, 1, 1, 0)
    near = move(send_near, 0, 1, 0)
    own_opposite = move(own_far, 1, 0, 0)
    near_opposite = move(near_far, 1, 0, 0)
    mine = [own, own_far, near_far, own_side, near_side, own_opposite]
    theirs = [
        move(jnp.concatenate([own_far, near_far]), 0, 0, 1),
        move(jnp.concatenate([own_side, near_side]), 0, 0, 1),
        move(jnp.concatenate([own, own_opposite]), 0, 0, 1),
        move(near, 0, 0, 1),
        move(c_own, 0, 0, 1),
    ]
    near_opposite, c_first = lax.optimization_barrier((near_opposite, c_own))
    opposite_theirs = move(near_opposite, 0, 0, 1)
    split_f = [like(slots * tile, whole, dtype=BF16)] * 2
    split_d = [like(whole, whole, dtype=BF16)] * 2
    grown, last_high, last_low, f_high, f_low, d_high, d_low = call(
        functools.partial(early_kernel, share, tile, slots),
        "early",
        [like(2 * tile, whole)] + [like(2 * tile, 128, dtype=BF16)] * 2 + split_f + split_d,
        [structure, live_counts, place],
        [c_first, *mine, near, *theirs],
        [pltpu.VMEM((2 * tile, slots * tile), F32)],
    )
    outs = call(
        functools.partial(product_kernel, share, tile, slots),
        "products",
        [like(tile, half)] * 2
        + [like(tile, 2 * width)] * 4
        + [like(share, whole, dtype=BF16)] * 2
        + [like(2 * width, whole, dtype=BF16)] * 2,
        [structure, live_counts, place],
        [grown, last_high, last_low, d_high, d_low, near_opposite, opposite_theirs],
        [pltpu.VMEM((2 * tile, whole), F32)],
    )
    panel, w, late = outs[:2], outs[2:6], outs[6:]
    w = [w[0]] + [move(w[step], step, 0, 0) for step in range(1, 4)]
    s_high, s_low, base = call(
        functools.partial(scaled_kernel, share),
        "scaled",
        split_f + [like(width, whole)],
        [place],
        [f_high, f_low, d_high, d_low, *late],
        [pltpu.VMEM(s.shape, BF16) for s in split_f + split_d],
    )
    panel_send, w[1] = lax.optimization_barrier((panel[1], w[1]))
    panel_got = move(panel_send, 0, 1, 0)
    keep, cross = call(
        functools.partial(diag_kernel, tile, slots),
        "diag_block",
        [like(width, half)] * 2,
        [structure, live_counts, place],
        [*w, s_high, s_low, base],
        [
            pltpu.VMEM((rows // 2, tile, 2 * width), F32),
            pltpu.VMEM((slots * tile, 2 * width), BF16),
            pltpu.VMEM((slots * tile, 2 * width), BF16),
            pltpu.VMEM((width, whole), F32),
        ],
    )
    met = send_to(cross, lambda z, x, c: (z, x, 1 - c) if c == x else (z, 1 - x, c))
    far = send_to(keep, lambda z, x, c: None if c == x else (z, 1 - x, 1 - c))
    lines = 2 * half // 128
    panel_got, keep = lax.optimization_barrier((panel_got, keep))
    (panel_lines,) = call(
        lines_kernel, "panel_lines", [like(tile * lines, 128)], [place], [panel[0], panel_got]
    )
    panel_lines, keep = lax.optimization_barrier((panel_lines, keep))
    (diag_lines,) = call(
        diag_lines_kernel, "diag_lines", [like(width * lines, 128)], [place], [keep, met, far]
    )

    def unfold(value, count):
        return value.reshape(count, half // 128, 2, 128).transpose(0, 2, 1, 3).reshape(count, 2, half)

    return unfold(panel_lines, tile), unfold(diag_lines, width)


def solution(mesh):
    placed = (
        P(("mp", "row"), None, "col", None),
        P(("mp", "row"), None, "col"),
        P("mp", None, "row"),
        P("mp", None),
        P("mp"),
    )
    return jax.shard_map(
        local,
        mesh=mesh,
        in_specs=placed,
        out_specs=(P(("mp", "row"), None, "col"), P(("mp", "row"), None, "col")),
        check_vma=False,
    )
```

```python
import functools

import jax
import jax.numpy as jnp
from jax import lax
from jax.experimental import pallas as pl
from jax.experimental.pallas import tpu as pltpu
from jax.sharding import PartitionSpec as P

F32 = jnp.float32
BF16 = jnp.bfloat16
NT = (((1,), (1,)), ((), ()))
NN = (((1,), (0,)), ((), ()))
TN = (((0,), (0,)), ((), ()))
VMEM_LIMIT = 20 * 1024 * 1024
THERE = ((2, 0), (0, 0), (0, 1), (1, 0), (1, 1), (3, 0), (4, 0))


def halves(value):
    high = value.astype(BF16)
    low = (value - high.astype(F32)).astype(BF16)
    return high, low


def dot3(left, right, dims):
    left_high, left_low = left
    right_high, right_low = right

    def one(a, b):
        return lax.dot_general(a, b, dims, preferred_element_type=F32)

    return one(left_high, right_low) + one(left_low, right_high) + one(left_high, right_high)


def split(value, high, low, at):
    high[at], low[at] = halves(value)


def pack_kernel(factor, inverse, cov, own, send, near, lines, held, sem):
    x = lax.axis_index("row") % 2
    c = lax.axis_index("col")
    width = held.shape[1]
    blocks = held.shape[2] // 128
    block = own.shape[0] // blocks
    share = block - width
    lanes = pl.ds(pl.multiple_of(c * held.shape[2], held.shape[2]), held.shape[2])
    copies = [
        pltpu.make_async_copy(factor, lines, sem.at[0]),
        pltpu.make_async_copy(inverse.at[:, :, lanes], held, sem.at[1]),
        pltpu.make_async_copy(cov, near.at[pl.ds(own.shape[0], cov.shape[0]), :], sem.at[2]),
    ]
    for copy in copies:
        copy.start()
    copies[0].wait()
    copies[1].wait()
    for outs, member in (((own,), x), ((send, near), 1 - x)):
        for b in range(blocks):
            rows = lines[pl.ds(2 * b + member, share, stride=2 * blocks), :]
            cols = held[member, :, b * 128:(b + 1) * 128]
            for out in outs:
                out[b * block:b * block + share, :] = rows
                out[b * block + share:(b + 1) * block, :] = cols
    copies[2].wait()


def product_kernel(share, tile, slots, structure, live, place, c_own, *refs):
    mine = refs[:8]
    theirs = refs[8:13]
    near_theirs, c_sib = refs[13:15]
    panel_out = refs[15:17]
    w_out = refs[17:21]
    f_high, f_low, d_high, d_low = refs[21:25]
    pick, product = refs[25:]
    z, x, c = place[0], place[1], place[2]
    size = mine[0].shape[0]
    whole = d_high.shape[0]
    half = whole // 2
    lane_blocks = half // 128
    block = size // lane_blocks
    width = block - share
    wide = 2 * width
    near_x = 1 - x
    sources = (
        2 * z + x,
        2 * (z ^ 2) + x,
        2 * (z ^ 2) + near_x,
        2 * (z ^ 1) + x,
        2 * (z ^ 1) + near_x,
        2 * (z ^ 3) + x,
        2 * (z ^ 3) + near_x,
        2 * z + near_x,
    )
    blocks = c_own.shape[0] // tile
    for slot in range(slots):
        anc = structure[x, slot]
        for which, (here, there, start) in enumerate(
            ((c_own, c_sib, 0), (mine[7], near_theirs, size))
        ):
            rows = pl.ds(start + anc // 2, tile, stride=blocks)
            value = jnp.where(anc % 2 == c, here[rows, :], there[rows, :])
            at = pl.ds(pl.multiple_of((x ^ which) * tile, tile), tile)
            pick[at, slot * tile:(slot + 1) * tile] = jnp.where(slot < live[x], value, 0.0)
    for index, source in enumerate(sources):
        f_at = pl.ds(pl.multiple_of(source * share, share), share)
        d_at = pl.ds(pl.multiple_of(source * width, width), width)
        there = (near_theirs, 0)
        if index < 7:
            message, start = THERE[index]
            there = (theirs[message], start * size)
        for first, (ref, start) in ((0, (mine[index], 0)), (half, there)):
            for b in range(lane_blocks):
                lanes = slice(first + b * 128, first + (b + 1) * 128)
                top = start + b * block
                split(ref[top:top + share, :], f_high, f_low, (f_at, lanes))
                split(ref[top + share:top + block, :], d_high, d_low, (d_at, lanes))
    grown = dot3(halves(pick[...]), (f_high[...], f_low[...]), NN)
    product[...] = dot3(halves(grown), (d_high[...], d_low[...]), NT)
    lanes = pl.ds(pl.multiple_of(c * half, half), half)
    for which in range(2):
        at = pl.ds(pl.multiple_of((x ^ which) * tile, tile), tile)
        used = False
        for slot in range(slots):
            used = used | ((slot < live[x]) & (structure[x, slot] == 2 * z + (x ^ which)))
        panel_out[which][...] = jnp.where(used, -product[at, lanes], 0.0)
    low_lane = lax.broadcasted_iota(jnp.int32, (tile, wide), 1) < width
    for step in range(4):
        columns = pl.ds(pl.multiple_of((z ^ step) * wide, wide), wide)
        first = product[:tile, columns]
        second = product[tile:, columns]
        left = jnp.where(c == 0, first, pltpu.roll(first, width, 1))
        right = jnp.where(c == 0, pltpu.roll(second, width, 1), second)
        w_out[step][...] = jnp.where(low_lane, left, right)


def scaled_kernel(place, f_high, f_low, d_high, d_low, s_high, s_low, base):
    z, c = place[0], place[2]
    width = base.shape[0]
    inverse = (d_high[...], d_low[...])
    scaled = dot3((f_high[...], f_low[...]), inverse, NT)
    s_high[...], s_low[...] = halves(scaled)
    at = pl.ds(pl.multiple_of((2 * z + c) * width, width), width)
    base[...] = dot3((d_high[at, :], d_low[at, :]), inverse, NT)


def diag_kernel(tile, slots, structure, live, place, w0, w1, w2, w3, s_high, s_low, base, *refs):
    keep, cross, w_all, pick_high, pick_low, total = refs
    z, x = place[0], place[1]
    half = keep.shape[1]
    width = keep.shape[0]
    for step, piece in enumerate((w0, w1, w2, w3)):
        w_all[z ^ step] = piece[...]
    for slot in range(slots):
        anc = structure[x, slot]
        value = w_all[anc // 2]
        value = jnp.where(anc % 2 == 0, value, pltpu.roll(value, width, 1))
        at = slice(slot * tile, (slot + 1) * tile)
        split(jnp.where(slot < live[x], value, 0.0), pick_high, pick_low, (at, slice(None)))
    picked = (pick_high[...], pick_low[...])
    total[...] = base[...] + dot3(picked, (s_high[...], s_low[...]), TN)[:width]
    keep[...] = total[:, pl.ds(pl.multiple_of(x * half, half), half)]
    cross[...] = total[:, pl.ds(pl.multiple_of((1 - x) * half, half), half)]


def lines_kernel(place, mine, other, out):
    x = place[1]
    blocks = mine.shape[1] // 128
    for member, value in ((x, mine), (1 - x, other)):
        for block in range(blocks):
            at = pl.ds(2 * block + member, mine.shape[0], stride=2 * blocks)
            out[at, :] = value[:, block * 128:(block + 1) * 128]


def diag_lines_kernel(place, keep, met, far, out):
    x, c = place[1], place[2]
    blocks = keep.shape[1] // 128
    mine = jnp.where(c == x, keep[...], met[...])
    other = jnp.where(c == x, met[...], far[...])
    for member, value in ((x, mine), (1 - x, other)):
        for block in range(blocks):
            at = pl.ds(2 * block + member, keep.shape[0], stride=2 * blocks)
            out[at, :] = value[:, block * 128:(block + 1) * 128]


def many_rows(ancestor_cov, panel_factor, diag_inverse, structure, live_counts):
    tile_rows = ancestor_cov.shape[0]
    local_blocks = ancestor_cov.shape[1]
    col_count = lax.axis_size("col")
    col_id = lax.axis_index("col")
    row_id = lax.axis_index("row")
    flat_cov = ancestor_cov.reshape(tile_rows, local_blocks * tile_rows)
    half_width = panel_factor.shape[2]
    slot_total = structure.shape[1]
    whole_inverse = lax.all_gather(diag_inverse, "row", axis=2, tiled=True)
    inverse_part = lax.dynamic_slice_in_dim(whole_inverse, col_id * half_width, half_width, 0)
    factor_term = jnp.einsum(
        "rsk,ksn->rsn", panel_factor, inverse_part, precision=lax.Precision.HIGHEST
    )
    slot_index = jnp.arange(slot_total, dtype=jnp.int32)
    slot_alive = slot_index[None, :] < live_counts[:, None]
    own_slot = slot_alive & (structure == row_id)
    in_struct = jnp.any(own_slot, axis=1)
    own_pos = jnp.sum(jnp.where(own_slot, slot_index[None, :], 0), axis=1)
    tile_offsets = jnp.arange(tile_rows, dtype=jnp.int32)
    factor_rows = lax.psum(factor_term, "col")
    arrived = lax.all_gather(factor_rows, "row", axis=0, tiled=True)
    row_count = arrived.shape[0]
    global_row = jnp.arange(row_count, dtype=jnp.int32)
    slot_of = global_row // tile_rows
    offset = global_row % tile_rows
    chooser = (slot_of[:, None] == slot_index[None, :]).astype(jnp.int32)
    product_list = []
    owned_list = []
    for member in range(2):
        anc_block = jnp.sum(chooser * structure[member][None, :], axis=1)
        is_live = slot_of < live_counts[member]
        is_match = is_live & (anc_block % col_count == col_id)
        column_index = anc_block // col_count * tile_rows + offset
        sig_cols = jnp.take(flat_cov, column_index, axis=1)
        weighted = jnp.where(is_match[:, None], arrived[:, member, :], 0.0)
        product_list.append(
            jnp.dot(
                sig_cols,
                weighted,
                precision=lax.Precision.HIGHEST,
                preferred_element_type=jnp.float32,
            )
        )
        source = own_pos[member] * tile_rows + tile_offsets
        in_range = in_struct[member] & (source >= 0) & (source < row_count)
        fetched = jnp.take(arrived[:, member, :], jnp.clip(source, 0, row_count - 1), axis=0)
        owned_list.append(jnp.where(in_range[:, None], fetched, 0.0))
    partial_sum = jnp.stack(product_list, axis=1)
    owned = jnp.stack(owned_list, axis=1)
    summed_all = lax.psum(partial_sum, "col")
    product_half = lax.dynamic_slice_in_dim(summed_all, col_id * half_width, half_width, 2)
    panel_cov = -product_half * in_struct.astype(jnp.float32)[None, :, None]
    spread_term = lax.psum_scatter(
        jnp.einsum("tsi,tsn->isn", owned, product_half, precision=lax.Precision.HIGHEST),
        "row",
        scatter_dimension=0,
        tiled=True,
    )
    inverse_half = lax.dynamic_slice_in_dim(whole_inverse, col_id * half_width, half_width, 2)
    base_term = jnp.einsum(
        "ksi,ksn->isn", diag_inverse, inverse_half, precision=lax.Precision.HIGHEST
    )
    diag_cov = base_term + spread_term
    return (panel_cov, diag_cov)


def local(ancestor_cov, panel_factor, diag_inverse, structure, live_counts):
    rows = lax.axis_size("row")
    if rows != 8:
        return many_rows(ancestor_cov, panel_factor, diag_inverse, structure, live_counts)
    tile = ancestor_cov.shape[0]
    share, _, half = panel_factor.shape
    whole, _, width = diag_inverse.shape
    slots = structure.shape[1]
    col = lax.axis_index("col")
    row = lax.axis_index("row")
    place = jnp.stack([row // 2, row % 2, col]).astype(jnp.int32)
    smem = pl.BlockSpec(memory_space=pltpu.SMEM)
    vmem = pl.BlockSpec(memory_space=pltpu.VMEM)

    def like(*shape, dtype=F32):
        return jax.ShapeDtypeStruct(shape, dtype)

    def call(kernel, name, outs, scalars, arrays, scratch=(), space=vmem, limit=VMEM_LIMIT):
        return pl.pallas_call(
            kernel,
            out_shape=outs,
            in_specs=[smem] * len(scalars) + [space] * len(arrays),
            out_specs=[vmem] * len(outs),
            scratch_shapes=list(scratch),
            compiler_params=pltpu.CompilerParams(vmem_limit_bytes=limit),
            name=name,
        )(*scalars, *arrays)

    def send_to(value, target):
        pairs = []
        for r in range(rows):
            for c in range(2):
                to = target(r // 2, r % 2, c)
                if to is not None:
                    pairs.append((r * 2 + c, (to[0] * 2 + to[1]) * 2 + to[2]))
        return lax.ppermute(value, ("row", "col"), pairs)

    def move(value, z_step, x_step, flip):
        return send_to(value, lambda z, x, c: (z ^ z_step, x ^ x_step, c ^ flip))

    factor_lines = (
        panel_factor.reshape(share, 2, half // 128, 128).transpose(0, 2, 1, 3).reshape(-1, 128)
    )
    c_own = ancestor_cov.reshape(-1, 128)
    bundle = (share + width) * half // 128
    own, send, send_near = call(
        pack_kernel,
        "pack",
        [like(bundle, 128)] * 2 + [like(bundle + c_own.shape[0], 128)],
        [],
        [
            pltpu.with_memory_space_constraint(v, pltpu.HBM)
            for v in (factor_lines, diag_inverse.transpose(1, 2, 0), c_own)
        ],
        [
            pltpu.VMEM(factor_lines.shape, F32),
            pltpu.VMEM((2, width, half), F32),
            pltpu.SemaphoreType.DMA((3,)),
        ],
        pl.BlockSpec(memory_space=pltpu.HBM),
    )
    own_far = move(own, 2, 0, 0)
    near_far = move(send, 2, 1, 0)
    own_side = move(own, 1, 0, 0)
    near_side = move(send, 1, 1, 0)
    near = move(send_near, 0, 1, 0)
    own_opposite = move(own_far, 1, 0, 0)
    near_opposite = move(near_far, 1, 0, 0)
    mine = [own, own_far, near_far, own_side, near_side, own_opposite, near_opposite, near]
    theirs = [
        move(jnp.concatenate([own_far, near_far]), 0, 0, 1),
        move(jnp.concatenate([own_side, near_side]), 0, 0, 1),
        move(own, 0, 0, 1),
        move(own_opposite, 0, 0, 1),
        move(near_opposite, 0, 0, 1),
        move(near, 0, 0, 1),
        move(c_own, 0, 0, 1),
    ]
    split_f = [like(slots * tile, whole, dtype=BF16)] * 2
    split_d = [like(whole, whole, dtype=BF16)] * 2
    outs = call(
        functools.partial(product_kernel, share, tile, slots),
        "products",
        [like(tile, half)] * 2 + [like(tile, 2 * width)] * 4 + split_f + split_d,
        [structure, live_counts, place],
        [c_own, *mine, *theirs],
        [pltpu.VMEM((2 * tile, slots * tile), F32), pltpu.VMEM((2 * tile, whole), F32)],
    )
    panel, w, parts = outs[:2], outs[2:6], outs[6:]
    w = [w[0]] + [move(w[step], step, 0, 0) for step in range(1, 4)]
    s_high, s_low, base = call(
        scaled_kernel, "scaled", split_f + [like(width, whole)], [place], parts
    )
    panel_send, w[1] = lax.optimization_barrier((panel[1], w[1]))
    panel_got = move(panel_send, 0, 1, 0)
    keep, cross = call(
        functools.partial(diag_kernel, tile, slots),
        "diag_block",
        [like(width, half)] * 2,
        [structure, live_counts, place],
        [*w, s_high, s_low, base],
        [
            pltpu.VMEM((rows // 2, tile, 2 * width), F32),
            pltpu.VMEM((slots * tile, 2 * width), BF16),
            pltpu.VMEM((slots * tile, 2 * width), BF16),
            pltpu.VMEM((width, whole), F32),
        ],
    )
    met = send_to(cross, lambda z, x, c: (z, x, 1 - c) if c == x else (z, 1 - x, c))
    far = send_to(keep, lambda z, x, c: None if c == x else (z, 1 - x, 1 - c))
    lines = 2 * half // 128
    panel_got, keep = lax.optimization_barrier((panel_got, keep))
    (panel_lines,) = call(
        lines_kernel, "panel_lines", [like(tile * lines, 128)], [place], [panel[0], panel_got]
    )
    panel_lines, keep = lax.optimization_barrier((panel_lines, keep))
    (diag_lines,) = call(
        diag_lines_kernel, "diag_lines", [like(width * lines, 128)], [place], [keep, met, far]
    )

    def unfold(value, count):
        return value.reshape(count, half // 128, 2, 128).transpose(0, 2, 1, 3).reshape(count, 2, half)

    return unfold(panel_lines, tile), unfold(diag_lines, width)


def solution(mesh):
    placed = (
        P(("mp", "row"), None, "col", None),
        P(("mp", "row"), None, "col"),
        P("mp", None, "row"),
        P("mp", None),
        P("mp"),
    )
    return jax.shard_map(
        local,
        mesh=mesh,
        in_specs=placed,
        out_specs=(P(("mp", "row"), None, "col"), P(("mp", "row"), None, "col")),
        check_vma=False,
    )
```

```python
import functools

import jax
import jax.numpy as jnp
from jax import lax
from jax.experimental import pallas as pl
from jax.experimental.pallas import tpu as pltpu
from jax.sharding import PartitionSpec as P

F32 = jnp.float32
BF16 = jnp.bfloat16
NT = (((1,), (1,)), ((), ()))
NN = (((1,), (0,)), ((), ()))
TN = (((0,), (0,)), ((), ()))
VMEM_LIMIT = 20 * 1024 * 1024
THERE = ((2, 0), (0, 0), (0, 1), (1, 0), (1, 1), (3, 0), (3, 1))


def halves(value):
    high = value.astype(BF16)
    low = (value - high.astype(F32)).astype(BF16)
    return high, low


def dot3(left, right, dims):
    left_high, left_low = left
    right_high, right_low = right

    def one(a, b):
        return lax.dot_general(a, b, dims, preferred_element_type=F32)

    return one(left_high, right_low) + one(left_low, right_high) + one(left_high, right_high)


def split(value, high, low, at):
    high[at], low[at] = halves(value)


def pack_kernel(factor, inverse, cov, own, send, near, lines, held, sem):
    x = lax.axis_index("row") % 2
    c = lax.axis_index("col")
    width = held.shape[1]
    blocks = held.shape[2] // 128
    block = own.shape[0] // blocks
    share = block - width
    lanes = pl.ds(pl.multiple_of(c * held.shape[2], held.shape[2]), held.shape[2])
    copies = [
        pltpu.make_async_copy(factor, lines, sem.at[0]),
        pltpu.make_async_copy(inverse.at[:, :, lanes], held, sem.at[1]),
        pltpu.make_async_copy(cov, near.at[pl.ds(own.shape[0], cov.shape[0]), :], sem.at[2]),
    ]
    for copy in copies:
        copy.start()
    copies[0].wait()
    copies[1].wait()
    for outs, member in (((own,), x), ((send, near), 1 - x)):
        for b in range(blocks):
            rows = lines[pl.ds(2 * b + member, share, stride=2 * blocks), :]
            cols = held[member, :, b * 128:(b + 1) * 128]
            for out in outs:
                out[b * block:b * block + share, :] = rows
                out[b * block + share:(b + 1) * block, :] = cols
    copies[2].wait()


def product_kernel(share, tile, slots, structure, live, place, c_own, *refs):
    mine = refs[:8]
    theirs = refs[8:12]
    near_theirs, c_sib = refs[12:14]
    panel_out = refs[14:16]
    w_out = refs[16:20]
    f_high, f_low, d_high, d_low = refs[20:24]
    pick, product = refs[24:]
    z, x, c = place[0], place[1], place[2]
    size = mine[0].shape[0]
    whole = d_high.shape[0]
    half = whole // 2
    lane_blocks = half // 128
    block = size // lane_blocks
    width = block - share
    wide = 2 * width
    near_x = 1 - x
    sources = (
        2 * z + x,
        2 * (z ^ 2) + x,
        2 * (z ^ 2) + near_x,
        2 * (z ^ 1) + x,
        2 * (z ^ 1) + near_x,
        2 * (z ^ 3) + x,
        2 * (z ^ 3) + near_x,
        2 * z + near_x,
    )
    blocks = c_own.shape[0] // tile
    for slot in range(slots):
        anc = structure[x, slot]
        for which, (here, there, start) in enumerate(
            ((c_own, c_sib, 0), (mine[7], near_theirs, size))
        ):
            rows = pl.ds(start + anc // 2, tile, stride=blocks)
            value = jnp.where(anc % 2 == c, here[rows, :], there[rows, :])
            at = pl.ds(pl.multiple_of((x ^ which) * tile, tile), tile)
            pick[at, slot * tile:(slot + 1) * tile] = jnp.where(slot < live[x], value, 0.0)
    for index, source in enumerate(sources):
        f_at = pl.ds(pl.multiple_of(source * share, share), share)
        d_at = pl.ds(pl.multiple_of(source * width, width), width)
        there = (near_theirs, 0)
        if index < 7:
            message, start = THERE[index]
            there = (theirs[message], start * size)
        for first, (ref, start) in ((0, (mine[index], 0)), (half, there)):
            for b in range(lane_blocks):
                lanes = slice(first + b * 128, first + (b + 1) * 128)
                top = start + b * block
                split(ref[top:top + share, :], f_high, f_low, (f_at, lanes))
                split(ref[top + share:top + block, :], d_high, d_low, (d_at, lanes))
    grown = dot3(halves(pick[...]), (f_high[...], f_low[...]), NN)
    product[...] = dot3(halves(grown), (d_high[...], d_low[...]), NT)
    lanes = pl.ds(pl.multiple_of(c * half, half), half)
    for which in range(2):
        at = pl.ds(pl.multiple_of((x ^ which) * tile, tile), tile)
        used = False
        for slot in range(slots):
            used = used | ((slot < live[x]) & (structure[x, slot] == 2 * z + (x ^ which)))
        panel_out[which][...] = jnp.where(used, -product[at, lanes], 0.0)
    low_lane = lax.broadcasted_iota(jnp.int32, (tile, wide), 1) < width
    for step in range(4):
        columns = pl.ds(pl.multiple_of((z ^ step) * wide, wide), wide)
        first = product[:tile, columns]
        second = product[tile:, columns]
        left = jnp.where(c == 0, first, pltpu.roll(first, width, 1))
        right = jnp.where(c == 0, pltpu.roll(second, width, 1), second)
        w_out[step][...] = jnp.where(low_lane, left, right)


def scaled_kernel(place, f_high, f_low, d_high, d_low, s_high, s_low, base):
    z, c = place[0], place[2]
    width = base.shape[0]
    inverse = (d_high[...], d_low[...])
    scaled = dot3((f_high[...], f_low[...]), inverse, NT)
    s_high[...], s_low[...] = halves(scaled)
    at = pl.ds(pl.multiple_of((2 * z + c) * width, width), width)
    base[...] = dot3((d_high[at, :], d_low[at, :]), inverse, NT)


def diag_kernel(tile, slots, structure, live, place, w0, w1, w2, w3, s_high, s_low, base, *refs):
    keep, cross, w_all, pick_high, pick_low, total = refs
    z, x = place[0], place[1]
    half = keep.shape[1]
    width = keep.shape[0]
    for step, piece in enumerate((w0, w1, w2, w3)):
        w_all[z ^ step] = piece[...]
    for slot in range(slots):
        anc = structure[x, slot]
        value = w_all[anc // 2]
        value = jnp.where(anc % 2 == 0, value, pltpu.roll(value, width, 1))
        at = slice(slot * tile, (slot + 1) * tile)
        split(jnp.where(slot < live[x], value, 0.0), pick_high, pick_low, (at, slice(None)))
    picked = (pick_high[...], pick_low[...])
    total[...] = base[...] + dot3(picked, (s_high[...], s_low[...]), TN)[:width]
    keep[...] = total[:, pl.ds(pl.multiple_of(x * half, half), half)]
    cross[...] = total[:, pl.ds(pl.multiple_of((1 - x) * half, half), half)]


def lines_kernel(place, mine, other, out):
    x = place[1]
    blocks = mine.shape[1] // 128
    for member, value in ((x, mine), (1 - x, other)):
        for block in range(blocks):
            at = pl.ds(2 * block + member, mine.shape[0], stride=2 * blocks)
            out[at, :] = value[:, block * 128:(block + 1) * 128]


def diag_lines_kernel(place, keep, met, far, out):
    x, c = place[1], place[2]
    blocks = keep.shape[1] // 128
    mine = jnp.where(c == x, keep[...], met[...])
    other = jnp.where(c == x, met[...], far[...])
    for member, value in ((x, mine), (1 - x, other)):
        for block in range(blocks):
            at = pl.ds(2 * block + member, keep.shape[0], stride=2 * blocks)
            out[at, :] = value[:, block * 128:(block + 1) * 128]


def many_rows(ancestor_cov, panel_factor, diag_inverse, structure, live_counts):
    tile_rows = ancestor_cov.shape[0]
    local_blocks = ancestor_cov.shape[1]
    col_count = lax.axis_size("col")
    col_id = lax.axis_index("col")
    row_id = lax.axis_index("row")
    flat_cov = ancestor_cov.reshape(tile_rows, local_blocks * tile_rows)
    half_width = panel_factor.shape[2]
    slot_total = structure.shape[1]
    whole_inverse = lax.all_gather(diag_inverse, "row", axis=2, tiled=True)
    inverse_part = lax.dynamic_slice_in_dim(whole_inverse, col_id * half_width, half_width, 0)
    factor_term = jnp.einsum(
        "rsk,ksn->rsn", panel_factor, inverse_part, precision=lax.Precision.HIGHEST
    )
    slot_index = jnp.arange(slot_total, dtype=jnp.int32)
    slot_alive = slot_index[None, :] < live_counts[:, None]
    own_slot = slot_alive & (structure == row_id)
    in_struct = jnp.any(own_slot, axis=1)
    own_pos = jnp.sum(jnp.where(own_slot, slot_index[None, :], 0), axis=1)
    tile_offsets = jnp.arange(tile_rows, dtype=jnp.int32)
    factor_rows = lax.psum(factor_term, "col")
    arrived = lax.all_gather(factor_rows, "row", axis=0, tiled=True)
    row_count = arrived.shape[0]
    global_row = jnp.arange(row_count, dtype=jnp.int32)
    slot_of = global_row // tile_rows
    offset = global_row % tile_rows
    chooser = (slot_of[:, None] == slot_index[None, :]).astype(jnp.int32)
    product_list = []
    owned_list = []
    for member in range(2):
        anc_block = jnp.sum(chooser * structure[member][None, :], axis=1)
        is_live = slot_of < live_counts[member]
        is_match = is_live & (anc_block % col_count == col_id)
        column_index = anc_block // col_count * tile_rows + offset
        sig_cols = jnp.take(flat_cov, column_index, axis=1)
        weighted = jnp.where(is_match[:, None], arrived[:, member, :], 0.0)
        product_list.append(
            jnp.dot(
                sig_cols,
                weighted,
                precision=lax.Precision.HIGHEST,
                preferred_element_type=jnp.float32,
            )
        )
        source = own_pos[member] * tile_rows + tile_offsets
        in_range = in_struct[member] & (source >= 0) & (source < row_count)
        fetched = jnp.take(arrived[:, member, :], jnp.clip(source, 0, row_count - 1), axis=0)
        owned_list.append(jnp.where(in_range[:, None], fetched, 0.0))
    partial_sum = jnp.stack(product_list, axis=1)
    owned = jnp.stack(owned_list, axis=1)
    summed_all = lax.psum(partial_sum, "col")
    product_half = lax.dynamic_slice_in_dim(summed_all, col_id * half_width, half_width, 2)
    panel_cov = -product_half * in_struct.astype(jnp.float32)[None, :, None]
    spread_term = lax.psum_scatter(
        jnp.einsum("tsi,tsn->isn", owned, product_half, precision=lax.Precision.HIGHEST),
        "row",
        scatter_dimension=0,
        tiled=True,
    )
    inverse_half = lax.dynamic_slice_in_dim(whole_inverse, col_id * half_width, half_width, 2)
    base_term = jnp.einsum(
        "ksi,ksn->isn", diag_inverse, inverse_half, precision=lax.Precision.HIGHEST
    )
    diag_cov = base_term + spread_term
    return (panel_cov, diag_cov)


def local(ancestor_cov, panel_factor, diag_inverse, structure, live_counts):
    rows = lax.axis_size("row")
    if rows != 8:
        return many_rows(ancestor_cov, panel_factor, diag_inverse, structure, live_counts)
    tile = ancestor_cov.shape[0]
    share, _, half = panel_factor.shape
    whole, _, width = diag_inverse.shape
    slots = structure.shape[1]
    col = lax.axis_index("col")
    row = lax.axis_index("row")
    place = jnp.stack([row // 2, row % 2, col]).astype(jnp.int32)
    smem = pl.BlockSpec(memory_space=pltpu.SMEM)
    vmem = pl.BlockSpec(memory_space=pltpu.VMEM)

    def like(*shape, dtype=F32):
        return jax.ShapeDtypeStruct(shape, dtype)

    def call(kernel, name, outs, scalars, arrays, scratch=(), space=vmem, limit=VMEM_LIMIT):
        return pl.pallas_call(
            kernel,
            out_shape=outs,
            in_specs=[smem] * len(scalars) + [space] * len(arrays),
            out_specs=[vmem] * len(outs),
            scratch_shapes=list(scratch),
            compiler_params=pltpu.CompilerParams(vmem_limit_bytes=limit),
            name=name,
        )(*scalars, *arrays)

    def send_to(value, target):
        pairs = []
        for r in range(rows):
            for c in range(2):
                to = target(r // 2, r % 2, c)
                if to is not None:
                    pairs.append((r * 2 + c, (to[0] * 2 + to[1]) * 2 + to[2]))
        return lax.ppermute(value, ("row", "col"), pairs)

    def move(value, z_step, x_step, flip):
        return send_to(value, lambda z, x, c: (z ^ z_step, x ^ x_step, c ^ flip))

    factor_lines = (
        panel_factor.reshape(share, 2, half // 128, 128).transpose(0, 2, 1, 3).reshape(-1, 128)
    )
    c_own = ancestor_cov.reshape(-1, 128)
    bundle = (share + width) * half // 128
    own, send, send_near = call(
        pack_kernel,
        "pack",
        [like(bundle, 128)] * 2 + [like(bundle + c_own.shape[0], 128)],
        [],
        [
            pltpu.with_memory_space_constraint(v, pltpu.HBM)
            for v in (factor_lines, diag_inverse.transpose(1, 2, 0), c_own)
        ],
        [
            pltpu.VMEM(factor_lines.shape, F32),
            pltpu.VMEM((2, width, half), F32),
            pltpu.SemaphoreType.DMA((3,)),
        ],
        pl.BlockSpec(memory_space=pltpu.HBM),
    )
    own_far = move(own, 2, 0, 0)
    near_far = move(send, 2, 1, 0)
    own_side = move(own, 1, 0, 0)
    near_side = move(send, 1, 1, 0)
    near = move(send_near, 0, 1, 0)
    own_opposite = move(own_far, 1, 0, 0)
    near_far, near = lax.optimization_barrier((near_far, near))
    near_opposite = move(near_far, 1, 0, 0)
    c_sib = move(c_own, 0, 0, 1)
    near_in, c_sib = lax.optimization_barrier((near, c_sib))
    mine = [own, own_far, near_far, own_side, near_side, own_opposite, near_opposite, near]
    theirs = [
        move(jnp.concatenate([own_far, near_far]), 0, 0, 1),
        move(jnp.concatenate([own_side, near_side]), 0, 0, 1),
        move(own, 0, 0, 1),
        move(jnp.concatenate([own_opposite, near_opposite]), 0, 0, 1),
        move(near_in, 0, 0, 1),
        c_sib,
    ]
    split_f = [like(slots * tile, whole, dtype=BF16)] * 2
    split_d = [like(whole, whole, dtype=BF16)] * 2
    outs = call(
        functools.partial(product_kernel, share, tile, slots),
        "products",
        [like(tile, half)] * 2 + [like(tile, 2 * width)] * 4 + split_f + split_d,
        [structure, live_counts, place],
        [c_own, *mine, *theirs],
        [pltpu.VMEM((2 * tile, slots * tile), F32), pltpu.VMEM((2 * tile, whole), F32)],
    )
    panel, w, parts = outs[:2], outs[2:6], outs[6:]
    w = [w[0]] + [move(w[step], step, 0, 0) for step in range(1, 4)]
    s_high, s_low, base = call(
        scaled_kernel, "scaled", split_f + [like(width, whole)], [place], parts
    )
    panel_send, w[1] = lax.optimization_barrier((panel[1], w[1]))
    panel_got = move(panel_send, 0, 1, 0)
    keep, cross = call(
        functools.partial(diag_kernel, tile, slots),
        "diag_block",
        [like(width, half)] * 2,
        [structure, live_counts, place],
        [*w, s_high, s_low, base],
        [
            pltpu.VMEM((rows // 2, tile, 2 * width), F32),
            pltpu.VMEM((slots * tile, 2 * width), BF16),
            pltpu.VMEM((slots * tile, 2 * width), BF16),
            pltpu.VMEM((width, whole), F32),
        ],
    )
    met = send_to(cross, lambda z, x, c: (z, x, 1 - c) if c == x else (z, 1 - x, c))
    far = send_to(keep, lambda z, x, c: None if c == x else (z, 1 - x, 1 - c))
    lines = 2 * half // 128
    panel_got, keep = lax.optimization_barrier((panel_got, keep))
    (panel_lines,) = call(
        lines_kernel, "panel_lines", [like(tile * lines, 128)], [place], [panel[0], panel_got]
    )
    panel_lines, keep = lax.optimization_barrier((panel_lines, keep))
    (diag_lines,) = call(
        diag_lines_kernel, "diag_lines", [like(width * lines, 128)], [place], [keep, met, far]
    )

    def unfold(value, count):
        return value.reshape(count, half // 128, 2, 128).transpose(0, 2, 1, 3).reshape(count, 2, half)

    return unfold(panel_lines, tile), unfold(diag_lines, width)


def solution(mesh):
    placed = (
        P(("mp", "row"), None, "col", None),
        P(("mp", "row"), None, "col"),
        P("mp", None, "row"),
        P("mp", None),
        P("mp"),
    )
    return jax.shard_map(
        local,
        mesh=mesh,
        in_specs=placed,
        out_specs=(P(("mp", "row"), None, "col"), P(("mp", "row"), None, "col")),
        check_vma=False,
    )
```

```python
import functools

import jax
import jax.numpy as jnp
from jax import lax
from jax.experimental import pallas as pl
from jax.experimental.pallas import tpu as pltpu
from jax.sharding import PartitionSpec as P

F32 = jnp.float32
BF16 = jnp.bfloat16
NT = (((1,), (1,)), ((), ()))
NN = (((1,), (0,)), ((), ()))
TN = (((0,), (0,)), ((), ()))
VMEM_LIMIT = 10 * 1024 * 1024
THERE = ((2, 0), (0, 0), (0, 1), (1, 0), (1, 1), (3, 0), (3, 1))


def halves(value):
    high = value.astype(BF16)
    low = (value - high.astype(F32)).astype(BF16)
    return high, low


def dot3(left, right, dims):
    left_high, left_low = left
    right_high, right_low = right

    def one(a, b):
        return lax.dot_general(a, b, dims, preferred_element_type=F32)

    return one(left_high, right_low) + one(left_low, right_high) + one(left_high, right_high)


def split(value, high, low, at):
    high[at], low[at] = halves(value)


def pack_kernel(factor, inverse, cov, own, send, near, lines, held, sem):
    x = lax.axis_index("row") % 2
    c = lax.axis_index("col")
    width = held.shape[1]
    blocks = held.shape[2] // 128
    block = own.shape[0] // blocks
    share = block - width
    lanes = pl.ds(pl.multiple_of(c * held.shape[2], held.shape[2]), held.shape[2])
    copies = [
        pltpu.make_async_copy(factor, lines, sem.at[0]),
        pltpu.make_async_copy(inverse.at[:, :, lanes], held, sem.at[1]),
        pltpu.make_async_copy(cov, near.at[pl.ds(own.shape[0], cov.shape[0]), :], sem.at[2]),
    ]
    for copy in copies:
        copy.start()
    copies[0].wait()
    copies[1].wait()
    for outs, member in (((own,), x), ((send, near), 1 - x)):
        for b in range(blocks):
            rows = lines[pl.ds(2 * b + member, share, stride=2 * blocks), :]
            cols = held[member, :, b * 128:(b + 1) * 128]
            for out in outs:
                out[b * block:b * block + share, :] = rows
                out[b * block + share:(b + 1) * block, :] = cols
    copies[2].wait()


def product_kernel(share, tile, slots, structure, live, place, c_own, *refs):
    mine = refs[:8]
    theirs = refs[8:12]
    near_theirs, c_sib = refs[12:14]
    panel_out = refs[14:16]
    w_out = refs[16:20]
    f_high, f_low, d_high, d_low = refs[20:24]
    pick, product = refs[24:]
    z, x, c = place[0], place[1], place[2]
    size = mine[0].shape[0]
    whole = d_high.shape[0]
    half = whole // 2
    lane_blocks = half // 128
    block = size // lane_blocks
    width = block - share
    wide = 2 * width
    near_x = 1 - x
    sources = (
        2 * z + x,
        2 * (z ^ 2) + x,
        2 * (z ^ 2) + near_x,
        2 * (z ^ 1) + x,
        2 * (z ^ 1) + near_x,
        2 * (z ^ 3) + x,
        2 * (z ^ 3) + near_x,
        2 * z + near_x,
    )
    blocks = c_own.shape[0] // tile
    for slot in range(slots):
        anc = structure[x, slot]
        for which, (here, there, start) in enumerate(
            ((c_own, c_sib, 0), (mine[7], near_theirs, size))
        ):
            rows = pl.ds(start + anc // 2, tile, stride=blocks)
            value = jnp.where(anc % 2 == c, here[rows, :], there[rows, :])
            at = pl.ds(pl.multiple_of((x ^ which) * tile, tile), tile)
            pick[at, slot * tile:(slot + 1) * tile] = jnp.where(slot < live[x], value, 0.0)
    for index, source in enumerate(sources):
        f_at = pl.ds(pl.multiple_of(source * share, share), share)
        d_at = pl.ds(pl.multiple_of(source * width, width), width)
        there = (near_theirs, 0)
        if index < 7:
            message, start = THERE[index]
            there = (theirs[message], start * size)
        for first, (ref, start) in ((0, (mine[index], 0)), (half, there)):
            for b in range(lane_blocks):
                lanes = slice(first + b * 128, first + (b + 1) * 128)
                top = start + b * block
                split(ref[top:top + share, :], f_high, f_low, (f_at, lanes))
                split(ref[top + share:top + block, :], d_high, d_low, (d_at, lanes))
    grown = dot3(halves(pick[...]), (f_high[...], f_low[...]), NN)
    product[...] = dot3(halves(grown), (d_high[...], d_low[...]), NT)
    lanes = pl.ds(pl.multiple_of(c * half, half), half)
    for which in range(2):
        at = pl.ds(pl.multiple_of((x ^ which) * tile, tile), tile)
        used = False
        for slot in range(slots):
            used = used | ((slot < live[x]) & (structure[x, slot] == 2 * z + (x ^ which)))
        panel_out[which][...] = jnp.where(used, -product[at, lanes], 0.0)
    low_lane = lax.broadcasted_iota(jnp.int32, (tile, wide), 1) < width
    for step in range(4):
        columns = pl.ds(pl.multiple_of((z ^ step) * wide, wide), wide)
        first = product[:tile, columns]
        second = product[tile:, columns]
        left = jnp.where(c == 0, first, pltpu.roll(first, width, 1))
        right = jnp.where(c == 0, pltpu.roll(second, width, 1), second)
        w_out[step][...] = jnp.where(low_lane, left, right)


def scaled_kernel(place, f_high, f_low, d_high, d_low, s_high, s_low, base):
    z, c = place[0], place[2]
    width = base.shape[0]
    inverse = (d_high[...], d_low[...])
    scaled = dot3((f_high[...], f_low[...]), inverse, NT)
    s_high[...], s_low[...] = halves(scaled)
    at = pl.ds(pl.multiple_of((2 * z + c) * width, width), width)
    base[...] = dot3((d_high[at, :], d_low[at, :]), inverse, NT)


def diag_kernel(tile, slots, structure, live, place, w0, w1, w2, w3, s_high, s_low, base, *refs):
    keep, cross, w_all, pick_high, pick_low, total = refs
    z, x = place[0], place[1]
    half = keep.shape[1]
    width = keep.shape[0]
    for step, piece in enumerate((w0, w1, w2, w3)):
        w_all[z ^ step] = piece[...]
    for slot in range(slots):
        anc = structure[x, slot]
        value = w_all[anc // 2]
        value = jnp.where(anc % 2 == 0, value, pltpu.roll(value, width, 1))
        at = slice(slot * tile, (slot + 1) * tile)
        split(jnp.where(slot < live[x], value, 0.0), pick_high, pick_low, (at, slice(None)))
    picked = (pick_high[...], pick_low[...])
    total[...] = base[...] + dot3(picked, (s_high[...], s_low[...]), TN)[:width]
    keep[...] = total[:, pl.ds(pl.multiple_of(x * half, half), half)]
    cross[...] = total[:, pl.ds(pl.multiple_of((1 - x) * half, half), half)]


def lines_kernel(place, mine, other, out):
    x = place[1]
    blocks = mine.shape[1] // 128
    for member, value in ((x, mine), (1 - x, other)):
        for block in range(blocks):
            at = pl.ds(2 * block + member, mine.shape[0], stride=2 * blocks)
            out[at, :] = value[:, block * 128:(block + 1) * 128]


def diag_lines_kernel(place, keep, met, far, out):
    x, c = place[1], place[2]
    blocks = keep.shape[1] // 128
    mine = jnp.where(c == x, keep[...], met[...])
    other = jnp.where(c == x, met[...], far[...])
    for member, value in ((x, mine), (1 - x, other)):
        for block in range(blocks):
            at = pl.ds(2 * block + member, keep.shape[0], stride=2 * blocks)
            out[at, :] = value[:, block * 128:(block + 1) * 128]


def many_rows(ancestor_cov, panel_factor, diag_inverse, structure, live_counts):
    tile_rows = ancestor_cov.shape[0]
    local_blocks = ancestor_cov.shape[1]
    col_count = lax.axis_size("col")
    col_id = lax.axis_index("col")
    row_id = lax.axis_index("row")
    flat_cov = ancestor_cov.reshape(tile_rows, local_blocks * tile_rows)
    half_width = panel_factor.shape[2]
    slot_total = structure.shape[1]
    whole_inverse = lax.all_gather(diag_inverse, "row", axis=2, tiled=True)
    inverse_part = lax.dynamic_slice_in_dim(whole_inverse, col_id * half_width, half_width, 0)
    factor_term = jnp.einsum(
        "rsk,ksn->rsn", panel_factor, inverse_part, precision=lax.Precision.HIGHEST
    )
    slot_index = jnp.arange(slot_total, dtype=jnp.int32)
    slot_alive = slot_index[None, :] < live_counts[:, None]
    own_slot = slot_alive & (structure == row_id)
    in_struct = jnp.any(own_slot, axis=1)
    own_pos = jnp.sum(jnp.where(own_slot, slot_index[None, :], 0), axis=1)
    tile_offsets = jnp.arange(tile_rows, dtype=jnp.int32)
    factor_rows = lax.psum(factor_term, "col")
    arrived = lax.all_gather(factor_rows, "row", axis=0, tiled=True)
    row_count = arrived.shape[0]
    global_row = jnp.arange(row_count, dtype=jnp.int32)
    slot_of = global_row // tile_rows
    offset = global_row % tile_rows
    chooser = (slot_of[:, None] == slot_index[None, :]).astype(jnp.int32)
    product_list = []
    owned_list = []
    for member in range(2):
        anc_block = jnp.sum(chooser * structure[member][None, :], axis=1)
        is_live = slot_of < live_counts[member]
        is_match = is_live & (anc_block % col_count == col_id)
        column_index = anc_block // col_count * tile_rows + offset
        sig_cols = jnp.take(flat_cov, column_index, axis=1)
        weighted = jnp.where(is_match[:, None], arrived[:, member, :], 0.0)
        product_list.append(
            jnp.dot(
                sig_cols,
                weighted,
                precision=lax.Precision.HIGHEST,
                preferred_element_type=jnp.float32,
            )
        )
        source = own_pos[member] * tile_rows + tile_offsets
        in_range = in_struct[member] & (source >= 0) & (source < row_count)
        fetched = jnp.take(arrived[:, member, :], jnp.clip(source, 0, row_count - 1), axis=0)
        owned_list.append(jnp.where(in_range[:, None], fetched, 0.0))
    partial_sum = jnp.stack(product_list, axis=1)
    owned = jnp.stack(owned_list, axis=1)
    summed_all = lax.psum(partial_sum, "col")
    product_half = lax.dynamic_slice_in_dim(summed_all, col_id * half_width, half_width, 2)
    panel_cov = -product_half * in_struct.astype(jnp.float32)[None, :, None]
    spread_term = lax.psum_scatter(
        jnp.einsum("tsi,tsn->isn", owned, product_half, precision=lax.Precision.HIGHEST),
        "row",
        scatter_dimension=0,
        tiled=True,
    )
    inverse_half = lax.dynamic_slice_in_dim(whole_inverse, col_id * half_width, half_width, 2)
    base_term = jnp.einsum(
        "ksi,ksn->isn", diag_inverse, inverse_half, precision=lax.Precision.HIGHEST
    )
    diag_cov = base_term + spread_term
    return (panel_cov, diag_cov)


def local(ancestor_cov, panel_factor, diag_inverse, structure, live_counts):
    rows = lax.axis_size("row")
    if rows != 8:
        return many_rows(ancestor_cov, panel_factor, diag_inverse, structure, live_counts)
    tile = ancestor_cov.shape[0]
    share, _, half = panel_factor.shape
    whole, _, width = diag_inverse.shape
    slots = structure.shape[1]
    col = lax.axis_index("col")
    row = lax.axis_index("row")
    place = jnp.stack([row // 2, row % 2, col]).astype(jnp.int32)
    smem = pl.BlockSpec(memory_space=pltpu.SMEM)
    vmem = pl.BlockSpec(memory_space=pltpu.VMEM)

    def like(*shape, dtype=F32):
        return jax.ShapeDtypeStruct(shape, dtype)

    def call(kernel, name, outs, scalars, arrays, scratch=(), space=vmem, limit=VMEM_LIMIT):
        return pl.pallas_call(
            kernel,
            out_shape=outs,
            in_specs=[smem] * len(scalars) + [space] * len(arrays),
            out_specs=[vmem] * len(outs),
            scratch_shapes=list(scratch),
            compiler_params=pltpu.CompilerParams(vmem_limit_bytes=limit),
            name=name,
        )(*scalars, *arrays)

    def send_to(value, target):
        pairs = []
        for r in range(rows):
            for c in range(2):
                to = target(r // 2, r % 2, c)
                if to is not None:
                    pairs.append((r * 2 + c, (to[0] * 2 + to[1]) * 2 + to[2]))
        return lax.ppermute(value, ("row", "col"), pairs)

    def move(value, z_step, x_step, flip):
        return send_to(value, lambda z, x, c: (z ^ z_step, x ^ x_step, c ^ flip))

    factor_lines = (
        panel_factor.reshape(share, 2, half // 128, 128).transpose(0, 2, 1, 3).reshape(-1, 128)
    )
    c_own = ancestor_cov.reshape(-1, 128)
    bundle = (share + width) * half // 128
    own, send, send_near = call(
        pack_kernel,
        "pack",
        [like(bundle, 128)] * 2 + [like(bundle + c_own.shape[0], 128)],
        [],
        [
            pltpu.with_memory_space_constraint(v, pltpu.HBM)
            for v in (factor_lines, diag_inverse.transpose(1, 2, 0), c_own)
        ],
        [
            pltpu.VMEM(factor_lines.shape, F32),
            pltpu.VMEM((2, width, half), F32),
            pltpu.SemaphoreType.DMA((3,)),
        ],
        pl.BlockSpec(memory_space=pltpu.HBM),
    )
    own_far = move(own, 2, 0, 0)
    near_far = move(send, 2, 1, 0)
    own_side = move(own, 1, 0, 0)
    near_side = move(send, 1, 1, 0)
    near = move(send_near, 0, 1, 0)
    own_opposite = move(own_far, 1, 0, 0)
    near_far, near = lax.optimization_barrier((near_far, near))
    near_opposite = move(near_far, 1, 0, 0)
    c_sib = move(c_own, 0, 0, 1)
    near_in, c_sib = lax.optimization_barrier((near, c_sib))
    mine = [own, own_far, near_far, own_side, near_side, own_opposite, near_opposite, near]
    theirs = [
        move(jnp.concatenate([own_far, near_far]), 0, 0, 1),
        move(jnp.concatenate([own_side, near_side]), 0, 0, 1),
        move(own, 0, 0, 1),
        move(jnp.concatenate([own_opposite, near_opposite]), 0, 0, 1),
        move(near_in, 0, 0, 1),
        c_sib,
    ]
    split_f = [like(slots * tile, whole, dtype=BF16)] * 2
    split_d = [like(whole, whole, dtype=BF16)] * 2
    outs = call(
        functools.partial(product_kernel, share, tile, slots),
        "products",
        [like(tile, half)] * 2 + [like(tile, 2 * width)] * 4 + split_f + split_d,
        [structure, live_counts, place],
        [c_own, *mine, *theirs],
        [pltpu.VMEM((2 * tile, slots * tile), F32), pltpu.VMEM((2 * tile, whole), F32)],
    )
    panel, w, parts = outs[:2], outs[2:6], outs[6:]
    w = [w[0]] + [move(w[step], step, 0, 0) for step in range(1, 4)]
    s_high, s_low, base = call(
        scaled_kernel, "scaled", split_f + [like(width, whole)], [place], parts
    )
    panel_send, w[1] = lax.optimization_barrier((panel[1], w[1]))
    panel_got = move(panel_send, 0, 1, 0)
    keep, cross = call(
        functools.partial(diag_kernel, tile, slots),
        "diag_block",
        [like(width, half)] * 2,
        [structure, live_counts, place],
        [*w, s_high, s_low, base],
        [
            pltpu.VMEM((rows // 2, tile, 2 * width), F32),
            pltpu.VMEM((slots * tile, 2 * width), BF16),
            pltpu.VMEM((slots * tile, 2 * width), BF16),
            pltpu.VMEM((width, whole), F32),
        ],
    )
    met = send_to(cross, lambda z, x, c: (z, x, 1 - c) if c == x else (z, 1 - x, c))
    far = send_to(keep, lambda z, x, c: None if c == x else (z, 1 - x, 1 - c))
    lines = 2 * half // 128
    panel_got, keep = lax.optimization_barrier((panel_got, keep))
    (panel_lines,) = call(
        lines_kernel, "panel_lines", [like(tile * lines, 128)], [place], [panel[0], panel_got]
    )
    panel_lines, keep = lax.optimization_barrier((panel_lines, keep))
    (diag_lines,) = call(
        diag_lines_kernel, "diag_lines", [like(width * lines, 128)], [place], [keep, met, far]
    )

    def unfold(value, count):
        return value.reshape(count, half // 128, 2, 128).transpose(0, 2, 1, 3).reshape(count, 2, half)

    return unfold(panel_lines, tile), unfold(diag_lines, width)


def solution(mesh):
    placed = (
        P(("mp", "row"), None, "col", None),
        P(("mp", "row"), None, "col"),
        P("mp", None, "row"),
        P("mp", None),
        P("mp"),
    )
    return jax.shard_map(
        local,
        mesh=mesh,
        in_specs=placed,
        out_specs=(P(("mp", "row"), None, "col"), P(("mp", "row"), None, "col")),
        check_vma=False,
    )
```

```python
import functools

import jax
import jax.numpy as jnp
from jax import lax
from jax.experimental import pallas as pl
from jax.experimental.pallas import tpu as pltpu
from jax.sharding import PartitionSpec as P

F32 = jnp.float32
BF16 = jnp.bfloat16
NT = (((1,), (1,)), ((), ()))
NN = (((1,), (0,)), ((), ()))
TN = (((0,), (0,)), ((), ()))
VMEM_LIMIT = 20 * 1024 * 1024
THERE = ((2, 0), (0, 0), (0, 1), (1, 0), (1, 1), (3, 0), (3, 1))


def halves(value):
    high = value.astype(BF16)
    low = (value - high.astype(F32)).astype(BF16)
    return high, low


def dot3(left, right, dims):
    left_high, left_low = left
    right_high, right_low = right

    def one(a, b):
        return lax.dot_general(a, b, dims, preferred_element_type=F32)

    return one(left_high, right_low) + one(left_low, right_high) + one(left_high, right_high)


def split(value, high, low, at):
    high[at], low[at] = halves(value)


def pack_kernel(factor, inverse, cov, own, send, near, lines, held, sem):
    x = lax.axis_index("row") % 2
    c = lax.axis_index("col")
    width = held.shape[1]
    blocks = held.shape[2] // 128
    block = own.shape[0] // blocks
    share = block - width
    lanes = pl.ds(pl.multiple_of(c * held.shape[2], held.shape[2]), held.shape[2])
    copies = [
        pltpu.make_async_copy(factor, lines, sem.at[0]),
        pltpu.make_async_copy(inverse.at[:, :, lanes], held, sem.at[1]),
        pltpu.make_async_copy(cov, near.at[pl.ds(own.shape[0], cov.shape[0]), :], sem.at[2]),
    ]
    for copy in copies:
        copy.start()
    copies[0].wait()
    copies[1].wait()
    for outs, member in (((own,), x), ((send, near), 1 - x)):
        for b in range(blocks):
            rows = lines[pl.ds(2 * b + member, share, stride=2 * blocks), :]
            cols = held[member, :, b * 128:(b + 1) * 128]
            for out in outs:
                out[b * block:b * block + share, :] = rows
                out[b * block + share:(b + 1) * block, :] = cols
    copies[2].wait()


def product_kernel(share, tile, slots, structure, live, place, c_own, *refs):
    mine = refs[:8]
    theirs = refs[8:12]
    near_theirs, c_sib = refs[12:14]
    panel_out = refs[14:16]
    w_out = refs[16:20]
    f_high, f_low, d_high, d_low = refs[20:24]
    pick, product = refs[24:]
    z, x, c = place[0], place[1], place[2]
    size = mine[0].shape[0]
    whole = d_high.shape[0]
    half = whole // 2
    lane_blocks = half // 128
    block = size // lane_blocks
    width = block - share
    wide = 2 * width
    near_x = 1 - x
    sources = (
        2 * z + x,
        2 * (z ^ 2) + x,
        2 * (z ^ 2) + near_x,
        2 * (z ^ 1) + x,
        2 * (z ^ 1) + near_x,
        2 * (z ^ 3) + x,
        2 * (z ^ 3) + near_x,
        2 * z + near_x,
    )
    blocks = c_own.shape[0] // tile
    for slot in range(slots):
        anc = structure[x, slot]
        for which, (here, there, start) in enumerate(
            ((c_own, c_sib, 0), (mine[7], near_theirs, size))
        ):
            rows = pl.ds(start + anc // 2, tile, stride=blocks)
            value = jnp.where(anc % 2 == c, here[rows, :], there[rows, :])
            at = pl.ds(pl.multiple_of((x ^ which) * tile, tile), tile)
            pick[at, slot * tile:(slot + 1) * tile] = jnp.where(slot < live[x], value, 0.0)
    for index, source in enumerate(sources):
        f_at = pl.ds(pl.multiple_of(source * share, share), share)
        d_at = pl.ds(pl.multiple_of(source * width, width), width)
        there = (near_theirs, 0)
        if index < 7:
            message, start = THERE[index]
            there = (theirs[message], start * size)
        for first, (ref, start) in ((0, (mine[index], 0)), (half, there)):
            for b in range(lane_blocks):
                lanes = slice(first + b * 128, first + (b + 1) * 128)
                top = start + b * block
                split(ref[top:top + share, :], f_high, f_low, (f_at, lanes))
                split(ref[top + share:top + block, :], d_high, d_low, (d_at, lanes))
    grown = dot3(halves(pick[...]), (f_high[...], f_low[...]), NN)
    product[...] = dot3(halves(grown), (d_high[...], d_low[...]), NT)
    lanes = pl.ds(pl.multiple_of(c * half, half), half)
    for which in range(2):
        at = pl.ds(pl.multiple_of((x ^ which) * tile, tile), tile)
        used = False
        for slot in range(slots):
            used = used | ((slot < live[x]) & (structure[x, slot] == 2 * z + (x ^ which)))
        panel_out[which][...] = jnp.where(used, -product[at, lanes], 0.0)
    low_lane = lax.broadcasted_iota(jnp.int32, (tile, wide), 1) < width
    for step in range(4):
        columns = pl.ds(pl.multiple_of((z ^ step) * wide, wide), wide)
        first = product[:tile, columns]
        second = product[tile:, columns]
        left = jnp.where(c == 0, first, pltpu.roll(first, width, 1))
        right = jnp.where(c == 0, pltpu.roll(second, width, 1), second)
        w_out[step][...] = jnp.where(low_lane, left, right)


def scaled_kernel(place, f_high, f_low, d_high, d_low, s_high, s_low, base):
    z, c = place[0], place[2]
    width = base.shape[0]
    inverse = (d_high[...], d_low[...])
    scaled = dot3((f_high[...], f_low[...]), inverse, NT)
    s_high[...], s_low[...] = halves(scaled)
    at = pl.ds(pl.multiple_of((2 * z + c) * width, width), width)
    base[...] = dot3((d_high[at, :], d_low[at, :]), inverse, NT)


def diag_kernel(tile, slots, structure, live, place, w0, w1, w2, w3, s_high, s_low, base, *refs):
    keep, cross, w_all, pick_high, pick_low, total = refs
    z, x = place[0], place[1]
    half = keep.shape[1]
    width = keep.shape[0]
    for step, piece in enumerate((w0, w1, w2, w3)):
        w_all[z ^ step] = piece[...]
    for slot in range(slots):
        anc = structure[x, slot]
        value = w_all[anc // 2]
        value = jnp.where(anc % 2 == 0, value, pltpu.roll(value, width, 1))
        at = slice(slot * tile, (slot + 1) * tile)
        split(jnp.where(slot < live[x], value, 0.0), pick_high, pick_low, (at, slice(None)))
    picked = (pick_high[...], pick_low[...])
    total[...] = base[...] + dot3(picked, (s_high[...], s_low[...]), TN)[:width]
    keep[...] = total[:, pl.ds(pl.multiple_of(x * half, half), half)]
    cross[...] = total[:, pl.ds(pl.multiple_of((1 - x) * half, half), half)]


def lines_kernel(place, mine, other, out):
    x = place[1]
    blocks = mine.shape[1] // 128
    for member, value in ((x, mine), (1 - x, other)):
        for block in range(blocks):
            at = pl.ds(2 * block + member, mine.shape[0], stride=2 * blocks)
            out[at, :] = value[:, block * 128:(block + 1) * 128]


def diag_lines_kernel(place, keep, met, far, out):
    x, c = place[1], place[2]
    blocks = keep.shape[1] // 128
    mine = jnp.where(c == x, keep[...], met[...])
    other = jnp.where(c == x, met[...], far[...])
    for member, value in ((x, mine), (1 - x, other)):
        for block in range(blocks):
            at = pl.ds(2 * block + member, keep.shape[0], stride=2 * blocks)
            out[at, :] = value[:, block * 128:(block + 1) * 128]


def many_rows(ancestor_cov, panel_factor, diag_inverse, structure, live_counts):
    tile_rows = ancestor_cov.shape[0]
    local_blocks = ancestor_cov.shape[1]
    col_count = lax.axis_size("col")
    col_id = lax.axis_index("col")
    row_id = lax.axis_index("row")
    flat_cov = ancestor_cov.reshape(tile_rows, local_blocks * tile_rows)
    half_width = panel_factor.shape[2]
    slot_total = structure.shape[1]
    whole_inverse = lax.all_gather(diag_inverse, "row", axis=2, tiled=True)
    inverse_part = lax.dynamic_slice_in_dim(whole_inverse, col_id * half_width, half_width, 0)
    factor_term = jnp.einsum(
        "rsk,ksn->rsn", panel_factor, inverse_part, precision=lax.Precision.HIGHEST
    )
    slot_index = jnp.arange(slot_total, dtype=jnp.int32)
    slot_alive = slot_index[None, :] < live_counts[:, None]
    own_slot = slot_alive & (structure == row_id)
    in_struct = jnp.any(own_slot, axis=1)
    own_pos = jnp.sum(jnp.where(own_slot, slot_index[None, :], 0), axis=1)
    tile_offsets = jnp.arange(tile_rows, dtype=jnp.int32)
    factor_rows = lax.psum(factor_term, "col")
    arrived = lax.all_gather(factor_rows, "row", axis=0, tiled=True)
    row_count = arrived.shape[0]
    global_row = jnp.arange(row_count, dtype=jnp.int32)
    slot_of = global_row // tile_rows
    offset = global_row % tile_rows
    chooser = (slot_of[:, None] == slot_index[None, :]).astype(jnp.int32)
    product_list = []
    owned_list = []
    for member in range(2):
        anc_block = jnp.sum(chooser * structure[member][None, :], axis=1)
        is_live = slot_of < live_counts[member]
        is_match = is_live & (anc_block % col_count == col_id)
        column_index = anc_block // col_count * tile_rows + offset
        sig_cols = jnp.take(flat_cov, column_index, axis=1)
        weighted = jnp.where(is_match[:, None], arrived[:, member, :], 0.0)
        product_list.append(
            jnp.dot(
                sig_cols,
                weighted,
                precision=lax.Precision.HIGHEST,
                preferred_element_type=jnp.float32,
            )
        )
        source = own_pos[member] * tile_rows + tile_offsets
        in_range = in_struct[member] & (source >= 0) & (source < row_count)
        fetched = jnp.take(arrived[:, member, :], jnp.clip(source, 0, row_count - 1), axis=0)
        owned_list.append(jnp.where(in_range[:, None], fetched, 0.0))
    partial_sum = jnp.stack(product_list, axis=1)
    owned = jnp.stack(owned_list, axis=1)
    summed_all = lax.psum(partial_sum, "col")
    product_half = lax.dynamic_slice_in_dim(summed_all, col_id * half_width, half_width, 2)
    panel_cov = -product_half * in_struct.astype(jnp.float32)[None, :, None]
    spread_term = lax.psum_scatter(
        jnp.einsum("tsi,tsn->isn", owned, product_half, precision=lax.Precision.HIGHEST),
        "row",
        scatter_dimension=0,
        tiled=True,
    )
    inverse_half = lax.dynamic_slice_in_dim(whole_inverse, col_id * half_width, half_width, 2)
    base_term = jnp.einsum(
        "ksi,ksn->isn", diag_inverse, inverse_half, precision=lax.Precision.HIGHEST
    )
    diag_cov = base_term + spread_term
    return (panel_cov, diag_cov)


def local(ancestor_cov, panel_factor, diag_inverse, structure, live_counts):
    rows = lax.axis_size("row")
    if rows != 8:
        return many_rows(ancestor_cov, panel_factor, diag_inverse, structure, live_counts)
    tile = ancestor_cov.shape[0]
    share, _, half = panel_factor.shape
    whole, _, width = diag_inverse.shape
    slots = structure.shape[1]
    col = lax.axis_index("col")
    row = lax.axis_index("row")
    place = jnp.stack([row // 2, row % 2, col]).astype(jnp.int32)
    smem = pl.BlockSpec(memory_space=pltpu.SMEM)
    vmem = pl.BlockSpec(memory_space=pltpu.VMEM)

    def like(*shape, dtype=F32):
        return jax.ShapeDtypeStruct(shape, dtype)

    def call(kernel, name, outs, scalars, arrays, scratch=(), space=vmem, limit=VMEM_LIMIT):
        return pl.pallas_call(
            kernel,
            out_shape=outs,
            in_specs=[smem] * len(scalars) + [space] * len(arrays),
            out_specs=[vmem] * len(outs),
            scratch_shapes=list(scratch),
            compiler_params=pltpu.CompilerParams(vmem_limit_bytes=limit),
            name=name,
        )(*scalars, *arrays)

    def send_to(value, target):
        pairs = []
        for r in range(rows):
            for c in range(2):
                to = target(r // 2, r % 2, c)
                if to is not None:
                    pairs.append((r * 2 + c, (to[0] * 2 + to[1]) * 2 + to[2]))
        return lax.ppermute(value, ("row", "col"), pairs)

    def move(value, z_step, x_step, flip):
        return send_to(value, lambda z, x, c: (z ^ z_step, x ^ x_step, c ^ flip))

    factor_lines = (
        panel_factor.reshape(share, 2, half // 128, 128).transpose(0, 2, 1, 3).reshape(-1, 128)
    )
    c_own = ancestor_cov.reshape(-1, 128)
    bundle = (share + width) * half // 128
    own, send, send_near = call(
        pack_kernel,
        "pack",
        [like(bundle, 128)] * 2 + [like(bundle + c_own.shape[0], 128)],
        [],
        [
            pltpu.with_memory_space_constraint(v, pltpu.HBM)
            for v in (factor_lines, diag_inverse.transpose(1, 2, 0), c_own)
        ],
        [
            pltpu.VMEM(factor_lines.shape, F32),
            pltpu.VMEM((2, width, half), F32),
            pltpu.SemaphoreType.DMA((3,)),
        ],
        pl.BlockSpec(memory_space=pltpu.HBM),
    )
    own_far = move(own, 2, 0, 0)
    near_far = move(send, 2, 1, 0)
    own_side = move(own, 1, 0, 0)
    near_side = move(send, 1, 1, 0)
    near = move(send_near, 0, 1, 0)
    own_opposite = move(own_far, 1, 0, 0)
    c_sib = move(c_own, 0, 0, 1)
    near_far, c_sib = lax.optimization_barrier((near_far, c_sib))
    near_opposite = move(near_far, 1, 0, 0)
    near_in, c_sib = lax.optimization_barrier((near, c_sib))
    mine = [own, own_far, near_far, own_side, near_side, own_opposite, near_opposite, near]
    theirs = [
        move(jnp.concatenate([own_far, near_far]), 0, 0, 1),
        move(jnp.concatenate([own_side, near_side]), 0, 0, 1),
        move(own, 0, 0, 1),
        move(jnp.concatenate([own_opposite, near_opposite]), 0, 0, 1),
        move(near_in, 0, 0, 1),
        c_sib,
    ]
    split_f = [like(slots * tile, whole, dtype=BF16)] * 2
    split_d = [like(whole, whole, dtype=BF16)] * 2
    outs = call(
        functools.partial(product_kernel, share, tile, slots),
        "products",
        [like(tile, half)] * 2 + [like(tile, 2 * width)] * 4 + split_f + split_d,
        [structure, live_counts, place],
        [c_own, *mine, *theirs],
        [pltpu.VMEM((2 * tile, slots * tile), F32), pltpu.VMEM((2 * tile, whole), F32)],
    )
    panel, w, parts = outs[:2], outs[2:6], outs[6:]
    w = [w[0]] + [move(w[step], step, 0, 0) for step in range(1, 4)]
    s_high, s_low, base = call(
        scaled_kernel, "scaled", split_f + [like(width, whole)], [place], parts
    )
    panel_send, w[1] = lax.optimization_barrier((panel[1], w[1]))
    panel_got = move(panel_send, 0, 1, 0)
    keep, cross = call(
        functools.partial(diag_kernel, tile, slots),
        "diag_block",
        [like(width, half)] * 2,
        [structure, live_counts, place],
        [*w, s_high, s_low, base],
        [
            pltpu.VMEM((rows // 2, tile, 2 * width), F32),
            pltpu.VMEM((slots * tile, 2 * width), BF16),
            pltpu.VMEM((slots * tile, 2 * width), BF16),
            pltpu.VMEM((width, whole), F32),
        ],
    )
    met = send_to(cross, lambda z, x, c: (z, x, 1 - c) if c == x else (z, 1 - x, c))
    far = send_to(keep, lambda z, x, c: None if c == x else (z, 1 - x, 1 - c))
    lines = 2 * half // 128
    panel_got, keep = lax.optimization_barrier((panel_got, keep))
    (panel_lines,) = call(
        lines_kernel, "panel_lines", [like(tile * lines, 128)], [place], [panel[0], panel_got]
    )
    panel_lines, keep = lax.optimization_barrier((panel_lines, keep))
    (diag_lines,) = call(
        diag_lines_kernel, "diag_lines", [like(width * lines, 128)], [place], [keep, met, far]
    )

    def unfold(value, count):
        return value.reshape(count, half // 128, 2, 128).transpose(0, 2, 1, 3).reshape(count, 2, half)

    return unfold(panel_lines, tile), unfold(diag_lines, width)


def solution(mesh):
    placed = (
        P(("mp", "row"), None, "col", None),
        P(("mp", "row"), None, "col"),
        P("mp", None, "row"),
        P("mp", None),
        P("mp"),
    )
    return jax.shard_map(
        local,
        mesh=mesh,
        in_specs=placed,
        out_specs=(P(("mp", "row"), None, "col"), P(("mp", "row"), None, "col")),
        check_vma=False,
    )
```

```python
import functools

import jax
import jax.numpy as jnp
from jax import lax
from jax.experimental import pallas as pl
from jax.experimental.pallas import tpu as pltpu
from jax.sharding import PartitionSpec as P

F32 = jnp.float32
BF16 = jnp.bfloat16
NT = (((1,), (1,)), ((), ()))
NN = (((1,), (0,)), ((), ()))
TN = (((0,), (0,)), ((), ()))
VMEM_LIMIT = 20 * 1024 * 1024
THERE = ((2, 0), (0, 0), (0, 1), (1, 0), (1, 1), (3, 0), (2, 1))


def halves(value):
    high = value.astype(BF16)
    low = (value - high.astype(F32)).astype(BF16)
    return high, low


def dot3(left, right, dims):
    left_high, left_low = left
    right_high, right_low = right

    def one(a, b):
        return lax.dot_general(a, b, dims, preferred_element_type=F32)

    return one(left_high, right_low) + one(left_low, right_high) + one(left_high, right_high)


def split(value, high, low, at):
    high[at], low[at] = halves(value)


def pack_kernel(factor, inverse, cov, own, send, near, lines, held, sem):
    x = lax.axis_index("row") % 2
    c = lax.axis_index("col")
    width = held.shape[1]
    blocks = held.shape[2] // 128
    block = own.shape[0] // blocks
    share = block - width
    lanes = pl.ds(pl.multiple_of(c * held.shape[2], held.shape[2]), held.shape[2])
    copies = [
        pltpu.make_async_copy(factor, lines, sem.at[0]),
        pltpu.make_async_copy(inverse.at[:, :, lanes], held, sem.at[1]),
        pltpu.make_async_copy(cov, near.at[pl.ds(own.shape[0], cov.shape[0]), :], sem.at[2]),
    ]
    for copy in copies:
        copy.start()
    copies[0].wait()
    copies[1].wait()
    for outs, member in (((own,), x), ((send, near), 1 - x)):
        for b in range(blocks):
            rows = lines[pl.ds(2 * b + member, share, stride=2 * blocks), :]
            cols = held[member, :, b * 128:(b + 1) * 128]
            for out in outs:
                out[b * block:b * block + share, :] = rows
                out[b * block + share:(b + 1) * block, :] = cols
    copies[2].wait()


def product_kernel(share, tile, slots, structure, live, place, c_own, *refs):
    mine = refs[:8]
    theirs = refs[8:12]
    near_theirs, c_sib = refs[12:14]
    panel_out = refs[14:16]
    w_out = refs[16:20]
    f_high, f_low, d_high, d_low = refs[20:24]
    pick, product = refs[24:]
    z, x, c = place[0], place[1], place[2]
    size = mine[0].shape[0]
    whole = d_high.shape[0]
    half = whole // 2
    lane_blocks = half // 128
    block = size // lane_blocks
    width = block - share
    wide = 2 * width
    near_x = 1 - x
    sources = (
        2 * z + x,
        2 * (z ^ 2) + x,
        2 * (z ^ 2) + near_x,
        2 * (z ^ 1) + x,
        2 * (z ^ 1) + near_x,
        2 * (z ^ 3) + x,
        2 * (z ^ 3) + near_x,
        2 * z + near_x,
    )
    blocks = c_own.shape[0] // tile
    for slot in range(slots):
        anc = structure[x, slot]
        for which, (here, there, start) in enumerate(
            ((c_own, c_sib, 0), (mine[7], near_theirs, size))
        ):
            rows = pl.ds(start + anc // 2, tile, stride=blocks)
            value = jnp.where(anc % 2 == c, here[rows, :], there[rows, :])
            at = pl.ds(pl.multiple_of((x ^ which) * tile, tile), tile)
            pick[at, slot * tile:(slot + 1) * tile] = jnp.where(slot < live[x], value, 0.0)
    for index, source in enumerate(sources):
        f_at = pl.ds(pl.multiple_of(source * share, share), share)
        d_at = pl.ds(pl.multiple_of(source * width, width), width)
        there = (near_theirs, 0)
        if index < 7:
            message, start = THERE[index]
            there = (theirs[message], start * size)
        for first, (ref, start) in ((0, (mine[index], 0)), (half, there)):
            for b in range(lane_blocks):
                lanes = slice(first + b * 128, first + (b + 1) * 128)
                top = start + b * block
                split(ref[top:top + share, :], f_high, f_low, (f_at, lanes))
                split(ref[top + share:top + block, :], d_high, d_low, (d_at, lanes))
    grown = dot3(halves(pick[...]), (f_high[...], f_low[...]), NN)
    product[...] = dot3(halves(grown), (d_high[...], d_low[...]), NT)
    lanes = pl.ds(pl.multiple_of(c * half, half), half)
    for which in range(2):
        at = pl.ds(pl.multiple_of((x ^ which) * tile, tile), tile)
        used = False
        for slot in range(slots):
            used = used | ((slot < live[x]) & (structure[x, slot] == 2 * z + (x ^ which)))
        panel_out[which][...] = jnp.where(used, -product[at, lanes], 0.0)
    low_lane = lax.broadcasted_iota(jnp.int32, (tile, wide), 1) < width
    for step in range(4):
        columns = pl.ds(pl.multiple_of((z ^ step) * wide, wide), wide)
        first = product[:tile, columns]
        second = product[tile:, columns]
        left = jnp.where(c == 0, first, pltpu.roll(first, width, 1))
        right = jnp.where(c == 0, pltpu.roll(second, width, 1), second)
        w_out[step][...] = jnp.where(low_lane, left, right)


def scaled_kernel(place, f_high, f_low, d_high, d_low, s_high, s_low, base):
    z, c = place[0], place[2]
    width = base.shape[0]
    inverse = (d_high[...], d_low[...])
    scaled = dot3((f_high[...], f_low[...]), inverse, NT)
    s_high[...], s_low[...] = halves(scaled)
    at = pl.ds(pl.multiple_of((2 * z + c) * width, width), width)
    base[...] = dot3((d_high[at, :], d_low[at, :]), inverse, NT)


def diag_kernel(tile, slots, structure, live, place, w0, w1, w2, w3, s_high, s_low, base, *refs):
    keep, cross, w_all, pick_high, pick_low, total = refs
    z, x = place[0], place[1]
    half = keep.shape[1]
    width = keep.shape[0]
    for step, piece in enumerate((w0, w1, w2, w3)):
        w_all[z ^ step] = piece[...]
    for slot in range(slots):
        anc = structure[x, slot]
        value = w_all[anc // 2]
        value = jnp.where(anc % 2 == 0, value, pltpu.roll(value, width, 1))
        at = slice(slot * tile, (slot + 1) * tile)
        split(jnp.where(slot < live[x], value, 0.0), pick_high, pick_low, (at, slice(None)))
    picked = (pick_high[...], pick_low[...])
    total[...] = base[...] + dot3(picked, (s_high[...], s_low[...]), TN)[:width]
    keep[...] = total[:, pl.ds(pl.multiple_of(x * half, half), half)]
    cross[...] = total[:, pl.ds(pl.multiple_of((1 - x) * half, half), half)]


def lines_kernel(place, mine, other, out):
    x = place[1]
    blocks = mine.shape[1] // 128
    for member, value in ((x, mine), (1 - x, other)):
        for block in range(blocks):
            at = pl.ds(2 * block + member, mine.shape[0], stride=2 * blocks)
            out[at, :] = value[:, block * 128:(block + 1) * 128]


def diag_lines_kernel(place, keep, met, far, out):
    x, c = place[1], place[2]
    blocks = keep.shape[1] // 128
    mine = jnp.where(c == x, keep[...], met[...])
    other = jnp.where(c == x, met[...], far[...])
    for member, value in ((x, mine), (1 - x, other)):
        for block in range(blocks):
            at = pl.ds(2 * block + member, keep.shape[0], stride=2 * blocks)
            out[at, :] = value[:, block * 128:(block + 1) * 128]


def many_rows(ancestor_cov, panel_factor, diag_inverse, structure, live_counts):
    tile_rows = ancestor_cov.shape[0]
    local_blocks = ancestor_cov.shape[1]
    col_count = lax.axis_size("col")
    col_id = lax.axis_index("col")
    row_id = lax.axis_index("row")
    flat_cov = ancestor_cov.reshape(tile_rows, local_blocks * tile_rows)
    half_width = panel_factor.shape[2]
    slot_total = structure.shape[1]
    whole_inverse = lax.all_gather(diag_inverse, "row", axis=2, tiled=True)
    inverse_part = lax.dynamic_slice_in_dim(whole_inverse, col_id * half_width, half_width, 0)
    factor_term = jnp.einsum(
        "rsk,ksn->rsn", panel_factor, inverse_part, precision=lax.Precision.HIGHEST
    )
    slot_index = jnp.arange(slot_total, dtype=jnp.int32)
    slot_alive = slot_index[None, :] < live_counts[:, None]
    own_slot = slot_alive & (structure == row_id)
    in_struct = jnp.any(own_slot, axis=1)
    own_pos = jnp.sum(jnp.where(own_slot, slot_index[None, :], 0), axis=1)
    tile_offsets = jnp.arange(tile_rows, dtype=jnp.int32)
    factor_rows = lax.psum(factor_term, "col")
    arrived = lax.all_gather(factor_rows, "row", axis=0, tiled=True)
    row_count = arrived.shape[0]
    global_row = jnp.arange(row_count, dtype=jnp.int32)
    slot_of = global_row // tile_rows
    offset = global_row % tile_rows
    chooser = (slot_of[:, None] == slot_index[None, :]).astype(jnp.int32)
    product_list = []
    owned_list = []
    for member in range(2):
        anc_block = jnp.sum(chooser * structure[member][None, :], axis=1)
        is_live = slot_of < live_counts[member]
        is_match = is_live & (anc_block % col_count == col_id)
        column_index = anc_block // col_count * tile_rows + offset
        sig_cols = jnp.take(flat_cov, column_index, axis=1)
        weighted = jnp.where(is_match[:, None], arrived[:, member, :], 0.0)
        product_list.append(
            jnp.dot(
                sig_cols,
                weighted,
                precision=lax.Precision.HIGHEST,
                preferred_element_type=jnp.float32,
            )
        )
        source = own_pos[member] * tile_rows + tile_offsets
        in_range = in_struct[member] & (source >= 0) & (source < row_count)
        fetched = jnp.take(arrived[:, member, :], jnp.clip(source, 0, row_count - 1), axis=0)
        owned_list.append(jnp.where(in_range[:, None], fetched, 0.0))
    partial_sum = jnp.stack(product_list, axis=1)
    owned = jnp.stack(owned_list, axis=1)
    summed_all = lax.psum(partial_sum, "col")
    product_half = lax.dynamic_slice_in_dim(summed_all, col_id * half_width, half_width, 2)
    panel_cov = -product_half * in_struct.astype(jnp.float32)[None, :, None]
    spread_term = lax.psum_scatter(
        jnp.einsum("tsi,tsn->isn", owned, product_half, precision=lax.Precision.HIGHEST),
        "row",
        scatter_dimension=0,
        tiled=True,
    )
    inverse_half = lax.dynamic_slice_in_dim(whole_inverse, col_id * half_width, half_width, 2)
    base_term = jnp.einsum(
        "ksi,ksn->isn", diag_inverse, inverse_half, precision=lax.Precision.HIGHEST
    )
    diag_cov = base_term + spread_term
    return (panel_cov, diag_cov)


def local(ancestor_cov, panel_factor, diag_inverse, structure, live_counts):
    rows = lax.axis_size("row")
    if rows != 8:
        return many_rows(ancestor_cov, panel_factor, diag_inverse, structure, live_counts)
    tile = ancestor_cov.shape[0]
    share, _, half = panel_factor.shape
    whole, _, width = diag_inverse.shape
    slots = structure.shape[1]
    col = lax.axis_index("col")
    row = lax.axis_index("row")
    place = jnp.stack([row // 2, row % 2, col]).astype(jnp.int32)
    smem = pl.BlockSpec(memory_space=pltpu.SMEM)
    vmem = pl.BlockSpec(memory_space=pltpu.VMEM)

    def like(*shape, dtype=F32):
        return jax.ShapeDtypeStruct(shape, dtype)

    def call(kernel, name, outs, scalars, arrays, scratch=(), space=vmem, limit=VMEM_LIMIT):
        return pl.pallas_call(
            kernel,
            out_shape=outs,
            in_specs=[smem] * len(scalars) + [space] * len(arrays),
            out_specs=[vmem] * len(outs),
            scratch_shapes=list(scratch),
            compiler_params=pltpu.CompilerParams(vmem_limit_bytes=limit),
            name=name,
        )(*scalars, *arrays)

    def send_to(value, target):
        pairs = []
        for r in range(rows):
            for c in range(2):
                to = target(r // 2, r % 2, c)
                if to is not None:
                    pairs.append((r * 2 + c, (to[0] * 2 + to[1]) * 2 + to[2]))
        return lax.ppermute(value, ("row", "col"), pairs)

    def move(value, z_step, x_step, flip):
        return send_to(value, lambda z, x, c: (z ^ z_step, x ^ x_step, c ^ flip))

    factor_lines = (
        panel_factor.reshape(share, 2, half // 128, 128).transpose(0, 2, 1, 3).reshape(-1, 128)
    )
    c_own = ancestor_cov.reshape(-1, 128)
    bundle = (share + width) * half // 128
    own, send, send_near = call(
        pack_kernel,
        "pack",
        [like(bundle, 128)] * 2 + [like(bundle + c_own.shape[0], 128)],
        [],
        [
            pltpu.with_memory_space_constraint(v, pltpu.HBM)
            for v in (factor_lines, diag_inverse.transpose(1, 2, 0), c_own)
        ],
        [
            pltpu.VMEM(factor_lines.shape, F32),
            pltpu.VMEM((2, width, half), F32),
            pltpu.SemaphoreType.DMA((3,)),
        ],
        pl.BlockSpec(memory_space=pltpu.HBM),
    )
    own_far = move(own, 2, 0, 0)
    near_far = move(send, 2, 1, 0)
    own_side = move(own, 1, 0, 0)
    near_side = move(send, 1, 1, 0)
    near = move(send_near, 0, 1, 0)
    own_opposite = move(own_far, 1, 0, 0)
    near_opposite = move(near_far, 1, 0, 0)
    c_sib = move(c_own, 0, 0, 1)
    near_in, c_sib = lax.optimization_barrier((near, c_sib))
    mine = [own, own_far, near_far, own_side, near_side, own_opposite, near_opposite, near]
    theirs = [
        move(jnp.concatenate([own_far, near_far]), 0, 0, 1),
        move(jnp.concatenate([own_side, near_side]), 0, 0, 1),
        move(jnp.concatenate([own, near_opposite]), 0, 0, 1),
        move(own_opposite, 0, 0, 1),
        move(near_in, 0, 0, 1),
        c_sib,
    ]
    split_f = [like(slots * tile, whole, dtype=BF16)] * 2
    split_d = [like(whole, whole, dtype=BF16)] * 2
    outs = call(
        functools.partial(product_kernel, share, tile, slots),
        "products",
        [like(tile, half)] * 2 + [like(tile, 2 * width)] * 4 + split_f + split_d,
        [structure, live_counts, place],
        [c_own, *mine, *theirs],
        [pltpu.VMEM((2 * tile, slots * tile), F32), pltpu.VMEM((2 * tile, whole), F32)],
    )
    panel, w, parts = outs[:2], outs[2:6], outs[6:]
    w = [w[0]] + [move(w[step], step, 0, 0) for step in range(1, 4)]
    s_high, s_low, base = call(
        scaled_kernel, "scaled", split_f + [like(width, whole)], [place], parts
    )
    panel_send, w[1] = lax.optimization_barrier((panel[1], w[1]))
    panel_got = move(panel_send, 0, 1, 0)
    keep, cross = call(
        functools.partial(diag_kernel, tile, slots),
        "diag_block",
        [like(width, half)] * 2,
        [structure, live_counts, place],
        [*w, s_high, s_low, base],
        [
            pltpu.VMEM((rows // 2, tile, 2 * width), F32),
            pltpu.VMEM((slots * tile, 2 * width), BF16),
            pltpu.VMEM((slots * tile, 2 * width), BF16),
            pltpu.VMEM((width, whole), F32),
        ],
    )
    met = send_to(cross, lambda z, x, c: (z, x, 1 - c) if c == x else (z, 1 - x, c))
    far = send_to(keep, lambda z, x, c: None if c == x else (z, 1 - x, 1 - c))
    lines = 2 * half // 128
    panel_got, keep = lax.optimization_barrier((panel_got, keep))
    (panel_lines,) = call(
        lines_kernel, "panel_lines", [like(tile * lines, 128)], [place], [panel[0], panel_got]
    )
    panel_lines, keep = lax.optimization_barrier((panel_lines, keep))
    (diag_lines,) = call(
        diag_lines_kernel, "diag_lines", [like(width * lines, 128)], [place], [keep, met, far]
    )

    def unfold(value, count):
        return value.reshape(count, half // 128, 2, 128).transpose(0, 2, 1, 3).reshape(count, 2, half)

    return unfold(panel_lines, tile), unfold(diag_lines, width)


def solution(mesh):
    placed = (
        P(("mp", "row"), None, "col", None),
        P(("mp", "row"), None, "col"),
        P("mp", None, "row"),
        P("mp", None),
        P("mp"),
    )
    return jax.shard_map(
        local,
        mesh=mesh,
        in_specs=placed,
        out_specs=(P(("mp", "row"), None, "col"), P(("mp", "row"), None, "col")),
        check_vma=False,
    )
```
